32 devices in a mesh: group: 4 (over y, x), member: 8 (over z, core).
Axes of the slice: x: 2, y: 2, z: 4, core: 2. Of those that a mesh axis runs over, the one named last changes fastest.
Arguments:
- old_ids: int32 [512], P(('group', 'member')), may hold values from -1 to 255, as said below
- field_old: float32 [512, 32, 1024], P(('group', 'member')), may hold values from -6 to 6
- source_old: float32 [512, 32, 1024], P(('group', 'member')), may hold values from -12 to 12
- kappa_old: float32 [512, 32, 1024], P(('group', 'member')), may hold values from 0.5 to 5
- refine: int32 [256], P(('group', 'member')), may hold values 0 or 1
- neighbors: int32 [256, 6], P(('group', 'member')), may hold values from -1 to 255, as said below
- coarse_inverse: float32 [4, 512, 512], P('group', 'member'), may hold values from -0.0546875 to 0.0546875
Outputs:
- solution: float32 [256, 32, 1024], P(('group', 'member'))
The draws below stay inside these ranges and needn't reach their ends.
Inputs may be any that keep to these rules, and one draw needn't show every extreme that they name: `old_ids`: on each device the live slots come first and hold consecutive curve indices in increasing order, devices following one another along the curve; every block's new owner (index // 8) is the device that holds it or the next one; some device fills all 16 slots. Blocks form a grid in Morton order (bit i of a curve index is a bit of coordinate i mod 3); neighbors[g, k] is either -1 or the block adjacent to g across face k in that grid; relations are mutual: neighbors[g, k] = h means neighbors[h, k xor 1] = g.
All inputs are finite; a program needn't handle non-finite values. No bound on the sum of `refine` on one device may be relied on, other than what follows from the above.
Results may differ from the reference program's by a relative error of at most 0.000078.
Values sent between devices are 32-bit elements; how exact they have to be, the bound alone decides.
A program may use at most 128 MiB of HBM per device.

```python
import math
import jax
import jax.numpy as jnp
from jax import lax

NB = 8
EDGE = 32
OLDCAP = 16
NBLK = 256
CG = 512
N_GROUP = 4
DEVICES = 32


def draw_old_ids(key, part):
    devices_all = NBLK // NB
    position = jnp.arange(devices_all + 1, dtype=jnp.int32)
    extra = jax.random.randint(key, (devices_all + 1,), 0, NB + 1).astype(jnp.int32)
    extra = jnp.where(position == 1, NB, extra)
    extra = jnp.where(position == devices_all - 1, NB, extra)
    extra = jnp.where(position == 0, 0, extra)
    extra = jnp.where(position == devices_all, 0, extra)
    starts = position * NB + extra
    counts = starts[1:] - starts[:-1]
    slot_ids = jnp.arange(2 * NB, dtype=jnp.int32)
    block_ids = starts[:-1, None] + slot_ids[None, :]
    return jnp.where(slot_ids[None, :] < counts[:, None], block_ids, -1).reshape(-1).astype(jnp.int32)


def decode_bits(block_ids, nbits):
    coords = [jnp.zeros_like(block_ids), jnp.zeros_like(block_ids), jnp.zeros_like(block_ids)]
    for bit_id in range(nbits):
        coords[bit_id % 3] = coords[bit_id % 3] + block_ids // 2 ** bit_id % 2 * 2 ** (bit_id // 3)
    return coords


def encode_bits(coords, nbits):
    result = jnp.zeros_like(coords[0])
    for bit_id in range(nbits):
        result = result + coords[bit_id % 3] // 2 ** (bit_id // 3) % 2 * 2 ** bit_id
    return result


def draw_neighbors(key, part):
    nbits = NBLK.bit_length() - 1
    block_ids = jnp.arange(NBLK, dtype=jnp.int32)
    coords = decode_bits(block_ids, nbits)
    extents = [2 ** len([bit_id for bit_id in range(nbits) if bit_id % 3 == axis_id]) for axis_id in range(3)]
    cut_plus = jax.random.randint(key, (NBLK, 3), 0, 8).astype(jnp.int32) == 0
    columns = []
    for axis_id in range(3):
        for step_sign in (-1, 1):
            moved = coords[axis_id] + step_sign
            inside = jnp.logical_and(moved >= 0, moved < extents[axis_id])
            new_coords = list(coords)
            new_coords[axis_id] = jnp.clip(moved, 0, extents[axis_id] - 1)
            target = encode_bits(new_coords, nbits)
            if step_sign == 1:
                cut_face = cut_plus[:, axis_id]
            else:
                cut_face = cut_plus[target, axis_id]
            columns.append(jnp.where(jnp.logical_and(inside, jnp.logical_not(cut_face)), target, -1))
    return jnp.stack(columns, axis=1).astype(jnp.int32)


def plant(drawn, rng, low, top_value):
    longest = drawn.shape.index(max(drawn.shape))
    spots = []
    for shift in (0, 1):
        where = [jax.random.randint(jax.random.fold_in(rng, axis), (), 0, length) for axis, length in enumerate(drawn.shape)]
        where[longest] = (where[longest] + shift) % drawn.shape[longest]
        spots.append(tuple(where))
    return drawn.at[spots[0]].set(low).at[spots[1]].set(top_value)


def block_scale(rng, shape, split, low, top_value):
    gain = 1.0
    for axis_at, parts in split:
        heights = jax.random.uniform(jax.random.fold_in(jax.random.fold_in(rng, 6), axis_at), (parts,), jnp.float32, low / len(split), top_value / len(split))
        gain = gain * jnp.repeat(jnp.exp(heights), shape[axis_at] // parts).reshape((-1,) + (1,) * (len(shape) - 1 - axis_at))
    return gain


def centred(stream_key, shape, width, bound, pieces=(), kind=jnp.bfloat16):
    values = width * jax.random.normal(stream_key, shape, jnp.float32)
    if pieces:
        values = values * block_scale(stream_key, shape, pieces, -0.22, 0.18)
    return jnp.clip(values, -bound, bound).astype(kind)


def setup_inputs(seed: int = 0) -> dict:
    splits = jax.random.split(jax.random.key(seed), 8)
    return {
        "old_ids": draw_old_ids(jax.random.fold_in(splits[7], 71), 0),
        "field_old": centred(splits[1], (DEVICES * OLDCAP, EDGE, EDGE * EDGE), 1.0, 6.0, ((0, 32),), jnp.float32),
        "source_old": centred(splits[2], (DEVICES * OLDCAP, EDGE, EDGE * EDGE), 2.0, 12.0, ((0, 32),), jnp.float32),
        "kappa_old": jnp.clip(jnp.exp(math.log(5.0) - 2.3025851 * jax.random.uniform(splits[3], (DEVICES * OLDCAP, EDGE, EDGE * EDGE), jnp.float32) ** block_scale(splits[3], (DEVICES * OLDCAP, EDGE, EDGE * EDGE), ((0, 32),), -0.2, 0.2)), 0.5, 5.0),
        "refine": plant((jax.random.randint(splits[4], (NBLK,), 0, 2) < 1).astype(jnp.int32), jax.random.fold_in(splits[4], 1), 0, 1),
        "neighbors": draw_neighbors(jax.random.fold_in(splits[7], 71), 0),
        "coarse_inverse": centred(splits[6], (N_GROUP, CG, CG), (25 * CG) ** -0.5, 0.0546875, ((0, 4), (1, 8)), jnp.float32),
    }


OMEGA = 0.8
OPPOSITE = (1, 0, 3, 2, 5, 4)


def face_layers(volume):
    blocks, edge_cells, face_cells = volume.shape
    cube_view = volume.reshape(blocks, edge_cells, edge_cells, edge_cells)
    planes = [cube_view[:, 0], cube_view[:, edge_cells - 1], cube_view[:, :, 0], cube_view[:, :, edge_cells - 1], cube_view[:, :, :, 0], cube_view[:, :, :, edge_cells - 1]]
    return jnp.stack([plane_one.reshape(blocks, face_cells) for plane_one in planes], axis=1)


def beside(values, ghosts):
    blocks, edge_cells, face_cells = values.shape
    sheets = ghosts.reshape(blocks, 6, edge_cells, edge_cells)
    x_minus = jnp.concatenate([ghosts[:, 0][:, None, :], values[:, :-1]], axis=1)
    x_plus = jnp.concatenate([values[:, 1:], ghosts[:, 1][:, None, :]], axis=1)
    y_minus = jnp.concatenate([sheets[:, 2], values[:, :, :-edge_cells]], axis=2)
    y_plus = jnp.concatenate([values[:, :, edge_cells:], sheets[:, 3]], axis=2)
    depth = lax.iota(jnp.int32, face_cells) % edge_cells
    zero_col = jnp.zeros_like(values[:, :, :1])
    z_minus = jnp.where(depth == 0, jnp.repeat(sheets[:, 4], edge_cells, axis=2), jnp.concatenate([zero_col, values[:, :, :-1]], axis=2))
    z_plus = jnp.where(depth == edge_cells - 1, jnp.repeat(sheets[:, 5], edge_cells, axis=2), jnp.concatenate([values[:, :, 1:], zero_col], axis=2))
    return [x_minus, x_plus, y_minus, y_plus, z_minus, z_plus]


def face_weights(kappa, kappa_ghosts, inv_spacing):
    return [inv_spacing * (0.5 * (kappa + across)) for across in beside(kappa, kappa_ghosts)]


def smooth_terms(values, ghosts, weights):
    applied = jnp.zeros_like(values)
    diagonal = jnp.zeros_like(values)
    for weight, across in zip(weights, beside(values, ghosts)):
        applied = applied + weight * (values - across)
        diagonal = diagonal + weight
    return applied, diagonal


def restrict(residual):
    blocks, edge_cells, face_cells = residual.shape
    half_edge = edge_cells // 2
    split_view = residual.reshape(blocks, 2, half_edge, 2, half_edge, 2, half_edge)
    return jnp.sum(split_view, axis=(2, 4, 6)).reshape(blocks * 8) * (half_edge ** -1.5)


def prolong(values, correction):
    blocks, edge_cells, face_cells = values.shape
    half_edge = edge_cells // 2
    split_view = values.reshape(blocks, 2, half_edge, 2, half_edge, 2, half_edge)
    lifted = correction.reshape(blocks, 2, 1, 2, 1, 2, 1)
    return (split_view + lifted).reshape(values.shape)


def reference(old_ids, field_old, source_old, kappa_old, refine, neighbors, coarse_inverse):
    places = jnp.where(old_ids >= 0, old_ids, NBLK).astype(jnp.int32)

    def settle(old_values):
        empty_set = jnp.zeros((NBLK + 1,) + old_values.shape[1:], jnp.float32)
        return empty_set.at[places].set(old_values)[:NBLK]

    field_new = settle(field_old)
    source = settle(source_old)
    kappa = settle(kappa_old)
    inv_spacing = (1.0 + refine.astype(jnp.float32))[:, None, None]
    opposite = jnp.array(OPPOSITE, jnp.int32)
    has_side = (neighbors >= 0)[:, :, None]
    source_rows = jnp.maximum(neighbors, 0).astype(jnp.int32)

    def ghosts_of(values):
        sheets = face_layers(values)
        return jnp.where(has_side, sheets[source_rows, opposite[None, :]], 0.0)

    kappa_ghosts = jnp.where(has_side, ghosts_of(kappa), face_layers(kappa))
    weights = face_weights(kappa, kappa_ghosts, inv_spacing)
    for sweep_id in range(2):
        applied, diagonal = smooth_terms(field_new, ghosts_of(field_new), weights)
        field_new = field_new + OMEGA * (source - applied) / diagonal
    applied, diagonal = smooth_terms(field_new, ghosts_of(field_new), weights)
    coarse = restrict(source - applied).reshape(N_GROUP, CG)
    correction = jnp.einsum("gij,gj->gi", coarse_inverse, coarse, precision=lax.Precision.HIGHEST)
    return prolong(field_new, correction.reshape(NBLK * 8))
```

```python
import functools

import jax
import jax.numpy as jnp
from jax import lax
from jax.experimental import pallas as pl
from jax.experimental.pallas import tpu as pltpu
from jax.sharding import PartitionSpec as P

OMEGA = 0.8
AXES = ("group", "member")
NB, EDGE, FACE, LANES = 8, 32, 1024, 128
TILES, PARTS, PITCH = 8, 4, 48
HIGHEST = lax.Precision.HIGHEST
VMEM_LIMIT = 60 * 2**20
VM = pl.BlockSpec(memory_space=pltpu.VMEM)
ANY = pl.BlockSpec(memory_space=pl.ANY)
SM = pl.BlockSpec(memory_space=pltpu.SMEM)
MESH = pl.DeviceIdType.MESH
FIELDS = (2, 1, 1)


def roll(value, steps):
    return pltpu.roll(value, steps % LANES, 1)


def spot(tile, part):
    return slice(PITCH * (tile + 1) + 8 + 8 * part, PITCH * (tile + 1) + 16 + 8 * part)


def flat(tile, part):
    return slice(EDGE * tile + 8 * part, EDGE * tile + 8 * part + 8)


def blocks_of(axis, side):
    return [b for b in range(NB) if (b >> axis) % 2 == side]


def octet_neighbors(octet, devices):
    nbits = devices.bit_length() - 1
    bits = [octet // 2**i % 2 for i in range(nbits)]
    result = []
    for axis in range(3):
        own = [i for i in range(nbits) if i % 3 == axis]
        extent = 2 ** len(own)
        coord = sum(bits[i] * 2**n for n, i in enumerate(own))
        base = octet - sum(bits[i] * 2**i for i in own)
        pair = []
        for step in (-1, 1):
            moved = coord + step
            inside = jnp.logical_and(moved >= 0, moved < extent)
            clipped = jnp.clip(moved, 0, extent - 1)
            index = base + sum(clipped // 2**n % 2 * 2**i for n, i in enumerate(own))
            pair.append((inside, index))
        result.append(pair)
    return result


def main_kernel(members, devices, old_ids, nbrs, refine, inverse, u_old, f_old, k_old, out_ref, *scratch):
    olds = scratch[0:3]
    u0, u1, k_ref, f_ref, omega, weight_sum, staged, moved, final_send, final_recv = scratch[3:13]
    send_out, own_in, recv_out, recv_in, ghosts = [scratch[13 + 3 * i : 16 + 3 * i] for i in range(5)]
    flags, acc, mine, all_sums, rows_e = scratch[28:33]
    in_sem, move_send, move_recv, out_send, out_recv, inner_send, inner_recv = scratch[33:40]
    flag_send, flag_recv, last_send, last_recv, sum_send, sum_recv = scratch[40:46]

    group, member = lax.axis_index("group"), lax.axis_index("member")
    here = group * members + member
    odd = here % 2 == 1
    even = here % 2 == 0
    has_q = here < devices - 1
    q_stays = jnp.logical_and(odd, has_q)
    p_split = jnp.logical_and(even, here > 0)
    around = [octet_neighbors(here, devices), octet_neighbors(here + 1, devices)]
    lane = lax.broadcasted_iota(jnp.int32, (8, LANES), 1)
    depth = lane % EDGE

    def where_is(index):
        return (index // members, index % members)

    loads = [
        pltpu.make_async_copy(ref, olds[i], in_sem.at[i]) for i, ref in enumerate((u_old, k_old, f_old))
    ]
    for load in loads:
        load.start()

    def both(*preds):
        result = preds[0]
        for pred in preds[1:]:
            result = jnp.logical_and(result, pred)
        return result

    outgoing, incoming = {}, {}
    for s in (0, 1):
        for axis in range(3):
            for side in (0, 1):
                inside, index = around[s][axis][side]
                exists = inside if s == 0 else both(inside, has_q)
                stays = inside if s == 0 else both(inside, q_stays)
                holder = both(index % 2 == 0, index > 0)
                for t in (0, 1):
                    target = index if t == 0 else jnp.maximum(index - 1, 0)
                    first = exists if t == 0 else both(exists, holder)
                    if s == 1 and t == 0 and axis == 0 and side == 0:
                        first = both(first, odd)
                    later = stays if t == 0 else both(stays, holder)
                    outgoing[s, axis, side, t] = (target, (first, later, later))
                receives = inside if s == 0 else both(inside, q_stays)
                for src in (0, 1):
                    source = index if src == 0 else jnp.maximum(index - 1, 0)
                    first = receives if src == 0 else both(receives, index > 0)
                    if s == 0 and src == 1 and axis == 0 and side == 1:
                        first = both(first, odd)
                    later = receives if src == 0 else both(receives, holder)
                    incoming[s, src, axis, side] = (source, (first, later, later))

    barrier = pltpu.get_barrier_semaphore()
    expected = jnp.int32(members - 1)
    for step in range(1, members):
        pl.semaphore_signal(
            barrier, inc=1, device_id={"member": (member + step) % members}, device_id_type=MESH
        )
    for target, preds in outgoing.values():
        expected = expected + both(preds[0], target // members != group).astype(jnp.int32)
    for source, preds in incoming.values():

        @pl.when(both(preds[0], source // members != group))
        def _():
            pl.semaphore_signal(barrier, inc=1, device_id=where_is(source), device_id_type=MESH)

    last = member == members - 1
    sends_last = both(last, has_q)
    gets_last = group > 0
    next_group = jnp.minimum(group + 1, devices // members - 1)
    prev_last = jnp.maximum(group * members - 1, 0)
    expected = expected + jnp.where(sends_last, members, 0)

    @pl.when(gets_last)
    def _():
        pl.semaphore_signal(barrier, inc=1, device_id=where_is(prev_last), device_id_type=MESH)

    first_in_group = both(member == 0, gets_last)
    expected = expected + first_in_group.astype(jnp.int32)

    @pl.when(sends_last)
    def _():
        pl.semaphore_signal(barrier, inc=1, device_id=(next_group, 0), device_id_type=MESH)

    kept, onward = jnp.int32(0), jnp.int32(0)
    for slot in range(2 * NB):
        index = old_ids[slot]
        kept = kept + both(index >= here * NB, index < here * NB + NB).astype(jnp.int32)
        onward = onward + (index >= here * NB + NB).astype(jnp.int32)
    kept = jnp.minimum(kept, NB)
    lacking = NB - kept

    for b in range(NB):
        for face in range(6):
            has = jnp.where(nbrs[b, face] >= 0, 1.0, 0.0).astype(jnp.float32)
            flags[b, face : face + 1, :] = jnp.full((1, LANES), has, jnp.float32)
        half_scale = 0.5 + 0.5 * refine[b].astype(jnp.float32)
        flags[b, 6:7, :] = jnp.full((1, LANES), half_scale, jnp.float32)
        flags[b, 7:8, :] = 1.0 / jnp.full((1, LANES), half_scale, jnp.float32)

    def settle(i, store):
        loads[i].wait()

        def own(p, carry):
            slot = jnp.maximum(p - lacking, 0)
            for tile in range(TILES):
                for part in range(PARTS):
                    value = olds[i][slot, 8 * part : 8 * part + 8, LANES * tile : LANES * (tile + 1)]
                    store(p, tile, part, jnp.where(p >= lacking, value, 0.0))
            return carry

        def following(p, carry):
            for tile in range(TILES):
                for part in range(PARTS):
                    value = olds[i][kept + p, 8 * part : 8 * part + 8, LANES * tile : LANES * (tile + 1)]
                    value = jnp.where(p < onward, value, 0.0)
                    store(NB + p, tile, part, value)
                    staged[i, p, flat(tile, part), :] = value
            return carry

        lax.fori_loop(0, NB, own, 0)
        lax.fori_loop(0, NB, following, 0)

    def pack(phase, s, field, volume, outer=True, inner=True):
        rows = EDGE * field

        def put(axis, side, bit, start, value):
            here_rows = pl.ds(rows + start, 8)
            if side == bit:
                send_out[phase][s, 2 * axis + side, here_rows, :] = value
            else:
                own_in[phase][s, bit, 3 * 0 + axis, here_rows, :] = value

        def wanted(side, bit):
            return outer if side == bit else inner

        for bit in (0, 1):
            for side in (0, 1):
                if not wanted(side, bit):
                    continue
                for j, b in enumerate(blocks_of(0, bit)):
                    line = volume[NB * s + b, pl.ds(PITCH + 8 + 31 * side, 8, stride=PITCH), :]
                    put(0, side, bit, 8 * j, line)
                for part in range(PARTS):
                    packed = jnp.zeros((8, LANES), jnp.float32)
                    for j, b in enumerate(blocks_of(1, bit)):
                        piece = volume[NB * s + b, spot(7 * side, part), :]
                        packed = jnp.where(lane // EDGE == j, roll(piece, EDGE * (j - 3 * side)), packed)
                    put(1, side, bit, 8 * part, packed)
            for quad in range(4):
                packed = [jnp.zeros((8, LANES), jnp.float32) for _ in (0, 1)]
                for half in (0, 1):
                    for j, b in enumerate(blocks_of(2, bit)):
                        for part in range(PARTS):
                            slot = 16 * half + 4 * j + part
                            piece = roll(volume[NB * s + b, spot(quad + 4 * half, part), :], slot)
                            for side in (0, 1):
                                if wanted(side, bit):
                                    packed[side] = jnp.where(
                                        depth == (slot + 31 * side) % EDGE, piece, packed[side]
                                    )
                for side in (0, 1):
                    if wanted(side, bit):
                        put(2, side, bit, 8 * quad, packed[side])

    def out_copy(phase, s, axis, side, t, target):
        return pltpu.make_async_remote_copy(
            src_ref=send_out[phase].at[s, 2 * axis + side],
            dst_ref=recv_out[phase].at[t, s, 2 * axis + 1 - side],
            send_sem=out_send.at[phase, s, 2 * axis + side, t],
            recv_sem=out_recv.at[phase, t, s, 2 * axis + 1 - side],
            device_id=where_is(target),
            device_id_type=MESH,
        )

    follower = jnp.minimum(here + 1, devices - 1)
    leader = jnp.maximum(here - 1, 0)

    def inner_copy(phase, s):
        return pltpu.make_async_remote_copy(
            src_ref=own_in[phase].at[s, 1 - s],
            dst_ref=recv_in[phase].at[1 - s],
            send_sem=inner_send.at[phase, s],
            recv_sem=inner_recv.at[phase, 1 - s],
            device_id=where_is(follower if s else leader),
            device_id_type=MESH,
        )

    flag_copy = pltpu.make_async_remote_copy(
        src_ref=flags.at[pl.ds(0, NB)],
        dst_ref=flags.at[pl.ds(NB, NB)],
        send_sem=flag_send,
        recv_sem=flag_recv,
        device_id=where_is(leader),
        device_id_type=MESH,
    )
    moves = [
        pltpu.make_async_remote_copy(
            src_ref=staged.at[i],
            dst_ref=moved.at[i],
            send_sem=move_send.at[i],
            recv_sem=move_recv.at[i],
            device_id=where_is(follower),
            device_id_type=MESH,
        )
        for i in range(3)
    ]

    def start_exchange(phase):
        for (s, axis, side, t), (target, preds) in outgoing.items():

            @pl.when(preds[phase])
            def _():
                out_copy(phase, s, axis, side, t, target).start()

        @pl.when(q_stays)
        def _():
            inner_copy(phase, 1).start()

        @pl.when(p_split)
        def _():
            inner_copy(phase, 0).start()

    def finish_exchange(phase):
        for (s, axis, side, t), (target, preds) in outgoing.items():

            @pl.when(preds[phase])
            def _():
                out_copy(phase, s, axis, side, t, target).wait_send()

        for (t, src, axis, side), (source, preds) in incoming.items():

            @pl.when(preds[phase])
            def _():
                out_copy(phase, src, axis, 1 - side, t, source).wait_recv()

        @pl.when(q_stays)
        def _():
            inner_copy(phase, 1).wait_send()
            inner_copy(phase, 0).wait_recv()

        @pl.when(p_split)
        def _():
            inner_copy(phase, 0).wait_send()
            inner_copy(phase, 1).wait_recv()

    def gather_ghosts(phase, t):
        split = (p_split, q_stays)[t]
        for axis in range(3):
            for side in (0, 1):
                face = 2 * axis + side
                total = 0.0
                for src in (0, 1):
                    pred = incoming[t, src, axis, side][1][phase]
                    if phase == 0 and (t, src, axis, side) == (0, 1, 0, 1):
                        own = jnp.where(even, send_out[0][1, 0], 0.0)
                        total = total + jnp.where(pred, recv_out[0][t, src, face], own)
                    else:
                        total = total + jnp.where(pred, recv_out[phase][t, src, face], 0.0)
                ghosts[phase][t, face] = total
                total = own_in[phase][t, side, axis]
                if side == t:
                    total = total + jnp.where(split, recv_in[phase][t, axis], 0.0)
                ghosts[phase][t, 6 + face] = total

    def fill(phase, q, field, volume, mirror):
        s, p = q // NB, q % NB
        rows = EDGE * field
        js = (p // 2, p % 2 + p // 4 * 2, p % 4)
        for side in (0, 1):
            kind = [jnp.where((p // 2**axis) % 2 == side, 0, 6) for axis in range(2)]
            ghost = ghosts[phase][s, kind[0] + side, pl.ds(pl.multiple_of(rows + 8 * js[0], 8), 8), :]
            has = flags[q, side : side + 1, :] > 0.5
            if mirror:
                spare = volume[q, pl.ds(PITCH + 8 + 31 * side, 8, stride=PITCH), :]
            else:
                spare = jnp.zeros_like(ghost)
            volume[q, pl.ds(PITCH + 7 + 33 * side, 8, stride=PITCH), :] = jnp.where(has, ghost, spare)
            has = flags[q, 2 + side : 3 + side, :] > 0.5
            for part in range(PARTS):
                ghost = ghosts[phase][s, kind[1] + 2 + side, rows + 8 * part : rows + 8 * part + 8, :]
                steps = EDGE * (3 - js[1]) if side == 0 else EDGE * ((4 - js[1]) % 4)
                ghost = pltpu.roll(ghost, steps, 1)
                if mirror:
                    spare = roll(volume[q, spot(7 * side, part), :], 96 - 64 * side)
                else:
                    spare = jnp.zeros_like(ghost)
                volume[q, spot(9 * side - 1, part), :] = jnp.where(has, ghost, spare)

    def stencil(phase, q, field, volume, mirror, part):
        s, p = q // NB, q % NB
        j = p % 4
        rows = EDGE * field
        bit = p // 4 % 2
        low_face = jnp.where(bit == 0, 0, 6) + 4
        high_face = jnp.where(bit == 1, 0, 6) + 5
        near = depth < EDGE // 2
        has = jnp.where(near, flags[q, 4:5, :], flags[q, 5:6, :]) > 0.5
        tiles = [volume[q, spot(t, part), :] for t in range(-1, TILES + 1)]
        down = [roll(t, EDGE) for t in tiles[:-1]]
        up = [None] + [roll(t, -EDGE) for t in tiles[1:]]
        for tile in range(TILES):
            value = tiles[tile + 1]
            top = PITCH * (tile + 1) + 8 + 8 * part
            x_minus = volume[q, top - 1 : top + 7, :]
            x_plus = volume[q, top + 1 : top + 9, :]
            y_minus = jnp.where(lane >= EDGE, down[tile + 1], down[tile])
            y_plus = jnp.where(lane < 3 * EDGE, up[tile + 1], up[tile + 2])
            base = 16 * (tile // 4) + part
            sheet = slice(rows + 8 * (tile % 4), rows + 8 * (tile % 4) + 8)
            low = pltpu.roll(ghosts[phase][s, low_face, sheet, :], 97 - base - 4 * j, 1)
            high = pltpu.roll(ghosts[phase][s, high_face, sheet, :], 31 - base - 4 * j, 1)
            edge = jnp.where(has, jnp.where(near, low, high), value if mirror else 0.0)
            z_minus = jnp.where(depth == 0, edge, roll(value, 1))
            z_plus = jnp.where(depth == EDGE - 1, edge, roll(value, -1))
            yield tile, value, (x_minus, x_plus, y_minus, y_plus, z_minus, z_plus)

    def valid(q):
        low = jnp.where(even, lacking, 0)
        return both(q >= low, q < NB + onward)

    def first_sweep(q, carry):
        fill(0, q, 0, u0, False)
        fill(0, q, 1, k_ref, True)
        holds = valid(q)
        for part in range(PARTS):
            pairs = zip(stencil(0, q, 0, u0, False, part), stencil(0, q, 1, k_ref, True, part))
            for (tile, u, u_beside), (_, k, k_beside) in pairs:
                weights = [k + beside for beside in k_beside]
                total = sum(weights[1:], weights[0])
                scale = jnp.where(holds, OMEGA / total, 0.0)
                place = flat(tile, part)
                weight_sum[q, place, :] = total * flags[q, 6:7, :] * (1.0 / OMEGA)
                gain = f_ref[q, place, :] * scale * flags[q, 7:8, :]
                f_ref[q, place, :] = gain
                new = (1.0 - OMEGA) * u + gain
                for face in range(6):
                    weight = weights[face] * scale
                    omega[q, face, place, :] = weight
                    new = new + weight * u_beside[face]
                u1[q, spot(tile, part), :] = new
        return carry

    def second_sweep(q, send):
        fill(1, q, 0, u1, False)
        for part in range(PARTS):
            for tile, u, beside in stencil(1, q, 0, u1, False, part):
                place = flat(tile, part)
                new = (1.0 - OMEGA) * u + f_ref[q, place, :]
                for face in range(6):
                    new = new + omega[q, face, place, :] * beside[face]
                u0[q, spot(tile, part), :] = new
                if send:
                    final_send[q - NB, place, :] = new

    def residual(q, carry):
        fill(2, q, 0, u0, False)
        totals = [jnp.zeros((8, LANES), jnp.float32) for _ in range(4)]
        for part in range(PARTS):
            for tile, u, beside in stencil(2, q, 0, u0, False, part):
                place = flat(tile, part)
                change = f_ref[q, place, :] - OMEGA * u
                for face in range(6):
                    change = change + omega[q, face, place, :] * beside[face]
                cell = part // 2 * 2 + tile // 4
                totals[cell] = totals[cell] + change * weight_sum[q, place, :]
        holds = valid(q)
        for cell in range(4):
            acc[4 * q + cell] = jnp.where(holds, totals[cell], 0.0)
        return carry

    sets = jnp.where(odd, 2, 1)
    blocks = NB * sets

    def pack_all(phase, field, volume):
        def body(s, carry):
            pack(phase, s, field, volume)
            return carry

        lax.fori_loop(0, 2 if phase == 0 else sets, body, 0)

    def gather_all(phase):
        gather_ghosts(phase, 0)

        @pl.when(odd)
        def _():
            gather_ghosts(phase, 1)

    def to_volume(volume):
        def store(q, tile, part, value):
            volume[q, spot(tile, part), :] = value

        return store

    def to_source(q, tile, part, value):
        f_ref[q, flat(tile, part), :] = value

    settle(0, to_volume(u0))
    pack_all(0, 0, u0)
    settle(1, to_volume(k_ref))
    pack_all(0, 1, k_ref)
    pl.semaphore_wait(barrier, expected)
    start_exchange(0)

    @pl.when(p_split)
    def _():
        flag_copy.start()

    @pl.when(even)
    def _():
        moves[0].start()
        moves[1].start()

    settle(2, to_source)

    @pl.when(even)
    def _():
        moves[2].start()

    @pl.when(odd)
    def _():
        for i in range(3):
            moves[i].wait_recv()

        def merge(p, carry):
            for tile in range(TILES):
                for part in range(PARTS):
                    for i, volume in enumerate((u0, k_ref)):
                        volume[p, spot(tile, part), :] += moved[i, p, flat(tile, part), :]
                    f_ref[p, flat(tile, part), :] += moved[2, p, flat(tile, part), :]
            return carry

        lax.fori_loop(0, NB, merge, 0)
        pack(0, 0, 0, u0, outer=False)
        pack(0, 0, 1, k_ref, outer=False)

    finish_exchange(0)

    @pl.when(p_split)
    def _():
        flag_copy.wait_send()

    @pl.when(q_stays)
    def _():
        flag_copy.wait_recv()

    gather_all(0)
    lax.fori_loop(0, blocks, first_sweep, 0)

    pack_all(1, 0, u1)
    start_exchange(1)
    finish_exchange(1)
    gather_all(1)

    def final_copy(p):
        return pltpu.make_async_remote_copy(
            src_ref=final_send.at[p],
            dst_ref=final_recv.at[p],
            send_sem=last_send.at[p],
            recv_sem=last_recv.at[p],
            device_id=where_is(follower),
            device_id_type=MESH,
        )

    @pl.when(odd)
    def _():
        def body(q, carry):
            second_sweep(q, True)

            @pl.when(has_q)
            def _():
                final_copy(q - NB).start()

            return carry

        lax.fori_loop(NB, 2 * NB, body, 0)

    def body(q, carry):
        second_sweep(q, False)
        return carry

    lax.fori_loop(0, NB, body, 0)

    pack_all(2, 0, u0)
    start_exchange(2)
    finish_exchange(2)
    gather_all(2)
    lax.fori_loop(0, blocks, residual, 0)

    sums = jnp.sum(acc[...], axis=1)
    halves = lax.broadcasted_iota(jnp.int32, (LANES, LANES), 0) % EDGE // (EDGE // 2)
    choose = halves == lax.broadcasted_iota(jnp.int32, (LANES, LANES), 1) % 2
    cells = jnp.dot(
        sums, choose.astype(jnp.float32), precision=HIGHEST, preferred_element_type=jnp.float32
    )
    row = lax.broadcasted_iota(jnp.int32, (8 * NB, LANES), 0)
    column = lax.broadcasted_iota(jnp.int32, (8 * NB, LANES), 1) // 2
    odd_int = odd.astype(jnp.int32)
    picked = jnp.logical_and((row + 32 * odd_int) % 64 == column, row < 32 + 32 * odd_int)
    total = jnp.sum(jnp.where(picked, cells, 0.0), axis=0, keepdims=True)
    mine[...] = jnp.broadcast_to(total * (EDGE // 2) ** (-1.5), (8, LANES))

    def sum_copy(step):
        return pltpu.make_async_remote_copy(
            src_ref=mine,
            dst_ref=all_sums.at[member],
            send_sem=sum_send.at[step],
            recv_sem=sum_recv.at[step],
            device_id={"member": (member + step) % members},
            device_id_type=MESH,
        )

    def on_copy(step):
        return pltpu.make_async_remote_copy(
            src_ref=mine,
            dst_ref=all_sums.at[members],
            send_sem=sum_send.at[members + step],
            recv_sem=sum_recv.at[0],
            device_id=(next_group, step),
            device_id_type=MESH,
        )

    for step in range(1, members):
        sum_copy(step).start()

    @pl.when(sends_last)
    def _():
        for step in range(members):
            on_copy(step).start()

    all_sums[member] = mine[...]
    for step in range(1, members):
        sum_copy(step).wait_send()
        sum_copy(step).wait_recv()

    @pl.when(sends_last)
    def _():
        for step in range(members):
            on_copy(step).wait_send()

    @pl.when(gets_last)
    def _():
        on_copy(0).wait_recv()

    correction = jnp.zeros((8 * NB, LANES), jnp.float32)
    lane_row = lax.broadcasted_iota(jnp.int32, (1, LANES), 1)
    for pair in range(members // 2):
        if pair == 0:
            before = jnp.where(gets_last, all_sums[members, 0:1, :], 0.0)
        else:
            before = all_sums[2 * pair - 1, 0:1, :]
        even_cells = all_sums[2 * pair, 0:1, :] + before
        vector = jnp.where(lane_row < 64, even_cells, all_sums[2 * pair + 1, 0:1, :])
        correction = correction + inverse[0, :, LANES * pair : LANES * (pair + 1)] * vector
    rows_e[...] = jnp.broadcast_to(jnp.sum(correction, axis=1, keepdims=True), (8 * NB, LANES))

    @pl.when(p_split)
    def _():
        for p in range(NB):
            final_copy(p).wait_recv()

    def finish(p, carry):
        for cell in range(4):
            first = pl.multiple_of(8 * p, 8) + 2 * cell
            lift = jnp.where(depth < EDGE // 2, rows_e[pl.ds(first, 1), :], rows_e[pl.ds(first + 1, 1), :])
            for part in (2 * (cell // 2), 2 * (cell // 2) + 1):
                for tile in range(4 * (cell % 2), 4 * (cell % 2) + 4):
                    arrived = jnp.where(p_split, final_recv[p, flat(tile, part), :], 0.0)
                    value = u0[p, spot(tile, part), :] + arrived + lift
                    out_ref[p, 8 * part : 8 * part + 8, LANES * tile : LANES * (tile + 1)] = value
        return carry

    lax.fori_loop(0, NB, finish, 0)

    @pl.when(even)
    def _():
        for i in range(3):
            moves[i].wait_send()

    @pl.when(q_stays)
    def _():
        for p in range(NB):
            final_copy(p).wait_send()


def local(old_ids, field_old, source_old, kappa_old, refine, neighbors, coarse_inverse):
    members = lax.axis_size("member")
    devices = lax.axis_size(AXES)
    flat_shape = (NB, TILES * EDGE, LANES)
    both_shape = (2 * NB, TILES * EDGE, LANES)
    padded = (2 * NB, 10 * PITCH, LANES)
    shapes = [field_old.shape] * 3 + [padded] * 3 + [both_shape]
    shapes += [(2 * NB, 6, TILES * EDGE, LANES), both_shape, (3,) + flat_shape, (3,) + flat_shape]
    shapes += [flat_shape, flat_shape]
    shapes += [(2, 6, EDGE * n, LANES) for n in FIELDS]
    shapes += [(2, 2, 3, EDGE * n, LANES) for n in FIELDS]
    shapes += [(2, 2, 6, EDGE * n, LANES) for n in FIELDS]
    shapes += [(2, 3, EDGE * n, LANES) for n in FIELDS]
    shapes += [(2, 12, EDGE * n, LANES) for n in FIELDS]
    shapes += [(2 * NB, 8, LANES), (8 * NB, 8, LANES), (8, LANES), (members + 1, 8, LANES)]
    shapes += [(8 * NB, LANES)]
    dma = pltpu.SemaphoreType.DMA
    scratch = [pltpu.VMEM(s, jnp.float32) for s in shapes]
    scratch += [dma((3,)), dma((3,)), dma((3,)), dma((3, 2, 6, 2)), dma((3, 2, 2, 6))]
    scratch += [dma((3, 2)), dma((3, 2)), dma, dma, dma((NB,)), dma((NB,))]
    scratch += [dma((2 * members,)), dma((members,))]
    return pl.pallas_call(
        functools.partial(main_kernel, members, devices),
        out_shape=jax.ShapeDtypeStruct((NB, EDGE, FACE), jnp.float32),
        in_specs=[SM, SM, SM, VM, ANY, ANY, ANY],
        out_specs=VM,
        scratch_shapes=scratch,
        compiler_params=pltpu.CompilerParams(
            collective_id=1, has_side_effects=True, vmem_limit_bytes=VMEM_LIMIT
        ),
    )(old_ids, neighbors, refine, coarse_inverse, field_old, source_old, kappa_old)


def solution(mesh):
    in_specs = (
        P(AXES),
        P(AXES, None, None),
        P(AXES, None, None),
        P(AXES, None, None),
        P(AXES),
        P(AXES, None),
        P("group", "member", None),
    )
    return jax.shard_map(
        local, mesh=mesh, in_specs=in_specs, out_specs=P(AXES, None, None), check_vma=False
    )
```

```python
import functools

import jax
import jax.numpy as jnp
from jax import lax
from jax.experimental import pallas as pl
from jax.experimental.pallas import tpu as pltpu
from jax.sharding import PartitionSpec as P

OMEGA = 0.8
AXES = ("group", "member")
NB, EDGE, FACE, LANES = 8, 32, 1024, 128
TILES, PARTS, PITCH = 8, 4, 48
HIGHEST = lax.Precision.HIGHEST
VMEM_LIMIT = 60 * 2**20
VM = pl.BlockSpec(memory_space=pltpu.VMEM)
ANY = pl.BlockSpec(memory_space=pl.ANY)
SM = pl.BlockSpec(memory_space=pltpu.SMEM)
MESH = pl.DeviceIdType.MESH
FIELDS = (2, 1, 1)
EARLY = 4


def roll(value, steps):
    return pltpu.roll(value, steps % LANES, 1)


def spot(tile, part):
    return slice(PITCH * (tile + 1) + 8 + 8 * part, PITCH * (tile + 1) + 16 + 8 * part)


def flat(tile, part):
    return slice(EDGE * tile + 8 * part, EDGE * tile + 8 * part + 8)


def blocks_of(axis, side):
    return [b for b in range(NB) if (b >> axis) % 2 == side]


def octet_neighbors(octet, devices):
    nbits = devices.bit_length() - 1
    bits = [octet // 2**i % 2 for i in range(nbits)]
    result = []
    for axis in range(3):
        own = [i for i in range(nbits) if i % 3 == axis]
        extent = 2 ** len(own)
        coord = sum(bits[i] * 2**n for n, i in enumerate(own))
        base = octet - sum(bits[i] * 2**i for i in own)
        pair = []
        for step in (-1, 1):
            moved = coord + step
            inside = jnp.logical_and(moved >= 0, moved < extent)
            clipped = jnp.clip(moved, 0, extent - 1)
            index = base + sum(clipped // 2**n % 2 * 2**i for n, i in enumerate(own))
            pair.append((inside, index))
        result.append(pair)
    return result


def main_kernel(members, devices, old_ids, nbrs, refine, inverse, u_old, f_old, k_old, out_ref, *scratch):
    olds = scratch[0:3]
    u0, u1, k_ref, f_ref, omega, weight_sum, staged, moved, final_send, final_recv = scratch[3:13]
    send_out, own_in, recv_out, recv_in, ghosts = [scratch[13 + 3 * i : 16 + 3 * i] for i in range(5)]
    flags, acc, mine, all_sums, rows_e = scratch[28:33]
    in_sem, move_send, move_recv, out_send, out_recv, inner_send, inner_recv = scratch[33:40]
    flag_send, flag_recv, last_send, last_recv, sum_send, sum_recv = scratch[40:46]

    group, member = lax.axis_index("group"), lax.axis_index("member")
    here = group * members + member
    odd = here % 2 == 1
    even = here % 2 == 0
    has_q = here < devices - 1
    q_stays = jnp.logical_and(odd, has_q)
    p_split = jnp.logical_and(even, here > 0)
    around = [octet_neighbors(here, devices), octet_neighbors(here + 1, devices)]
    lane = lax.broadcasted_iota(jnp.int32, (8, LANES), 1)
    depth = lane % EDGE

    def where_is(index):
        return (index // members, index % members)

    loads = [
        pltpu.make_async_copy(ref, olds[i], in_sem.at[i]) for i, ref in enumerate((u_old, k_old, f_old))
    ]
    for load in loads:
        load.start()

    def both(*preds):
        result = preds[0]
        for pred in preds[1:]:
            result = jnp.logical_and(result, pred)
        return result

    outgoing, incoming = {}, {}
    for s in (0, 1):
        for axis in range(3):
            for side in (0, 1):
                inside, index = around[s][axis][side]
                exists = inside if s == 0 else both(inside, has_q)
                stays = inside if s == 0 else both(inside, q_stays)
                holder = both(index % 2 == 0, index > 0)
                for t in (0, 1):
                    target = index if t == 0 else jnp.maximum(index - 1, 0)
                    first = exists if t == 0 else both(exists, holder)
                    if s == 1 and t == 0 and axis == 0 and side == 0:
                        first = both(first, odd)
                    later = stays if t == 0 else both(stays, holder)
                    outgoing[s, axis, side, t] = (target, (first, later, later))
                receives = inside if s == 0 else both(inside, q_stays)
                for src in (0, 1):
                    source = index if src == 0 else jnp.maximum(index - 1, 0)
                    first = receives if src == 0 else both(receives, index > 0)
                    if s == 0 and src == 1 and axis == 0 and side == 1:
                        first = both(first, odd)
                    later = receives if src == 0 else both(receives, holder)
                    incoming[s, src, axis, side] = (source, (first, later, later))

    barrier = pltpu.get_barrier_semaphore()
    expected = jnp.int32(members - 1)
    for step in range(1, members):
        pl.semaphore_signal(
            barrier, inc=1, device_id={"member": (member + step) % members}, device_id_type=MESH
        )
    for target, preds in outgoing.values():
        expected = expected + both(preds[0], target // members != group).astype(jnp.int32)
    for source, preds in incoming.values():

        @pl.when(both(preds[0], source // members != group))
        def _():
            pl.semaphore_signal(barrier, inc=1, device_id=where_is(source), device_id_type=MESH)

    last = member == members - 1
    sends_last = both(last, has_q)
    gets_last = group > 0
    next_group = jnp.minimum(group + 1, devices // members - 1)
    prev_last = jnp.maximum(group * members - 1, 0)
    expected = expected + jnp.where(sends_last, members, 0)

    @pl.when(gets_last)
    def _():
        pl.semaphore_signal(barrier, inc=1, device_id=where_is(prev_last), device_id_type=MESH)

    first_in_group = both(member == 0, gets_last)
    expected = expected + first_in_group.astype(jnp.int32)

    @pl.when(sends_last)
    def _():
        pl.semaphore_signal(barrier, inc=1, device_id=(next_group, 0), device_id_type=MESH)

    kept, onward = jnp.int32(0), jnp.int32(0)
    for slot in range(2 * NB):
        index = old_ids[slot]
        kept = kept + both(index >= here * NB, index < here * NB + NB).astype(jnp.int32)
        onward = onward + (index >= here * NB + NB).astype(jnp.int32)
    kept = jnp.minimum(kept, NB)
    lacking = NB - kept

    for b in range(NB):
        for face in range(6):
            has = jnp.where(nbrs[b, face] >= 0, 1.0, 0.0).astype(jnp.float32)
            flags[b, face : face + 1, :] = jnp.full((1, LANES), has, jnp.float32)
        half_scale = 0.5 + 0.5 * refine[b].astype(jnp.float32)
        flags[b, 6:7, :] = jnp.full((1, LANES), half_scale, jnp.float32)
        flags[b, 7:8, :] = 1.0 / jnp.full((1, LANES), half_scale, jnp.float32)

    def settle(i, store):
        loads[i].wait()

        def own(p, carry):
            slot = jnp.maximum(p - lacking, 0)
            for tile in range(TILES):
                for part in range(PARTS):
                    value = olds[i][slot, 8 * part : 8 * part + 8, LANES * tile : LANES * (tile + 1)]
                    store(p, tile, part, jnp.where(p >= lacking, value, 0.0))
            return carry

        def following(p, carry):
            for tile in range(TILES):
                for part in range(PARTS):
                    value = olds[i][kept + p, 8 * part : 8 * part + 8, LANES * tile : LANES * (tile + 1)]
                    value = jnp.where(p < onward, value, 0.0)
                    store(NB + p, tile, part, value)
                    staged[i, p, flat(tile, part), :] = value
            return carry

        lax.fori_loop(0, NB, own, 0)
        lax.fori_loop(0, NB, following, 0)

    def pack(phase, s, field, volume, outer=True, inner=True):
        rows = EDGE * field

        def put(axis, side, bit, start, value):
            here_rows = pl.ds(rows + start, 8)
            if side == bit:
                send_out[phase][s, 2 * axis + side, here_rows, :] = value
            else:
                own_in[phase][s, bit, 3 * 0 + axis, here_rows, :] = value

        def wanted(side, bit):
            return outer if side == bit else inner

        for bit in (0, 1):
            for side in (0, 1):
                if not wanted(side, bit):
                    continue
                for j, b in enumerate(blocks_of(0, bit)):
                    line = volume[NB * s + b, pl.ds(PITCH + 8 + 31 * side, 8, stride=PITCH), :]
                    put(0, side, bit, 8 * j, line)
                for part in range(PARTS):
                    packed = jnp.zeros((8, LANES), jnp.float32)
                    for j, b in enumerate(blocks_of(1, bit)):
                        piece = volume[NB * s + b, spot(7 * side, part), :]
                        packed = jnp.where(lane // EDGE == j, roll(piece, EDGE * (j - 3 * side)), packed)
                    put(1, side, bit, 8 * part, packed)
            for quad in range(4):
                packed = [jnp.zeros((8, LANES), jnp.float32) for _ in (0, 1)]
                for half in (0, 1):
                    for j, b in enumerate(blocks_of(2, bit)):
                        for part in range(PARTS):
                            slot = 16 * half + 4 * j + part
                            piece = roll(volume[NB * s + b, spot(quad + 4 * half, part), :], slot)
                            for side in (0, 1):
                                if wanted(side, bit):
                                    packed[side] = jnp.where(
                                        depth == (slot + 31 * side) % EDGE, piece, packed[side]
                                    )
                for side in (0, 1):
                    if wanted(side, bit):
                        put(2, side, bit, 8 * quad, packed[side])

    def out_copy(phase, s, axis, side, t, target):
        return pltpu.make_async_remote_copy(
            src_ref=send_out[phase].at[s, 2 * axis + side],
            dst_ref=recv_out[phase].at[t, s, 2 * axis + 1 - side],
            send_sem=out_send.at[phase, s, 2 * axis + side, t],
            recv_sem=out_recv.at[phase, t, s, 2 * axis + 1 - side],
            device_id=where_is(target),
            device_id_type=MESH,
        )

    follower = jnp.minimum(here + 1, devices - 1)
    leader = jnp.maximum(here - 1, 0)

    def inner_copy(phase, s):
        return pltpu.make_async_remote_copy(
            src_ref=own_in[phase].at[s, 1 - s],
            dst_ref=recv_in[phase].at[1 - s],
            send_sem=inner_send.at[phase, s],
            recv_sem=inner_recv.at[phase, 1 - s],
            device_id=where_is(follower if s else leader),
            device_id_type=MESH,
        )

    flag_copy = pltpu.make_async_remote_copy(
        src_ref=flags.at[pl.ds(0, NB)],
        dst_ref=flags.at[pl.ds(NB, NB)],
        send_sem=flag_send,
        recv_sem=flag_recv,
        device_id=where_is(leader),
        device_id_type=MESH,
    )
    moves = [
        pltpu.make_async_remote_copy(
            src_ref=staged.at[i],
            dst_ref=moved.at[i],
            send_sem=move_send.at[i],
            recv_sem=move_recv.at[i],
            device_id=where_is(follower),
            device_id_type=MESH,
        )
        for i in range(3)
    ]

    def start_exchange(phase):
        for (s, axis, side, t), (target, preds) in outgoing.items():

            @pl.when(preds[phase])
            def _():
                out_copy(phase, s, axis, side, t, target).start()

        @pl.when(q_stays)
        def _():
            inner_copy(phase, 1).start()

        @pl.when(p_split)
        def _():
            inner_copy(phase, 0).start()

    def finish_exchange(phase):
        for (s, axis, side, t), (target, preds) in outgoing.items():

            @pl.when(preds[phase])
            def _():
                out_copy(phase, s, axis, side, t, target).wait_send()

        for (t, src, axis, side), (source, preds) in incoming.items():

            @pl.when(preds[phase])
            def _():
                out_copy(phase, src, axis, 1 - side, t, source).wait_recv()

        @pl.when(q_stays)
        def _():
            inner_copy(phase, 1).wait_send()
            inner_copy(phase, 0).wait_recv()

        @pl.when(p_split)
        def _():
            inner_copy(phase, 0).wait_send()
            inner_copy(phase, 1).wait_recv()

    def gather_ghosts(phase, t):
        split = (p_split, q_stays)[t]
        for axis in range(3):
            for side in (0, 1):
                face = 2 * axis + side
                total = 0.0
                for src in (0, 1):
                    pred = incoming[t, src, axis, side][1][phase]
                    if phase == 0 and (t, src, axis, side) == (0, 1, 0, 1):
                        own = jnp.where(even, send_out[0][1, 0], 0.0)
                        total = total + jnp.where(pred, recv_out[0][t, src, face], own)
                    else:
                        total = total + jnp.where(pred, recv_out[phase][t, src, face], 0.0)
                ghosts[phase][t, face] = total
                total = own_in[phase][t, side, axis]
                if side == t:
                    total = total + jnp.where(split, recv_in[phase][t, axis], 0.0)
                ghosts[phase][t, 6 + face] = total

    def fill(phase, q, field, volume, mirror):
        s, p = q // NB, q % NB
        rows = EDGE * field
        js = (p // 2, p % 2 + p // 4 * 2, p % 4)
        for side in (0, 1):
            kind = [jnp.where((p // 2**axis) % 2 == side, 0, 6) for axis in range(2)]
            ghost = ghosts[phase][s, kind[0] + side, pl.ds(pl.multiple_of(rows + 8 * js[0], 8), 8), :]
            has = flags[q, side : side + 1, :] > 0.5
            if mirror:
                spare = volume[q, pl.ds(PITCH + 8 + 31 * side, 8, stride=PITCH), :]
            else:
                spare = jnp.zeros_like(ghost)
            volume[q, pl.ds(PITCH + 7 + 33 * side, 8, stride=PITCH), :] = jnp.where(has, ghost, spare)
            has = flags[q, 2 + side : 3 + side, :] > 0.5
            for part in range(PARTS):
                ghost = ghosts[phase][s, kind[1] + 2 + side, rows + 8 * part : rows + 8 * part + 8, :]
                steps = EDGE * (3 - js[1]) if side == 0 else EDGE * ((4 - js[1]) % 4)
                ghost = pltpu.roll(ghost, steps, 1)
                if mirror:
                    spare = roll(volume[q, spot(7 * side, part), :], 96 - 64 * side)
                else:
                    spare = jnp.zeros_like(ghost)
                volume[q, spot(9 * side - 1, part), :] = jnp.where(has, ghost, spare)

    def stencil(phase, q, field, volume, mirror, part):
        s, p = q // NB, q % NB
        j = p % 4
        rows = EDGE * field
        bit = p // 4 % 2
        low_face = jnp.where(bit == 0, 0, 6) + 4
        high_face = jnp.where(bit == 1, 0, 6) + 5
        near = depth < EDGE // 2
        has = jnp.where(near, flags[q, 4:5, :], flags[q, 5:6, :]) > 0.5
        tiles = [volume[q, spot(t, part), :] for t in range(-1, TILES + 1)]
        down = [roll(t, EDGE) for t in tiles[:-1]]
        up = [None] + [roll(t, -EDGE) for t in tiles[1:]]
        for tile in range(TILES):
            value = tiles[tile + 1]
            top = PITCH * (tile + 1) + 8 + 8 * part
            x_minus = volume[q, top - 1 : top + 7, :]
            x_plus = volume[q, top + 1 : top + 9, :]
            y_minus = jnp.where(lane >= EDGE, down[tile + 1], down[tile])
            y_plus = jnp.where(lane < 3 * EDGE, up[tile + 1], up[tile + 2])
            base = 16 * (tile // 4) + part
            sheet = slice(rows + 8 * (tile % 4), rows + 8 * (tile % 4) + 8)
            low = pltpu.roll(ghosts[phase][s, low_face, sheet, :], 97 - base - 4 * j, 1)
            high = pltpu.roll(ghosts[phase][s, high_face, sheet, :], 31 - base - 4 * j, 1)
            edge = jnp.where(has, jnp.where(near, low, high), value if mirror else 0.0)
            z_minus = jnp.where(depth == 0, edge, roll(value, 1))
            z_plus = jnp.where(depth == EDGE - 1, edge, roll(value, -1))
            yield tile, value, (x_minus, x_plus, y_minus, y_plus, z_minus, z_plus)

    def valid(q):
        low = jnp.where(even, lacking, 0)
        return both(q >= low, q < NB + onward)

    def first_sweep(q, carry):
        fill(0, q, 0, u0, False)
        fill(0, q, 1, k_ref, True)
        holds = valid(q)
        for part in range(PARTS):
            pairs = zip(stencil(0, q, 0, u0, False, part), stencil(0, q, 1, k_ref, True, part))
            for (tile, u, u_beside), (_, k, k_beside) in pairs:
                weights = [k + beside for beside in k_beside]
                total = sum(weights[1:], weights[0])
                scale = jnp.where(holds, OMEGA / total, 0.0)
                place = flat(tile, part)
                weight_sum[q, place, :] = total * flags[q, 6:7, :] * (1.0 / OMEGA)
                gain = f_ref[q, place, :] * scale * flags[q, 7:8, :]
                f_ref[q, place, :] = gain
                new = (1.0 - OMEGA) * u + gain
                for face in range(6):
                    weight = weights[face] * scale
                    omega[q, face, place, :] = weight
                    new = new + weight * u_beside[face]
                u1[q, spot(tile, part), :] = new
        return carry

    def second_sweep(q, send):
        fill(1, q, 0, u1, False)
        for part in range(PARTS):
            for tile, u, beside in stencil(1, q, 0, u1, False, part):
                place = flat(tile, part)
                new = (1.0 - OMEGA) * u + f_ref[q, place, :]
                for face in range(6):
                    new = new + omega[q, face, place, :] * beside[face]
                u0[q, spot(tile, part), :] = new
                if send:
                    final_send[q - NB, place, :] = new

    def residual(q, carry):
        fill(2, q, 0, u0, False)
        totals = [jnp.zeros((8, LANES), jnp.float32) for _ in range(4)]
        for part in range(PARTS):
            for tile, u, beside in stencil(2, q, 0, u0, False, part):
                place = flat(tile, part)
                change = f_ref[q, place, :] - OMEGA * u
                for face in range(6):
                    change = change + omega[q, face, place, :] * beside[face]
                cell = part // 2 * 2 + tile // 4
                totals[cell] = totals[cell] + change * weight_sum[q, place, :]
        holds = valid(q)
        for cell in range(4):
            acc[4 * q + cell] = jnp.where(holds, totals[cell], 0.0)
        return carry

    sets = jnp.where(odd, 2, 1)
    blocks = NB * sets

    def pack_all(phase, field, volume):
        def body(s, carry):
            pack(phase, s, field, volume)
            return carry

        lax.fori_loop(0, 2 if phase == 0 else sets, body, 0)

    def gather_all(phase):
        gather_ghosts(phase, 0)

        @pl.when(odd)
        def _():
            gather_ghosts(phase, 1)

    def to_volume(volume):
        def store(q, tile, part, value):
            volume[q, spot(tile, part), :] = value

        return store

    def to_source(q, tile, part, value):
        f_ref[q, flat(tile, part), :] = value

    settle(0, to_volume(u0))
    pack_all(0, 0, u0)
    settle(1, to_volume(k_ref))
    pack_all(0, 1, k_ref)
    pl.semaphore_wait(barrier, expected)
    start_exchange(0)

    @pl.when(p_split)
    def _():
        flag_copy.start()

    @pl.when(even)
    def _():
        moves[0].start()
        moves[1].start()

    settle(2, to_source)

    @pl.when(even)
    def _():
        moves[2].start()

    @pl.when(odd)
    def _():
        for i in range(3):
            moves[i].wait_recv()

        def merge(p, carry):
            for tile in range(TILES):
                for part in range(PARTS):
                    for i, volume in enumerate((u0, k_ref)):
                        volume[p, spot(tile, part), :] += moved[i, p, flat(tile, part), :]
                    f_ref[p, flat(tile, part), :] += moved[2, p, flat(tile, part), :]
            return carry

        lax.fori_loop(0, NB, merge, 0)
        pack(0, 0, 0, u0, outer=False)
        pack(0, 0, 1, k_ref, outer=False)

    finish_exchange(0)

    @pl.when(p_split)
    def _():
        flag_copy.wait_send()

    @pl.when(q_stays)
    def _():
        flag_copy.wait_recv()

    gather_all(0)
    lax.fori_loop(0, blocks, first_sweep, 0)

    pack_all(1, 0, u1)
    start_exchange(1)
    finish_exchange(1)
    gather_all(1)

    def final_copy(p):
        return pltpu.make_async_remote_copy(
            src_ref=final_send.at[p],
            dst_ref=final_recv.at[p],
            send_sem=last_send.at[p],
            recv_sem=last_recv.at[p],
            device_id=where_is(follower),
            device_id_type=MESH,
        )

    @pl.when(odd)
    def _():
        def body(q, carry):
            second_sweep(q, True)

            @pl.when(both(has_q, q < NB + EARLY))
            def _():
                final_copy(q - NB).start()

            return carry

        lax.fori_loop(NB, 2 * NB, body, 0)

    def body(q, carry):
        second_sweep(q, False)
        return carry

    lax.fori_loop(0, NB, body, 0)

    pack_all(2, 0, u0)
    start_exchange(2)

    @pl.when(q_stays)
    def _():
        for p in range(EARLY, NB):
            final_copy(p).start()

    finish_exchange(2)
    gather_all(2)
    lax.fori_loop(0, blocks, residual, 0)

    sums = jnp.sum(acc[...], axis=1)
    halves = lax.broadcasted_iota(jnp.int32, (LANES, LANES), 0) % EDGE // (EDGE // 2)
    choose = halves == lax.broadcasted_iota(jnp.int32, (LANES, LANES), 1) % 2
    cells = jnp.dot(
        sums, choose.astype(jnp.float32), precision=HIGHEST, preferred_element_type=jnp.float32
    )
    row = lax.broadcasted_iota(jnp.int32, (8 * NB, LANES), 0)
    column = lax.broadcasted_iota(jnp.int32, (8 * NB, LANES), 1) // 2
    odd_int = odd.astype(jnp.int32)
    picked = jnp.logical_and((row + 32 * odd_int) % 64 == column, row < 32 + 32 * odd_int)
    total = jnp.sum(jnp.where(picked, cells, 0.0), axis=0, keepdims=True)
    mine[...] = jnp.broadcast_to(total * (EDGE // 2) ** (-1.5), (8, LANES))

    def sum_copy(step):
        return pltpu.make_async_remote_copy(
            src_ref=mine,
            dst_ref=all_sums.at[member],
            send_sem=sum_send.at[step],
            recv_sem=sum_recv.at[step],
            device_id={"member": (member + step) % members},
            device_id_type=MESH,
        )

    def on_copy(step):
        return pltpu.make_async_remote_copy(
            src_ref=mine,
            dst_ref=all_sums.at[members],
            send_sem=sum_send.at[members + step],
            recv_sem=sum_recv.at[0],
            device_id=(next_group, step),
            device_id_type=MESH,
        )

    for step in range(1, members):
        sum_copy(step).start()

    @pl.when(sends_last)
    def _():
        for step in range(members):
            on_copy(step).start()

    all_sums[member] = mine[...]
    for step in range(1, members):
        sum_copy(step).wait_send()
        sum_copy(step).wait_recv()

    @pl.when(sends_last)
    def _():
        for step in range(members):
            on_copy(step).wait_send()

    @pl.when(gets_last)
    def _():
        on_copy(0).wait_recv()

    correction = jnp.zeros((8 * NB, LANES), jnp.float32)
    lane_row = lax.broadcasted_iota(jnp.int32, (1, LANES), 1)
    for pair in range(members // 2):
        if pair == 0:
            before = jnp.where(gets_last, all_sums[members, 0:1, :], 0.0)
        else:
            before = all_sums[2 * pair - 1, 0:1, :]
        even_cells = all_sums[2 * pair, 0:1, :] + before
        vector = jnp.where(lane_row < 64, even_cells, all_sums[2 * pair + 1, 0:1, :])
        correction = correction + inverse[0, :, LANES * pair : LANES * (pair + 1)] * vector
    rows_e[...] = jnp.broadcast_to(jnp.sum(correction, axis=1, keepdims=True), (8 * NB, LANES))

    @pl.when(p_split)
    def _():
        for p in range(NB):
            final_copy(p).wait_recv()

    def finish(p, carry):
        for cell in range(4):
            first = pl.multiple_of(8 * p, 8) + 2 * cell
            lift = jnp.where(depth < EDGE // 2, rows_e[pl.ds(first, 1), :], rows_e[pl.ds(first + 1, 1), :])
            for part in (2 * (cell // 2), 2 * (cell // 2) + 1):
                for tile in range(4 * (cell % 2), 4 * (cell % 2) + 4):
                    arrived = jnp.where(p_split, final_recv[p, flat(tile, part), :], 0.0)
                    value = u0[p, spot(tile, part), :] + arrived + lift
                    out_ref[p, 8 * part : 8 * part + 8, LANES * tile : LANES * (tile + 1)] = value
        return carry

    lax.fori_loop(0, NB, finish, 0)

    @pl.when(even)
    def _():
        for i in range(3):
            moves[i].wait_send()

    @pl.when(q_stays)
    def _():
        for p in range(NB):
            final_copy(p).wait_send()


def local(old_ids, field_old, source_old, kappa_old, refine, neighbors, coarse_inverse):
    members = lax.axis_size("member")
    devices = lax.axis_size(AXES)
    flat_shape = (NB, TILES * EDGE, LANES)
    both_shape = (2 * NB, TILES * EDGE, LANES)
    padded = (2 * NB, 10 * PITCH, LANES)
    shapes = [field_old.shape] * 3 + [padded] * 3 + [both_shape]
    shapes += [(2 * NB, 6, TILES * EDGE, LANES), both_shape, (3,) + flat_shape, (3,) + flat_shape]
    shapes += [flat_shape, flat_shape]
    shapes += [(2, 6, EDGE * n, LANES) for n in FIELDS]
    shapes += [(2, 2, 3, EDGE * n, LANES) for n in FIELDS]
    shapes += [(2, 2, 6, EDGE * n, LANES) for n in FIELDS]
    shapes += [(2, 3, EDGE * n, LANES) for n in FIELDS]
    shapes += [(2, 12, EDGE * n, LANES) for n in FIELDS]
    shapes += [(2 * NB, 8, LANES), (8 * NB, 8, LANES), (8, LANES), (members + 1, 8, LANES)]
    shapes += [(8 * NB, LANES)]
    dma = pltpu.SemaphoreType.DMA
    scratch = [pltpu.VMEM(s, jnp.float32) for s in shapes]
    scratch += [dma((3,)), dma((3,)), dma((3,)), dma((3, 2, 6, 2)), dma((3, 2, 2, 6))]
    scratch += [dma((3, 2)), dma((3, 2)), dma, dma, dma((NB,)), dma((NB,))]
    scratch += [dma((2 * members,)), dma((members,))]
    return pl.pallas_call(
        functools.partial(main_kernel, members, devices),
        out_shape=jax.ShapeDtypeStruct((NB, EDGE, FACE), jnp.float32),
        in_specs=[SM, SM, SM, VM, ANY, ANY, ANY],
        out_specs=VM,
        scratch_shapes=scratch,
        compiler_params=pltpu.CompilerParams(
            collective_id=1, has_side_effects=True, vmem_limit_bytes=VMEM_LIMIT
        ),
    )(old_ids, neighbors, refine, coarse_inverse, field_old, source_old, kappa_old)


def solution(mesh):
    in_specs = (
        P(AXES),
        P(AXES, None, None),
        P(AXES, None, None),
        P(AXES, None, None),
        P(AXES),
        P(AXES, None),
        P("group", "member", None),
    )
    return jax.shard_map(
        local, mesh=mesh, in_specs=in_specs, out_specs=P(AXES, None, None), check_vma=False
    )
```

```python
import functools

import jax
import jax.numpy as jnp
from jax import lax
from jax.experimental import pallas as pl
from jax.experimental.pallas import tpu as pltpu
from jax.sharding import PartitionSpec as P

OMEGA = 0.8
AXES = ("group", "member")
NB, EDGE, FACE, LANES = 8, 32, 1024, 128
TILES, PARTS, PITCH = 8, 4, 48
HIGHEST = lax.Precision.HIGHEST
VMEM_LIMIT = 60 * 2**20
VM = pl.BlockSpec(memory_space=pltpu.VMEM)
ANY = pl.BlockSpec(memory_space=pl.ANY)
SM = pl.BlockSpec(memory_space=pltpu.SMEM)
MESH = pl.DeviceIdType.MESH
FIELDS = (2, 1)
EARLY, MIDDLE = 3, 5
OWN, ALONG_X, ALONG_Y, ALONG_Z, SOURCE = range(5)


def roll(value, steps):
    return pltpu.roll(value, steps % LANES, 1)


def spot(tile, part):
    return slice(PITCH * (tile + 1) + 8 + 8 * part, PITCH * (tile + 1) + 16 + 8 * part)


def flat(tile, part):
    return slice(EDGE * tile + 8 * part, EDGE * tile + 8 * part + 8)


def blocks_of(axis, side):
    return [b for b in range(NB) if (b >> axis) % 2 == side]


def octet_neighbors(octet, devices):
    nbits = devices.bit_length() - 1
    bits = [octet // 2**i % 2 for i in range(nbits)]
    result = []
    for axis in range(3):
        own = [i for i in range(nbits) if i % 3 == axis]
        extent = 2 ** len(own)
        coord = sum(bits[i] * 2**n for n, i in enumerate(own))
        base = octet - sum(bits[i] * 2**i for i in own)
        pair = []
        for step in (-1, 1):
            moved = coord + step
            inside = jnp.logical_and(moved >= 0, moved < extent)
            clipped = jnp.clip(moved, 0, extent - 1)
            index = base + sum(clipped // 2**n % 2 * 2**i for n, i in enumerate(own))
            pair.append((inside, index))
        result.append(pair)
    return result


def main_kernel(members, devices, old_ids, nbrs, refine, inverse, u_old, f_old, k_old, out_ref, *scratch):
    olds = scratch[0:3]
    u0, u1, k_ref, f_ref, omega, weight_sum, staged, moved, final_send, final_recv = scratch[3:13]
    send_out, own_in, recv_out, recv_in, ghosts = [scratch[13 + 2 * i : 15 + 2 * i] for i in range(5)]
    flags, acc, mine, all_sums, rows_e, edge_sums, got_sums, split_sums = scratch[23:31]
    in_sem, move_send, move_recv, out_send, out_recv, inner_send, inner_recv = scratch[31:38]
    flag_send, flag_recv, last_send, last_recv, sum_send, sum_recv = scratch[38:44]

    group, member = lax.axis_index("group"), lax.axis_index("member")
    here = group * members + member
    odd = here % 2 == 1
    even = here % 2 == 0
    has_q = here < devices - 1
    q_stays = jnp.logical_and(odd, has_q)
    p_split = jnp.logical_and(even, here > 0)
    around = [octet_neighbors(here, devices), octet_neighbors(here + 1, devices)]
    lane = lax.broadcasted_iota(jnp.int32, (8, LANES), 1)
    depth = lane % EDGE

    def where_is(index):
        return (index // members, index % members)

    loads = [
        pltpu.make_async_copy(ref, olds[i], in_sem.at[i]) for i, ref in enumerate((u_old, k_old, f_old))
    ]
    for load in loads:
        load.start()

    def both(*preds):
        result = preds[0]
        for pred in preds[1:]:
            result = jnp.logical_and(result, pred)
        return result

    outgoing, incoming = {}, {}
    for s in (0, 1):
        for axis in range(3):
            for side in (0, 1):
                inside, index = around[s][axis][side]
                exists = inside if s == 0 else both(inside, has_q)
                stays = inside if s == 0 else both(inside, q_stays)
                holder = both(index % 2 == 0, index > 0)
                for t in (0, 1):
                    target = index if t == 0 else jnp.maximum(index - 1, 0)
                    first = exists if t == 0 else both(exists, holder)
                    if s == 1 and t == 0 and axis == 0 and side == 0:
                        first = both(first, odd)
                    later = stays if t == 0 else both(stays, holder)
                    outgoing[s, axis, side, t] = (target, (first, later, later))
                receives = inside if s == 0 else both(inside, q_stays)
                for src in (0, 1):
                    source = index if src == 0 else jnp.maximum(index - 1, 0)
                    first = receives if src == 0 else both(receives, index > 0)
                    if s == 0 and src == 1 and axis == 0 and side == 1:
                        first = both(first, odd)
                    later = receives if src == 0 else both(receives, holder)
                    incoming[s, src, axis, side] = (source, (first, later, later))

    for b in range(NB):
        flags[NB + b] = jnp.ones((8, LANES), jnp.float32)
    barrier = pltpu.get_barrier_semaphore()
    expected = jnp.int32(members - 1)
    for step in range(1, members):
        pl.semaphore_signal(
            barrier, inc=1, device_id={"member": (member + step) % members}, device_id_type=MESH
        )
    for target, preds in outgoing.values():
        expected = expected + both(preds[0], target // members != group).astype(jnp.int32)
    for source, preds in incoming.values():

        @pl.when(both(preds[0], source // members != group))
        def _():
            pl.semaphore_signal(barrier, inc=1, device_id=where_is(source), device_id_type=MESH)

    last = member == members - 1
    sends_last = both(last, has_q)
    gets_last = group > 0
    next_group = jnp.minimum(group + 1, devices // members - 1)
    prev_last = jnp.maximum(group * members - 1, 0)
    expected = expected + jnp.where(sends_last, members, 0)

    @pl.when(gets_last)
    def _():
        pl.semaphore_signal(barrier, inc=1, device_id=where_is(prev_last), device_id_type=MESH)

    first_in_group = both(member == 0, gets_last)
    expected = expected + first_in_group.astype(jnp.int32)

    @pl.when(sends_last)
    def _():
        pl.semaphore_signal(barrier, inc=1, device_id=(next_group, 0), device_id_type=MESH)

    kept, onward = jnp.int32(0), jnp.int32(0)
    for slot in range(2 * NB):
        index = old_ids[slot]
        kept = kept + both(index >= here * NB, index < here * NB + NB).astype(jnp.int32)
        onward = onward + (index >= here * NB + NB).astype(jnp.int32)
    kept = jnp.minimum(kept, NB)
    lacking = NB - kept

    for b in range(NB):
        for face in range(6):
            has = jnp.where(nbrs[b, face] >= 0, 1.0, 0.0).astype(jnp.float32)
            flags[b, face : face + 1, :] = jnp.full((1, LANES), has, jnp.float32)
        half_scale = 0.5 + 0.5 * refine[b].astype(jnp.float32)
        flags[b, 6:7, :] = jnp.full((1, LANES), half_scale, jnp.float32)
        flags[b, 7:8, :] = 1.0 / jnp.full((1, LANES), half_scale, jnp.float32)

    def settle(i, store):
        loads[i].wait()

        def own(p, carry):
            slot = jnp.maximum(p - lacking, 0)
            for tile in range(TILES):
                for part in range(PARTS):
                    value = olds[i][slot, 8 * part : 8 * part + 8, LANES * tile : LANES * (tile + 1)]
                    store(p, tile, part, jnp.where(p >= lacking, value, 0.0))
            return carry

        def following(p, carry):
            for tile in range(TILES):
                for part in range(PARTS):
                    value = olds[i][kept + p, 8 * part : 8 * part + 8, LANES * tile : LANES * (tile + 1)]
                    value = jnp.where(p < onward, value, 0.0)
                    store(NB + p, tile, part, value)
                    staged[i, p, flat(tile, part), :] = value
            return carry

        lax.fori_loop(0, NB, own, 0)
        lax.fori_loop(0, NB, following, 0)

    def pack(phase, s, field, volume, outer=True, inner=True):
        rows = EDGE * field

        def put(axis, side, bit, start, value):
            here_rows = pl.ds(rows + start, 8)
            if side == bit:
                send_out[phase][s, 2 * axis + side, here_rows, :] = value
            else:
                own_in[phase][s, bit, 3 * 0 + axis, here_rows, :] = value

        def wanted(side, bit):
            return outer if side == bit else inner

        for bit in (0, 1):
            for side in (0, 1):
                if not wanted(side, bit):
                    continue
                for j, b in enumerate(blocks_of(0, bit)):
                    line = volume[NB * s + b, pl.ds(PITCH + 8 + 31 * side, 8, stride=PITCH), :]
                    put(0, side, bit, 8 * j, line)
                for part in range(PARTS):
                    packed = jnp.zeros((8, LANES), jnp.float32)
                    for j, b in enumerate(blocks_of(1, bit)):
                        piece = volume[NB * s + b, spot(7 * side, part), :]
                        packed = jnp.where(lane // EDGE == j, roll(piece, EDGE * (j - 3 * side)), packed)
                    put(1, side, bit, 8 * part, packed)
            for quad in range(4):
                packed = [jnp.zeros((8, LANES), jnp.float32) for _ in (0, 1)]
                for half in (0, 1):
                    for j, b in enumerate(blocks_of(2, bit)):
                        for part in range(PARTS):
                            slot = 16 * half + 4 * j + part
                            piece = roll(volume[NB * s + b, spot(quad + 4 * half, part), :], slot)
                            for side in (0, 1):
                                if wanted(side, bit):
                                    packed[side] = jnp.where(
                                        depth == (slot + 31 * side) % EDGE, piece, packed[side]
                                    )
                for side in (0, 1):
                    if wanted(side, bit):
                        put(2, side, bit, 8 * quad, packed[side])

    def out_copy(phase, s, axis, side, t, target):
        face = 2 * axis + 1 - side
        if phase == 2:
            source, place = edge_sums.at[s], got_sums.at[t, s, face]
        else:
            source, place = send_out[phase].at[s, 2 * axis + side], recv_out[phase].at[t, s, face]
        return pltpu.make_async_remote_copy(
            src_ref=source,
            dst_ref=place,
            send_sem=out_send.at[phase, s, 2 * axis + side, t],
            recv_sem=out_recv.at[phase, t, s, face],
            device_id=where_is(target),
            device_id_type=MESH,
        )

    follower = jnp.minimum(here + 1, devices - 1)
    leader = jnp.maximum(here - 1, 0)

    def inner_copy(phase, s):
        if phase == 2:
            source, place = edge_sums.at[s], split_sums.at[1 - s]
        else:
            source, place = own_in[phase].at[s, 1 - s], recv_in[phase].at[1 - s]
        return pltpu.make_async_remote_copy(
            src_ref=source,
            dst_ref=place,
            send_sem=inner_send.at[phase, s],
            recv_sem=inner_recv.at[phase, 1 - s],
            device_id=where_is(follower if s else leader),
            device_id_type=MESH,
        )

    flag_copy = pltpu.make_async_remote_copy(
        src_ref=flags.at[pl.ds(0, NB)],
        dst_ref=flags.at[pl.ds(NB, NB)],
        send_sem=flag_send,
        recv_sem=flag_recv,
        device_id=where_is(leader),
        device_id_type=MESH,
    )
    moves = [
        pltpu.make_async_remote_copy(
            src_ref=staged.at[i],
            dst_ref=moved.at[i],
            send_sem=move_send.at[i],
            recv_sem=move_recv.at[i],
            device_id=where_is(follower),
            device_id_type=MESH,
        )
        for i in range(3)
    ]

    def start_exchange(phase, which):
        for (s, axis, side, t), (target, preds) in outgoing.items():
            if s == which:

                @pl.when(preds[phase])
                def _():
                    out_copy(phase, s, axis, side, t, target).start()

        @pl.when((p_split, q_stays)[which])
        def _():
            inner_copy(phase, which).start()

    def finish_exchange(phase):
        for (s, axis, side, t), (target, preds) in outgoing.items():

            @pl.when(preds[phase])
            def _():
                out_copy(phase, s, axis, side, t, target).wait_send()

        for (t, src, axis, side), (source, preds) in incoming.items():

            @pl.when(preds[phase])
            def _():
                out_copy(phase, src, axis, 1 - side, t, source).wait_recv()

        @pl.when(q_stays)
        def _():
            inner_copy(phase, 1).wait_send()
            inner_copy(phase, 0).wait_recv()

        @pl.when(p_split)
        def _():
            inner_copy(phase, 0).wait_send()
            inner_copy(phase, 1).wait_recv()

    def gather_ghosts(phase, t):
        split = (p_split, q_stays)[t]
        for axis in range(3):
            for side in (0, 1):
                face = 2 * axis + side
                total = 0.0
                for src in (0, 1):
                    pred = incoming[t, src, axis, side][1][phase]
                    if phase == 0 and (t, src, axis, side) == (0, 1, 0, 1):
                        own = jnp.where(even, send_out[0][1, 0], 0.0)
                        total = total + jnp.where(pred, recv_out[0][t, src, face], own)
                    else:
                        total = total + jnp.where(pred, recv_out[phase][t, src, face], 0.0)
                ghosts[phase][t, face] = total
                total = own_in[phase][t, side, axis]
                if side == t:
                    total = total + jnp.where(split, recv_in[phase][t, axis], 0.0)
                ghosts[phase][t, 6 + face] = total

    def fill(phase, q, field, volume, mirror):
        s, p = q // NB, q % NB
        rows = EDGE * field
        js = (p // 2, p % 2 + p // 4 * 2, p % 4)
        for side in (0, 1):
            kind = [jnp.where((p // 2**axis) % 2 == side, 0, 6) for axis in range(2)]
            ghost = ghosts[phase][s, kind[0] + side, pl.ds(pl.multiple_of(rows + 8 * js[0], 8), 8), :]
            has = flags[q, side : side + 1, :] > 0.5
            if mirror:
                spare = volume[q, pl.ds(PITCH + 8 + 31 * side, 8, stride=PITCH), :]
            else:
                spare = jnp.zeros_like(ghost)
            volume[q, pl.ds(PITCH + 7 + 33 * side, 8, stride=PITCH), :] = jnp.where(has, ghost, spare)
            has = flags[q, 2 + side : 3 + side, :] > 0.5
            for part in range(PARTS):
                ghost = ghosts[phase][s, kind[1] + 2 + side, rows + 8 * part : rows + 8 * part + 8, :]
                steps = EDGE * (3 - js[1]) if side == 0 else EDGE * ((4 - js[1]) % 4)
                ghost = pltpu.roll(ghost, steps, 1)
                if mirror:
                    spare = roll(volume[q, spot(7 * side, part), :], 96 - 64 * side)
                else:
                    spare = jnp.zeros_like(ghost)
                volume[q, spot(9 * side - 1, part), :] = jnp.where(has, ghost, spare)

    def stencil(phase, q, field, volume, mirror, part):
        s, p = q // NB, q % NB
        j = p % 4
        rows = EDGE * field
        bit = p // 4 % 2
        low_face = jnp.where(bit == 0, 0, 6) + 4
        high_face = jnp.where(bit == 1, 0, 6) + 5
        near = depth < EDGE // 2
        has = jnp.where(near, flags[q, 4:5, :], flags[q, 5:6, :]) > 0.5
        tiles = [volume[q, spot(t, part), :] for t in range(-1, TILES + 1)]
        down = [roll(t, EDGE) for t in tiles[:-1]]
        up = [None] + [roll(t, -EDGE) for t in tiles[1:]]
        for tile in range(TILES):
            value = tiles[tile + 1]
            top = PITCH * (tile + 1) + 8 + 8 * part
            x_minus = volume[q, top - 1 : top + 7, :]
            x_plus = volume[q, top + 1 : top + 9, :]
            y_minus = jnp.where(lane >= EDGE, down[tile + 1], down[tile])
            y_plus = jnp.where(lane < 3 * EDGE, up[tile + 1], up[tile + 2])
            base = 16 * (tile // 4) + part
            sheet = slice(rows + 8 * (tile % 4), rows + 8 * (tile % 4) + 8)
            low = pltpu.roll(ghosts[phase][s, low_face, sheet, :], 97 - base - 4 * j, 1)
            high = pltpu.roll(ghosts[phase][s, high_face, sheet, :], 31 - base - 4 * j, 1)
            edge = jnp.where(has, jnp.where(near, low, high), value if mirror else 0.0)
            z_minus = jnp.where(depth == 0, edge, roll(value, 1))
            z_plus = jnp.where(depth == EDGE - 1, edge, roll(value, -1))
            yield tile, value, (x_minus, x_plus, y_minus, y_plus, z_minus, z_plus)

    def valid(q):
        low = jnp.where(even, lacking, 0)
        return both(q >= low, q < NB + onward)

    def keep(kind, q, cell, value):
        acc[pl.ds(pl.multiple_of(8 * (8 * NB * kind + 4 * q + cell), 8), 8), :] = value

    def first_sweep(q, carry):
        fill(0, q, 0, u0, False)
        fill(0, q, 1, k_ref, True)
        holds = valid(q)
        totals = [jnp.zeros((8, LANES), jnp.float32) for _ in range(4)]
        for part in range(PARTS):
            pairs = zip(stencil(0, q, 0, u0, False, part), stencil(0, q, 1, k_ref, True, part))
            for (tile, u, u_beside), (_, k, k_beside) in pairs:
                weights = [k + beside for beside in k_beside]
                total = sum(weights[1:], weights[0])
                scale = jnp.where(holds, OMEGA / total, 0.0)
                place = flat(tile, part)
                weight_sum[q, place, :] = total * (1.0 / OMEGA)
                right = f_ref[q, place, :]
                cell = part // 2 * 2 + tile // 4
                totals[cell] = totals[cell] + right
                gain = right * scale * flags[q, 7:8, :]
                f_ref[q, place, :] = gain
                new = (1.0 - OMEGA) * u + gain
                for face in range(6):
                    weight = weights[face] * scale
                    omega[q, face, place, :] = weight
                    new = new + weight * u_beside[face]
                u1[q, spot(tile, part), :] = new
        for cell in range(4):
            keep(SOURCE, q, cell, totals[cell])
        return carry

    sublane = lax.broadcasted_iota(jnp.int32, (8, LANES), 0)

    def second_sweep(q, send):
        fill(1, q, 0, u1, False)
        zero = jnp.zeros((8, LANES), jnp.float32)
        along_z = [zero] * 4
        along_y = {(layer, half): zero for layer in (0, 15, 16, 31) for half in (0, 1)}
        for part in range(PARTS):
            for tile, u, beside in stencil(1, q, 0, u1, False, part):
                place = flat(tile, part)
                new = (1.0 - OMEGA) * u + f_ref[q, place, :]
                weights = [omega[q, face, place, :] for face in range(6)]
                for face in range(6):
                    new = new + weights[face] * beside[face]
                u0[q, spot(tile, part), :] = new
                if send:
                    final_send[q - NB, place, :] = new
                scaled = new * weight_sum[q, place, :]
                half, cell = part // 2, part // 2 * 2 + tile // 4
                outward = jnp.where(depth % (EDGE // 2) == EDGE // 2 - 1, weights[5], weights[4])
                along_z[cell] = along_z[cell] + outward * scaled
                if tile in (0, 4):
                    layer = 4 * tile
                    along_y[layer, half] = along_y[layer, half] + weights[2] * scaled
                if tile in (3, 7):
                    layer = 4 * tile + 3
                    along_y[layer, half] = along_y[layer, half] + weights[3] * scaled
        for layer, half in along_y:
            inside = lane < EDGE if layer in (0, 16) else lane >= 3 * EDGE
            along_y[layer, half] = jnp.where(inside, along_y[layer, half], 0.0)
        along_x = {}
        for layer, face in ((0, 0), (15, 1), (16, 0), (31, 1)):
            rows = pl.ds(layer, 8, stride=EDGE)
            value = u0[q, pl.ds(PITCH + 8 + layer, 8, stride=PITCH), :]
            along_x[layer] = omega[q, face, rows, :] * weight_sum[q, rows, :] * value
        middle = along_x[15] - along_x[16]
        own_x = (along_x[0] + middle, along_x[31] - middle)
        for a in (0, 1):
            middle = along_y[15, a] - along_y[16, a]
            own_y = (along_y[0, a] + middle, along_y[31, a] - middle)
            for b in (0, 1):
                upper = sublane // 4 == b
                keep(OWN, q, 2 * a + b, jnp.where(upper, own_x[a], 0.0) + own_y[b])
                keep(ALONG_X, q, 2 * a + b, jnp.where(upper, along_x[31 * a], 0.0))
                keep(ALONG_Y, q, 2 * a + b, along_y[31 * a, b])
                keep(ALONG_Z, q, 2 * a + b, along_z[2 * a + b])

    cell_lane = lax.broadcasted_iota(jnp.int32, (1, LANES), 1)
    block_of = cell_lane // 8 % NB
    corner = (cell_lane // 4 % 2, cell_lane // 2 % 2, cell_lane % 2)
    wide = (LANES, LANES)
    from_depth = lax.broadcasted_iota(jnp.int32, wide, 0) % EDGE
    to_corner = lax.broadcasted_iota(jnp.int32, wide, 1) % 2
    by_half = (from_depth // (EDGE // 2) == to_corner).astype(jnp.float32)

    def one_at(level):
        return (from_depth == level).astype(jnp.float32)

    def take(value, choose):
        return jnp.dot(value, choose, precision=HIGHEST, preferred_element_type=jnp.float32)

    def sums_of(kind):
        groups = []
        for group in range(8):
            start = 8 * (8 * NB * kind + 8 * group)
            groups.append(sum(acc[pl.ds(start + i, 8, stride=8), :] for i in range(8)))
        return jnp.concatenate(groups, axis=0)

    def pick(value, s, block, place):
        rows = lax.broadcasted_iota(jnp.int32, (4 * NB, LANES), 0)
        part = value[4 * NB * s : 4 * NB * (s + 1), :]
        return jnp.sum(jnp.where(rows == 4 * block + place, part, 0.0), axis=0, keepdims=True)

    def other(axis):
        bit = block_of // 2**axis % 2
        return block_of + 2**axis * (1 - 2 * bit)


    def pack_all(field, volume):
        def body(s, carry):
            pack(0, s, field, volume)
            return carry

        lax.fori_loop(0, 2, body, 0)

    def gather_all(phase):
        gather_ghosts(phase, 0)

        @pl.when(odd)
        def _():
            gather_ghosts(phase, 1)

    def to_volume(volume):
        def store(q, tile, part, value):
            volume[q, spot(tile, part), :] = value

        return store

    def to_source(q, tile, part, value):
        f_ref[q, flat(tile, part), :] = value

    settle(0, to_volume(u0))
    pack_all(0, u0)
    settle(1, to_volume(k_ref))
    pack_all(1, k_ref)
    pl.semaphore_wait(barrier, expected)
    start_exchange(0, 1)
    start_exchange(0, 0)

    @pl.when(p_split)
    def _():
        flag_copy.start()

    @pl.when(even)
    def _():
        moves[0].start()
        moves[1].start()

    settle(2, to_source)

    @pl.when(even)
    def _():
        moves[2].start()

    @pl.when(odd)
    def _():
        for i in range(3):
            moves[i].wait_recv()

        def merge(p, carry):
            for tile in range(TILES):
                for part in range(PARTS):
                    for i, volume in enumerate((u0, k_ref)):
                        volume[p, spot(tile, part), :] += moved[i, p, flat(tile, part), :]
                    f_ref[p, flat(tile, part), :] += moved[2, p, flat(tile, part), :]
            return carry

        lax.fori_loop(0, NB, merge, 0)
        pack(0, 0, 0, u0, outer=False)
        pack(0, 0, 1, k_ref, outer=False)

    finish_exchange(0)

    @pl.when(p_split)
    def _():
        flag_copy.wait_send()

    @pl.when(q_stays)
    def _():
        flag_copy.wait_recv()

    gather_all(0)

    @pl.when(odd)
    def _():
        lax.fori_loop(NB, 2 * NB, first_sweep, 0)
        pack(1, 1, 0, u1)
        start_exchange(1, 1)

    lax.fori_loop(0, NB, first_sweep, 0)
    pack(1, 0, 0, u1)
    start_exchange(1, 0)

    cells = take(sums_of(SOURCE), by_half)
    source_sums = [pick(cells, s, block_of, cell_lane // 2 % 4) for s in (0, 1)]
    finish_exchange(1)
    gather_all(1)

    def final_copy(p):
        return pltpu.make_async_remote_copy(
            src_ref=final_send.at[p],
            dst_ref=final_recv.at[p],
            send_sem=last_send.at[p],
            recv_sem=last_recv.at[p],
            device_id=where_is(follower),
            device_id_type=MESH,
        )

    @pl.when(odd)
    def _():
        def body(q, carry):
            second_sweep(q, True)

            @pl.when(both(has_q, q < NB + EARLY))
            def _():
                final_copy(q - NB).start()

            return carry

        lax.fori_loop(NB, 2 * NB, body, 0)

    def body(q, carry):
        second_sweep(q, False)
        return carry

    lax.fori_loop(0, NB, body, 0)

    middle = take(jnp.concatenate([sums_of(kind) for kind in (OWN, ALONG_X, ALONG_Y)], axis=0), by_half)
    crossing = one_at(15) - one_at(16)
    low_cells, high_cells = one_at(0) + crossing, one_at(EDGE - 1) - crossing
    z_sums = sums_of(ALONG_Z)
    own_z = take(z_sums, jnp.where(to_corner == 0, low_cells, high_cells))
    face_z = take(z_sums, jnp.where(to_corner == 0, one_at(EDGE - 1), one_at(0)))
    size = 8 * NB
    own_sums = []
    for s in (0, 1):
        own_sums.append(pick(middle[:size] + own_z, s, block_of, cell_lane // 2 % 4))
        face_x = pick(middle[size : 2 * size], s, other(0), 2 * (1 - corner[0]) + corner[1])
        face_y = pick(middle[2 * size :], s, other(1), 2 * (1 - corner[1]) + corner[0])
        near_z = pick(face_z, s, other(2), cell_lane // 2 % 4)
        edge_sums[s] = jnp.where(sublane == 0, face_x, jnp.where(sublane == 1, face_y, near_z))
    start_exchange(2, 0)

    @pl.when(odd)
    def _():
        start_exchange(2, 1)

    @pl.when(q_stays)
    def _():
        for p in range(EARLY, MIDDLE):
            final_copy(p).start()

    finish_exchange(2)
    totals = []
    for t in (0, 1):
        combined = jnp.zeros((8, LANES), jnp.float32)
        for p in range(NB):
            combined = jnp.where(lane // 8 % NB == p, flags[NB * t + p], combined)
        beyond = jnp.zeros((1, LANES), jnp.float32)
        for axis in range(3):
            row = slice(axis, axis + 1)
            outer, linked = [], []
            for side in (0, 1):
                face = 2 * axis + side
                total = 0.0
                for src in (0, 1):
                    pred = incoming[t, src, axis, side][1][2]
                    total = total + jnp.where(pred, got_sums[t, src, face, row, :], 0.0)
                outer.append(total)
                linked.append(combined[face : face + 1, :])
            split = jnp.where((p_split, q_stays)[t], split_sums[t, row, :], 0.0)
            inner = edge_sums[t, row, :] + split
            outer = jnp.where(corner[axis] == 0, outer[0], outer[1])
            linked = jnp.where(corner[axis] == 0, linked[0], linked[1])
            beside = jnp.where(block_of // 2**axis % 2 == corner[axis], outer, inner)
            beyond = beyond + jnp.where(linked > 0.5, beside, 0.0)
        held = block_of < onward if t else block_of >= jnp.where(even, lacking, 0)
        change = combined[6:7, :] * (beyond - own_sums[t])
        totals.append(jnp.where(held, source_sums[t] + change, 0.0))
    low_half = jnp.where(odd, totals[1], totals[0])
    total = jnp.where(cell_lane < 64, low_half, jnp.where(odd, totals[0], 0.0))
    mine[...] = jnp.broadcast_to(total * (EDGE // 2) ** (-1.5), (8, LANES))

    def sum_copy(step):
        return pltpu.make_async_remote_copy(
            src_ref=mine,
            dst_ref=all_sums.at[member],
            send_sem=sum_send.at[step],
            recv_sem=sum_recv.at[step],
            device_id={"member": (member + step) % members},
            device_id_type=MESH,
        )

    def on_copy(step):
        return pltpu.make_async_remote_copy(
            src_ref=mine,
            dst_ref=all_sums.at[members],
            send_sem=sum_send.at[members + step],
            recv_sem=sum_recv.at[0],
            device_id=(next_group, step),
            device_id_type=MESH,
        )

    for step in range(1, members):
        sum_copy(step).start()

    @pl.when(sends_last)
    def _():
        for step in range(members):
            on_copy(step).start()

    @pl.when(q_stays)
    def _():
        for p in range(MIDDLE, NB):
            final_copy(p).start()

    all_sums[member] = mine[...]
    for step in range(1, members):
        sum_copy(step).wait_send()
        sum_copy(step).wait_recv()

    @pl.when(sends_last)
    def _():
        for step in range(members):
            on_copy(step).wait_send()

    @pl.when(gets_last)
    def _():
        on_copy(0).wait_recv()

    correction = jnp.zeros((8 * NB, LANES), jnp.float32)
    for pair in range(members // 2):
        if pair == 0:
            before = jnp.where(gets_last, all_sums[members, 0:1, :], 0.0)
        else:
            before = all_sums[2 * pair - 1, 0:1, :]
        even_cells = all_sums[2 * pair, 0:1, :] + before
        vector = jnp.where(cell_lane < 64, even_cells, all_sums[2 * pair + 1, 0:1, :])
        correction = correction + inverse[0, :, LANES * pair : LANES * (pair + 1)] * vector
    rows_e[...] = jnp.broadcast_to(jnp.sum(correction, axis=1, keepdims=True), (8 * NB, LANES))

    @pl.when(p_split)
    def _():
        for p in range(NB):
            final_copy(p).wait_recv()

    def finish(p, carry):
        for cell in range(4):
            first = pl.multiple_of(8 * p, 8) + 2 * cell
            lift = jnp.where(depth < EDGE // 2, rows_e[pl.ds(first, 1), :], rows_e[pl.ds(first + 1, 1), :])
            for part in (2 * (cell // 2), 2 * (cell // 2) + 1):
                for tile in range(4 * (cell % 2), 4 * (cell % 2) + 4):
                    arrived = jnp.where(p_split, final_recv[p, flat(tile, part), :], 0.0)
                    value = u0[p, spot(tile, part), :] + arrived + lift
                    out_ref[p, 8 * part : 8 * part + 8, LANES * tile : LANES * (tile + 1)] = value
        return carry

    lax.fori_loop(0, NB, finish, 0)

    @pl.when(even)
    def _():
        for i in range(3):
            moves[i].wait_send()

    @pl.when(q_stays)
    def _():
        for p in range(NB):
            final_copy(p).wait_send()


def local(old_ids, field_old, source_old, kappa_old, refine, neighbors, coarse_inverse):
    members = lax.axis_size("member")
    devices = lax.axis_size(AXES)
    flat_shape = (NB, TILES * EDGE, LANES)
    both_shape = (2 * NB, TILES * EDGE, LANES)
    padded = (2 * NB, 10 * PITCH, LANES)
    shapes = [field_old.shape] * 3 + [padded] * 3 + [both_shape]
    shapes += [(2 * NB, 6, TILES * EDGE, LANES), both_shape, (3,) + flat_shape, (3,) + flat_shape]
    shapes += [flat_shape, flat_shape]
    shapes += [(2, 6, EDGE * n, LANES) for n in FIELDS]
    shapes += [(2, 2, 3, EDGE * n, LANES) for n in FIELDS]
    shapes += [(2, 2, 6, EDGE * n, LANES) for n in FIELDS]
    shapes += [(2, 3, EDGE * n, LANES) for n in FIELDS]
    shapes += [(2, 12, EDGE * n, LANES) for n in FIELDS]
    shapes += [(2 * NB, 8, LANES), (5 * 64 * NB, LANES), (8, LANES), (members + 1, 8, LANES)]
    shapes += [(8 * NB, LANES), (2, 8, LANES), (2, 2, 6, 8, LANES), (2, 8, LANES)]
    dma = pltpu.SemaphoreType.DMA
    scratch = [pltpu.VMEM(s, jnp.float32) for s in shapes]
    scratch += [dma((3,)), dma((3,)), dma((3,)), dma((3, 2, 6, 2)), dma((3, 2, 2, 6))]
    scratch += [dma((3, 2)), dma((3, 2)), dma, dma, dma((NB,)), dma((NB,))]
    scratch += [dma((2 * members,)), dma((members,))]
    return pl.pallas_call(
        functools.partial(main_kernel, members, devices),
        out_shape=jax.ShapeDtypeStruct((NB, EDGE, FACE), jnp.float32),
        in_specs=[SM, SM, SM, VM, ANY, ANY, ANY],
        out_specs=VM,
        scratch_shapes=scratch,
        compiler_params=pltpu.CompilerParams(
            collective_id=1, has_side_effects=True, vmem_limit_bytes=VMEM_LIMIT
        ),
    )(old_ids, neighbors, refine, coarse_inverse, field_old, source_old, kappa_old)


def solution(mesh):
    in_specs = (
        P(AXES),
        P(AXES, None, None),
        P(AXES, None, None),
        P(AXES, None, None),
        P(AXES),
        P(AXES, None),
        P("group", "member", None),
    )
    return jax.shard_map(
        local, mesh=mesh, in_specs=in_specs, out_specs=P(AXES, None, None), check_vma=False
    )
```

```python
import functools

import jax
import jax.numpy as jnp
from jax import lax
from jax.experimental import pallas as pl
from jax.experimental.pallas import tpu as pltpu
from jax.sharding import PartitionSpec as P

OMEGA = 0.8
AXES = ("group", "member")
NB, EDGE, FACE, LANES = 8, 32, 1024, 128
TILES, PARTS, PITCH = 8, 4, 48
HIGHEST = lax.Precision.HIGHEST
VMEM_LIMIT = 60 * 2**20
VM = pl.BlockSpec(memory_space=pltpu.VMEM)
ANY = pl.BlockSpec(memory_space=pl.ANY)
SM = pl.BlockSpec(memory_space=pltpu.SMEM)
MESH = pl.DeviceIdType.MESH
FIELDS = (2, 1)
EARLY, MIDDLE = 4, 6
OWN, ALONG_X, ALONG_Y, ALONG_Z, SOURCE = range(5)


def roll(value, steps):
    return pltpu.roll(value, steps % LANES, 1)


def spot(tile, part):
    return slice(PITCH * (tile + 1) + 8 + 8 * part, PITCH * (tile + 1) + 16 + 8 * part)


def flat(tile, part):
    return slice(EDGE * tile + 8 * part, EDGE * tile + 8 * part + 8)


def blocks_of(axis, side):
    return [b for b in range(NB) if (b >> axis) % 2 == side]


def octet_neighbors(octet, devices):
    nbits = devices.bit_length() - 1
    bits = [octet // 2**i % 2 for i in range(nbits)]
    result = []
    for axis in range(3):
        own = [i for i in range(nbits) if i % 3 == axis]
        extent = 2 ** len(own)
        coord = sum(bits[i] * 2**n for n, i in enumerate(own))
        base = octet - sum(bits[i] * 2**i for i in own)
        pair = []
        for step in (-1, 1):
            moved = coord + step
            inside = jnp.logical_and(moved >= 0, moved < extent)
            clipped = jnp.clip(moved, 0, extent - 1)
            index = base + sum(clipped // 2**n % 2 * 2**i for n, i in enumerate(own))
            pair.append((inside, index))
        result.append(pair)
    return result


def main_kernel(members, devices, old_ids, nbrs, refine, inverse, u_old, f_old, k_old, out_ref, *scratch):
    olds = scratch[0:3]
    u0, u1, k_ref, f_ref, omega, weight_sum, staged, moved, final_send, final_recv = scratch[3:13]
    send_out, own_in, recv_out, recv_in, ghosts = [scratch[13 + 2 * i : 15 + 2 * i] for i in range(5)]
    flags, acc, mine, all_sums, rows_e, edge_sums, got_sums, split_sums = scratch[23:31]
    edges = scratch[31:33]
    in_sem, move_send, move_recv, out_send, out_recv, inner_send, inner_recv = scratch[33:40]
    flag_send, flag_recv, last_send, last_recv, sum_send, sum_recv = scratch[40:46]

    group, member = lax.axis_index("group"), lax.axis_index("member")
    here = group * members + member
    odd = here % 2 == 1
    even = here % 2 == 0
    has_q = here < devices - 1
    q_stays = jnp.logical_and(odd, has_q)
    p_split = jnp.logical_and(even, here > 0)
    around = [octet_neighbors(here, devices), octet_neighbors(here + 1, devices)]
    lane = lax.broadcasted_iota(jnp.int32, (8, LANES), 1)
    depth = lane % EDGE

    def where_is(index):
        return (index // members, index % members)

    loads = [
        pltpu.make_async_copy(ref, olds[i], in_sem.at[i]) for i, ref in enumerate((u_old, k_old, f_old))
    ]
    loads[0].start()

    def both(*preds):
        result = preds[0]
        for pred in preds[1:]:
            result = jnp.logical_and(result, pred)
        return result

    outgoing, incoming = {}, {}
    for s in (0, 1):
        for axis in range(3):
            for side in (0, 1):
                inside, index = around[s][axis][side]
                exists = inside if s == 0 else both(inside, has_q)
                stays = inside if s == 0 else both(inside, q_stays)
                holder = both(index % 2 == 0, index > 0)
                for t in (0, 1):
                    target = index if t == 0 else jnp.maximum(index - 1, 0)
                    first = exists if t == 0 else both(exists, holder)
                    if s == 1 and t == 0 and axis == 0 and side == 0:
                        first = both(first, odd)
                    later = stays if t == 0 else both(stays, holder)
                    outgoing[s, axis, side, t] = (target, (first, later, later))
                receives = inside if s == 0 else both(inside, q_stays)
                for src in (0, 1):
                    source = index if src == 0 else jnp.maximum(index - 1, 0)
                    first = receives if src == 0 else both(receives, index > 0)
                    if s == 0 and src == 1 and axis == 0 and side == 1:
                        first = both(first, odd)
                    later = receives if src == 0 else both(receives, holder)
                    incoming[s, src, axis, side] = (source, (first, later, later))

    for b in range(NB):
        flags[NB + b] = jnp.ones((8, LANES), jnp.float32)
    barrier = pltpu.get_barrier_semaphore()
    expected = jnp.int32(members - 1)
    for step in range(1, members):
        pl.semaphore_signal(
            barrier, inc=1, device_id={"member": (member + step) % members}, device_id_type=MESH
        )
    for target, preds in outgoing.values():
        expected = expected + both(preds[0], target // members != group).astype(jnp.int32)
    for source, preds in incoming.values():

        @pl.when(both(preds[0], source // members != group))
        def _():
            pl.semaphore_signal(barrier, inc=1, device_id=where_is(source), device_id_type=MESH)

    last = member == members - 1
    sends_last = both(last, has_q)
    gets_last = group > 0
    next_group = jnp.minimum(group + 1, devices // members - 1)
    prev_last = jnp.maximum(group * members - 1, 0)
    expected = expected + jnp.where(sends_last, members, 0)

    @pl.when(gets_last)
    def _():
        pl.semaphore_signal(barrier, inc=1, device_id=where_is(prev_last), device_id_type=MESH)

    first_in_group = both(member == 0, gets_last)
    expected = expected + first_in_group.astype(jnp.int32)

    @pl.when(sends_last)
    def _():
        pl.semaphore_signal(barrier, inc=1, device_id=(next_group, 0), device_id_type=MESH)

    kept, onward = jnp.int32(0), jnp.int32(0)
    for slot in range(2 * NB):
        index = old_ids[slot]
        kept = kept + both(index >= here * NB, index < here * NB + NB).astype(jnp.int32)
        onward = onward + (index >= here * NB + NB).astype(jnp.int32)
    kept = jnp.minimum(kept, NB)
    lacking = NB - kept

    for b in range(NB):
        for face in range(6):
            has = jnp.where(nbrs[b, face] >= 0, 1.0, 0.0).astype(jnp.float32)
            flags[b, face : face + 1, :] = jnp.full((1, LANES), has, jnp.float32)
        half_scale = 0.5 + 0.5 * refine[b].astype(jnp.float32)
        flags[b, 6:7, :] = jnp.full((1, LANES), half_scale, jnp.float32)
        flags[b, 7:8, :] = 1.0 / jnp.full((1, LANES), half_scale, jnp.float32)

    def settle(i, store):
        loads[i].wait()
        if i < 2:
            loads[i + 1].start()

        def own(p, carry):
            slot = jnp.maximum(p - lacking, 0)
            for tile in range(TILES):
                for part in range(PARTS):
                    value = olds[i][slot, 8 * part : 8 * part + 8, LANES * tile : LANES * (tile + 1)]
                    store(p, tile, part, jnp.where(p >= lacking, value, 0.0))
            return carry

        def following(p, carry):
            for tile in range(TILES):
                for part in range(PARTS):
                    value = olds[i][kept + p, 8 * part : 8 * part + 8, LANES * tile : LANES * (tile + 1)]
                    value = jnp.where(p < onward, value, 0.0)
                    store(NB + p, tile, part, value)
                    staged[i, p, flat(tile, part), :] = value
            return carry

        lax.fori_loop(0, NB, own, 0)
        lax.fori_loop(0, NB, following, 0)

    def pack(phase, s, field, volume, outer=True, inner=True):
        rows = EDGE * field

        def put(axis, side, bit, start, value):
            here_rows = pl.ds(rows + start, 8)
            if side == bit:
                send_out[phase][s, 2 * axis + side, here_rows, :] = value
            else:
                own_in[phase][s, bit, 3 * 0 + axis, here_rows, :] = value

        def wanted(side, bit):
            return outer if side == bit else inner

        for bit in (0, 1):
            for side in (0, 1):
                if not wanted(side, bit):
                    continue
                for j, b in enumerate(blocks_of(0, bit)):
                    line = volume[NB * s + b, pl.ds(PITCH + 8 + 31 * side, 8, stride=PITCH), :]
                    put(0, side, bit, 8 * j, line)
                for part in range(PARTS):
                    packed = jnp.zeros((8, LANES), jnp.float32)
                    for j, b in enumerate(blocks_of(1, bit)):
                        piece = volume[NB * s + b, spot(7 * side, part), :]
                        packed = jnp.where(lane // EDGE == j, roll(piece, EDGE * (j - 3 * side)), packed)
                    put(1, side, bit, 8 * part, packed)
            for quad in range(4):
                packed = [jnp.zeros((8, LANES), jnp.float32) for _ in (0, 1)]
                for half in (0, 1):
                    for j, b in enumerate(blocks_of(2, bit)):
                        for part in range(PARTS):
                            slot = 8 * j + 2 * part + half
                            piece = roll(volume[NB * s + b, spot(quad + 4 * half, part), :], slot)
                            for side in (0, 1):
                                if wanted(side, bit):
                                    packed[side] = jnp.where(
                                        depth == (slot + 31 * side) % EDGE, piece, packed[side]
                                    )
                for side in (0, 1):
                    if wanted(side, bit):
                        put(2, side, bit, 8 * quad, packed[side])

    def out_copy(phase, s, axis, side, t, target):
        face = 2 * axis + 1 - side
        if phase == 2:
            source, place = edge_sums.at[s], got_sums.at[t, s, face]
        else:
            source, place = send_out[phase].at[s, 2 * axis + side], recv_out[phase].at[t, s, face]
        return pltpu.make_async_remote_copy(
            src_ref=source,
            dst_ref=place,
            send_sem=out_send.at[phase, s, 2 * axis + side, t],
            recv_sem=out_recv.at[phase, t, s, face],
            device_id=where_is(target),
            device_id_type=MESH,
        )

    follower = jnp.minimum(here + 1, devices - 1)
    leader = jnp.maximum(here - 1, 0)

    def inner_copy(phase, s):
        if phase == 2:
            source, place = edge_sums.at[s], split_sums.at[1 - s]
        else:
            source, place = own_in[phase].at[s, 1 - s], recv_in[phase].at[1 - s]
        return pltpu.make_async_remote_copy(
            src_ref=source,
            dst_ref=place,
            send_sem=inner_send.at[phase, s],
            recv_sem=inner_recv.at[phase, 1 - s],
            device_id=where_is(follower if s else leader),
            device_id_type=MESH,
        )

    flag_copy = pltpu.make_async_remote_copy(
        src_ref=flags.at[pl.ds(0, NB)],
        dst_ref=flags.at[pl.ds(NB, NB)],
        send_sem=flag_send,
        recv_sem=flag_recv,
        device_id=where_is(leader),
        device_id_type=MESH,
    )
    moves = [
        pltpu.make_async_remote_copy(
            src_ref=staged.at[i],
            dst_ref=moved.at[i],
            send_sem=move_send.at[i],
            recv_sem=move_recv.at[i],
            device_id=where_is(follower),
            device_id_type=MESH,
        )
        for i in range(3)
    ]

    def start_exchange(phase, which):
        for (s, axis, side, t), (target, preds) in outgoing.items():
            if s == which:

                @pl.when(preds[phase])
                def _():
                    out_copy(phase, s, axis, side, t, target).start()

        @pl.when((p_split, q_stays)[which])
        def _():
            inner_copy(phase, which).start()

    def finish_exchange(phase):
        for (s, axis, side, t), (target, preds) in outgoing.items():

            @pl.when(preds[phase])
            def _():
                out_copy(phase, s, axis, side, t, target).wait_send()

        for (t, src, axis, side), (source, preds) in incoming.items():

            @pl.when(preds[phase])
            def _():
                out_copy(phase, src, axis, 1 - side, t, source).wait_recv()

        @pl.when(q_stays)
        def _():
            inner_copy(phase, 1).wait_send()
            inner_copy(phase, 0).wait_recv()

        @pl.when(p_split)
        def _():
            inner_copy(phase, 0).wait_send()
            inner_copy(phase, 1).wait_recv()

    def gather_ghosts(phase, t):
        split = (p_split, q_stays)[t]
        for axis in range(3):
            for side in (0, 1):
                face = 2 * axis + side
                total = 0.0
                for src in (0, 1):
                    pred = incoming[t, src, axis, side][1][phase]
                    if phase == 0 and (t, src, axis, side) == (0, 1, 0, 1):
                        own = jnp.where(even, send_out[0][1, 0], 0.0)
                        total = total + jnp.where(pred, recv_out[0][t, src, face], own)
                    else:
                        total = total + jnp.where(pred, recv_out[phase][t, src, face], 0.0)
                ghosts[phase][t, face] = total
                total = own_in[phase][t, side, axis]
                if side == t:
                    total = total + jnp.where(split, recv_in[phase][t, axis], 0.0)
                ghosts[phase][t, 6 + face] = total
        for bit in (0, 1):
            low, high = (4 if bit == 0 else 10), (5 if bit == 1 else 11)
            for chunk in range(4 * FIELDS[phase]):
                rows = slice(8 * chunk, 8 * chunk + 8)
                first = ghosts[phase][t, low, rows, :]
                second = roll(ghosts[phase][t, high, rows, :], 62)
                for half in (0, 1):
                    both_ends = jnp.where(depth % 2 != half, first, second)
                    edges[phase][t, 2 * bit + half, rows, :] = both_ends

    def fill(phase, q, field, volume, mirror):
        s, p = q // NB, q % NB
        rows = EDGE * field
        js = (p // 2, p % 2 + p // 4 * 2, p % 4)
        for side in (0, 1):
            kind = [jnp.where((p // 2**axis) % 2 == side, 0, 6) for axis in range(2)]
            ghost = ghosts[phase][s, kind[0] + side, pl.ds(pl.multiple_of(rows + 8 * js[0], 8), 8), :]
            has = flags[q, side : side + 1, :] > 0.5
            if mirror:
                spare = volume[q, pl.ds(PITCH + 8 + 31 * side, 8, stride=PITCH), :]
            else:
                spare = jnp.zeros_like(ghost)
            volume[q, pl.ds(PITCH + 7 + 33 * side, 8, stride=PITCH), :] = jnp.where(has, ghost, spare)
            has = flags[q, 2 + side : 3 + side, :] > 0.5
            for part in range(PARTS):
                ghost = ghosts[phase][s, kind[1] + 2 + side, rows + 8 * part : rows + 8 * part + 8, :]
                steps = EDGE * (3 - js[1]) if side == 0 else EDGE * ((4 - js[1]) % 4)
                ghost = pltpu.roll(ghost, steps, 1)
                if mirror:
                    spare = roll(volume[q, spot(7 * side, part), :], 96 - 64 * side)
                else:
                    spare = jnp.zeros_like(ghost)
                volume[q, spot(9 * side - 1, part), :] = jnp.where(has, ghost, spare)

    def z_edge(phase, q, field, tile, part, spare):
        s, p = q // NB, q % NB
        start = EDGE * field + 8 * (tile % 4)
        sheet = edges[phase][s, 2 * (p // 4) + tile // 4, start : start + 8, :]
        ghost = pltpu.roll(sheet, 97 - 2 * part - tile // 4 - 8 * (p % 4), 1)
        has = jnp.where(depth < EDGE // 2, flags[q, 4:5, :], flags[q, 5:6, :]) > 0.5
        return jnp.where(has, ghost, spare)

    def stencil(phase, q, volume, part):
        tiles = [volume[q, spot(t, part), :] for t in range(-1, TILES + 1)]
        down = [roll(t, EDGE) for t in tiles[:-1]]
        up = [None] + [roll(t, -EDGE) for t in tiles[1:]]
        for tile in range(TILES):
            value = tiles[tile + 1]
            top = PITCH * (tile + 1) + 8 + 8 * part
            x_minus = volume[q, top - 1 : top + 7, :]
            x_plus = volume[q, top + 1 : top + 9, :]
            y_minus = jnp.where(lane >= EDGE, down[tile + 1], down[tile])
            y_plus = jnp.where(lane < 3 * EDGE, up[tile + 1], up[tile + 2])
            edge = z_edge(phase, q, 0, tile, part, 0.0)
            z_minus = jnp.where(depth == 0, edge, roll(value, 1))
            z_plus = jnp.where(depth == EDGE - 1, edge, roll(value, -1))
            yield tile, value, (x_minus, x_plus, y_minus, y_plus, z_minus, z_plus)

    def weigh_inside(q, carry):
        for part in range(PARTS):
            tiles = [k_ref[q, spot(t, part), :] for t in range(TILES)]
            down = [roll(t, EDGE) for t in tiles]
            up = [roll(t, -EDGE) for t in tiles]
            for tile in range(TILES):
                place, k = flat(tile, part), tiles[tile]
                before, after = down[max(tile - 1, 0)], up[min(tile + 1, TILES - 1)]
                omega[q, 2, place, :] = k + jnp.where(lane >= EDGE, down[tile], before)
                omega[q, 3, place, :] = k + jnp.where(lane < 3 * EDGE, up[tile], after)
                omega[q, 4, place, :] = k + roll(k, 1)
                omega[q, 5, place, :] = k + roll(k, -1)
        return carry

    def weigh(q, part):
        before = roll(k_ref[q, spot(-1, part), :], EDGE)
        after = roll(k_ref[q, spot(TILES, part), :], -EDGE)
        for tile in range(TILES):
            place, k = flat(tile, part), k_ref[q, spot(tile, part), :]
            top = PITCH * (tile + 1) + 8 + 8 * part
            around_k = [k_ref[q, top - 1 : top + 7, :], k_ref[q, top + 1 : top + 9, :]]
            inside = [omega[q, face, place, :] for face in range(2, 6)]
            if tile == 0:
                inside[0] = jnp.where(lane >= EDGE, inside[0], k + before)
            if tile == TILES - 1:
                inside[1] = jnp.where(lane < 3 * EDGE, inside[1], k + after)
            edge = k + z_edge(0, q, 1, tile, part, k)
            inside[2] = jnp.where(depth == 0, edge, inside[2])
            inside[3] = jnp.where(depth == EDGE - 1, edge, inside[3])
            yield [k + beside for beside in around_k] + inside

    def valid(q):
        low = jnp.where(even, lacking, 0)
        return both(q >= low, q < NB + onward)

    def keep(kind, q, cell, value):
        acc[pl.ds(pl.multiple_of(8 * (8 * NB * kind + 4 * q + cell), 8), 8), :] = value

    def first_sweep(q, carry):
        fill(0, q, 0, u0, False)
        fill(0, q, 1, k_ref, True)
        holds = valid(q)
        totals = [jnp.zeros((8, LANES), jnp.float32) for _ in range(4)]
        for part in range(PARTS):
            for (tile, u, u_beside), weights in zip(stencil(0, q, u0, part), weigh(q, part)):
                total = sum(weights[1:], weights[0])
                scale = jnp.where(holds, OMEGA / total, 0.0)
                place = flat(tile, part)
                weight_sum[q, place, :] = total * (1.0 / OMEGA)
                right = f_ref[q, place, :]
                cell = part // 2 * 2 + tile // 4
                totals[cell] = totals[cell] + right
                gain = right * scale * flags[q, 7:8, :]
                f_ref[q, place, :] = gain
                new = (1.0 - OMEGA) * u + gain
                for face in range(6):
                    weight = weights[face] * scale
                    omega[q, face, place, :] = weight
                    new = new + weight * u_beside[face]
                u1[q, spot(tile, part), :] = new
        for cell in range(4):
            keep(SOURCE, q, cell, totals[cell])
        return carry

    sublane = lax.broadcasted_iota(jnp.int32, (8, LANES), 0)

    def second_sweep(q, send):
        fill(1, q, 0, u1, False)
        zero = jnp.zeros((8, LANES), jnp.float32)
        along_z = [zero] * 4
        along_y = {(layer, half): zero for layer in (0, 15, 16, 31) for half in (0, 1)}
        for part in range(PARTS):
            for tile, u, beside in stencil(1, q, u1, part):
                place = flat(tile, part)
                new = (1.0 - OMEGA) * u + f_ref[q, place, :]
                weights = [omega[q, face, place, :] for face in range(6)]
                for face in range(6):
                    new = new + weights[face] * beside[face]
                u0[q, spot(tile, part), :] = new
                if send:
                    final_send[q - NB, place, :] = new
                scaled = new * weight_sum[q, place, :]
                half, cell = part // 2, part // 2 * 2 + tile // 4
                outward = jnp.where(depth % (EDGE // 2) == EDGE // 2 - 1, weights[5], weights[4])
                along_z[cell] = along_z[cell] + outward * scaled
                if tile in (0, 4):
                    layer = 4 * tile
                    along_y[layer, half] = along_y[layer, half] + weights[2] * scaled
                if tile in (3, 7):
                    layer = 4 * tile + 3
                    along_y[layer, half] = along_y[layer, half] + weights[3] * scaled
        for layer, half in along_y:
            inside = lane < EDGE if layer in (0, 16) else lane >= 3 * EDGE
            along_y[layer, half] = jnp.where(inside, along_y[layer, half], 0.0)
        along_x = {}
        for layer, face in ((0, 0), (15, 1), (16, 0), (31, 1)):
            rows = pl.ds(layer, 8, stride=EDGE)
            value = u0[q, pl.ds(PITCH + 8 + layer, 8, stride=PITCH), :]
            along_x[layer] = omega[q, face, rows, :] * weight_sum[q, rows, :] * value
        middle = along_x[15] - along_x[16]
        own_x = (along_x[0] + middle, along_x[31] - middle)
        for a in (0, 1):
            middle = along_y[15, a] - along_y[16, a]
            own_y = (along_y[0, a] + middle, along_y[31, a] - middle)
            for b in (0, 1):
                upper = sublane // 4 == b
                keep(OWN, q, 2 * a + b, jnp.where(upper, own_x[a], 0.0) + own_y[b])
                keep(ALONG_X, q, 2 * a + b, jnp.where(upper, along_x[31 * a], 0.0))
                keep(ALONG_Y, q, 2 * a + b, along_y[31 * a, b])
                keep(ALONG_Z, q, 2 * a + b, along_z[2 * a + b])

    cell_lane = lax.broadcasted_iota(jnp.int32, (1, LANES), 1)
    block_of = cell_lane // 8 % NB
    corner = (cell_lane // 4 % 2, cell_lane // 2 % 2, cell_lane % 2)
    wide = (LANES, LANES)
    from_depth = lax.broadcasted_iota(jnp.int32, wide, 0) % EDGE
    to_corner = lax.broadcasted_iota(jnp.int32, wide, 1) % 2
    by_half = (from_depth // (EDGE // 2) == to_corner).astype(jnp.float32)

    def one_at(level):
        return (from_depth == level).astype(jnp.float32)

    def take(value, choose):
        return jnp.dot(value, choose, precision=HIGHEST, preferred_element_type=jnp.float32)

    def sums_of(kind):
        groups = []
        for group in range(8):
            start = 8 * (8 * NB * kind + 8 * group)
            groups.append(sum(acc[pl.ds(start + i, 8, stride=8), :] for i in range(8)))
        return jnp.concatenate(groups, axis=0)

    def pick(value, s, block, place):
        rows = lax.broadcasted_iota(jnp.int32, (4 * NB, LANES), 0)
        part = value[4 * NB * s : 4 * NB * (s + 1), :]
        return jnp.sum(jnp.where(rows == 4 * block + place, part, 0.0), axis=0, keepdims=True)

    def other(axis):
        bit = block_of // 2**axis % 2
        return block_of + 2**axis * (1 - 2 * bit)


    def pack_all(field, volume):
        def body(s, carry):
            pack(0, s, field, volume)
            return carry

        lax.fori_loop(0, 2, body, 0)

    def gather_all(phase):
        gather_ghosts(phase, 0)

        @pl.when(odd)
        def _():
            gather_ghosts(phase, 1)

    def to_volume(volume):
        def store(q, tile, part, value):
            volume[q, spot(tile, part), :] = value

        return store

    def to_source(q, tile, part, value):
        f_ref[q, flat(tile, part), :] = value

    settle(0, to_volume(u0))
    pack_all(0, u0)
    settle(1, to_volume(k_ref))
    pack_all(1, k_ref)
    pl.semaphore_wait(barrier, expected)
    start_exchange(0, 1)
    start_exchange(0, 0)

    @pl.when(p_split)
    def _():
        flag_copy.start()

    @pl.when(even)
    def _():
        moves[0].start()
        moves[1].start()

    settle(2, to_source)

    @pl.when(even)
    def _():
        moves[2].start()

    @pl.when(odd)
    def _():
        lax.fori_loop(NB, 2 * NB, weigh_inside, 0)
        for i in range(3):
            moves[i].wait_recv()

        def merge(p, carry):
            for tile in range(TILES):
                for part in range(PARTS):
                    for i, volume in enumerate((u0, k_ref)):
                        volume[p, spot(tile, part), :] += moved[i, p, flat(tile, part), :]
                    f_ref[p, flat(tile, part), :] += moved[2, p, flat(tile, part), :]
            return carry

        lax.fori_loop(0, NB, merge, 0)
        pack(0, 0, 0, u0, outer=False)
        pack(0, 0, 1, k_ref, outer=False)

    lax.fori_loop(0, NB, weigh_inside, 0)
    finish_exchange(0)

    @pl.when(p_split)
    def _():
        flag_copy.wait_send()

    @pl.when(q_stays)
    def _():
        flag_copy.wait_recv()

    gather_all(0)

    @pl.when(odd)
    def _():
        lax.fori_loop(NB, 2 * NB, first_sweep, 0)
        pack(1, 1, 0, u1)
        start_exchange(1, 1)

    lax.fori_loop(0, NB, first_sweep, 0)
    pack(1, 0, 0, u1)
    start_exchange(1, 0)

    cells = take(sums_of(SOURCE), by_half)
    source_sums = [pick(cells, s, block_of, cell_lane // 2 % 4) for s in (0, 1)]
    finish_exchange(1)
    gather_all(1)

    def final_copy(p):
        return pltpu.make_async_remote_copy(
            src_ref=final_send.at[p],
            dst_ref=final_recv.at[p],
            send_sem=last_send.at[p],
            recv_sem=last_recv.at[p],
            device_id=where_is(follower),
            device_id_type=MESH,
        )

    @pl.when(odd)
    def _():
        def body(q, carry):
            second_sweep(q, True)

            @pl.when(both(has_q, q < NB + EARLY))
            def _():
                final_copy(q - NB).start()

            return carry

        lax.fori_loop(NB, 2 * NB, body, 0)

    def body(q, carry):
        second_sweep(q, False)
        return carry

    lax.fori_loop(0, NB, body, 0)

    middle = take(jnp.concatenate([sums_of(kind) for kind in (OWN, ALONG_X, ALONG_Y)], axis=0), by_half)
    crossing = one_at(15) - one_at(16)
    low_cells, high_cells = one_at(0) + crossing, one_at(EDGE - 1) - crossing
    z_sums = sums_of(ALONG_Z)
    own_z = take(z_sums, jnp.where(to_corner == 0, low_cells, high_cells))
    face_z = take(z_sums, jnp.where(to_corner == 0, one_at(EDGE - 1), one_at(0)))
    size = 8 * NB
    own_sums = []
    for s in (0, 1):
        own_sums.append(pick(middle[:size] + own_z, s, block_of, cell_lane // 2 % 4))
        face_x = pick(middle[size : 2 * size], s, other(0), 2 * (1 - corner[0]) + corner[1])
        face_y = pick(middle[2 * size :], s, other(1), 2 * (1 - corner[1]) + corner[0])
        near_z = pick(face_z, s, other(2), cell_lane // 2 % 4)
        edge_sums[s] = jnp.where(sublane == 0, face_x, jnp.where(sublane == 1, face_y, near_z))
    start_exchange(2, 0)

    @pl.when(odd)
    def _():
        start_exchange(2, 1)

    @pl.when(q_stays)
    def _():
        for p in range(EARLY, MIDDLE):
            final_copy(p).start()

    finish_exchange(2)
    totals = []
    for t in (0, 1):
        combined = jnp.zeros((8, LANES), jnp.float32)
        for p in range(NB):
            combined = jnp.where(lane // 8 % NB == p, flags[NB * t + p], combined)
        beyond = jnp.zeros((1, LANES), jnp.float32)
        for axis in range(3):
            row = slice(axis, axis + 1)
            outer, linked = [], []
            for side in (0, 1):
                face = 2 * axis + side
                total = 0.0
                for src in (0, 1):
                    pred = incoming[t, src, axis, side][1][2]
                    total = total + jnp.where(pred, got_sums[t, src, face, row, :], 0.0)
                outer.append(total)
                linked.append(combined[face : face + 1, :])
            split = jnp.where((p_split, q_stays)[t], split_sums[t, row, :], 0.0)
            inner = edge_sums[t, row, :] + split
            outer = jnp.where(corner[axis] == 0, outer[0], outer[1])
            linked = jnp.where(corner[axis] == 0, linked[0], linked[1])
            beside = jnp.where(block_of // 2**axis % 2 == corner[axis], outer, inner)
            beyond = beyond + jnp.where(linked > 0.5, beside, 0.0)
        held = block_of < onward if t else block_of >= jnp.where(even, lacking, 0)
        change = combined[6:7, :] * (beyond - own_sums[t])
        totals.append(jnp.where(held, source_sums[t] + change, 0.0))
    low_half = jnp.where(odd, totals[1], totals[0])
    total = jnp.where(cell_lane < 64, low_half, jnp.where(odd, totals[0], 0.0))
    mine[...] = jnp.broadcast_to(total * (EDGE // 2) ** (-1.5), (8, LANES))

    def sum_copy(step):
        return pltpu.make_async_remote_copy(
            src_ref=mine,
            dst_ref=all_sums.at[member],
            send_sem=sum_send.at[step],
            recv_sem=sum_recv.at[step],
            device_id={"member": (member + step) % members},
            device_id_type=MESH,
        )

    def on_copy(step):
        return pltpu.make_async_remote_copy(
            src_ref=mine,
            dst_ref=all_sums.at[members],
            send_sem=sum_send.at[members + step],
            recv_sem=sum_recv.at[0],
            device_id=(next_group, step),
            device_id_type=MESH,
        )

    for step in range(1, members):
        sum_copy(step).start()

    @pl.when(sends_last)
    def _():
        for step in range(members):
            on_copy(step).start()

    @pl.when(q_stays)
    def _():
        for p in range(MIDDLE, NB):
            final_copy(p).start()

    all_sums[member] = mine[...]
    for step in range(1, members):
        sum_copy(step).wait_send()
        sum_copy(step).wait_recv()

    @pl.when(sends_last)
    def _():
        for step in range(members):
            on_copy(step).wait_send()

    @pl.when(gets_last)
    def _():
        on_copy(0).wait_recv()

    correction = jnp.zeros((8 * NB, LANES), jnp.float32)
    for pair in range(members // 2):
        if pair == 0:
            before = jnp.where(gets_last, all_sums[members, 0:1, :], 0.0)
        else:
            before = all_sums[2 * pair - 1, 0:1, :]
        even_cells = all_sums[2 * pair, 0:1, :] + before
        vector = jnp.where(cell_lane < 64, even_cells, all_sums[2 * pair + 1, 0:1, :])
        correction = correction + inverse[0, :, LANES * pair : LANES * (pair + 1)] * vector
    rows_e[...] = jnp.broadcast_to(jnp.sum(correction, axis=1, keepdims=True), (8 * NB, LANES))

    @pl.when(p_split)
    def _():
        for p in range(NB):
            final_copy(p).wait_recv()

    def finish(p, carry):
        for cell in range(4):
            first = pl.multiple_of(8 * p, 8) + 2 * cell
            lift = jnp.where(depth < EDGE // 2, rows_e[pl.ds(first, 1), :], rows_e[pl.ds(first + 1, 1), :])
            for part in (2 * (cell // 2), 2 * (cell // 2) + 1):
                for tile in range(4 * (cell % 2), 4 * (cell % 2) + 4):
                    arrived = jnp.where(p_split, final_recv[p, flat(tile, part), :], 0.0)
                    value = u0[p, spot(tile, part), :] + arrived + lift
                    out_ref[p, 8 * part : 8 * part + 8, LANES * tile : LANES * (tile + 1)] = value
        return carry

    lax.fori_loop(0, NB, finish, 0)

    @pl.when(even)
    def _():
        for i in range(3):
            moves[i].wait_send()

    @pl.when(q_stays)
    def _():
        for p in range(NB):
            final_copy(p).wait_send()


def local(old_ids, field_old, source_old, kappa_old, refine, neighbors, coarse_inverse):
    members = lax.axis_size("member")
    devices = lax.axis_size(AXES)
    flat_shape = (NB, TILES * EDGE, LANES)
    both_shape = (2 * NB, TILES * EDGE, LANES)
    padded = (2 * NB, 10 * PITCH, LANES)
    shapes = [field_old.shape] * 3 + [padded] * 3 + [both_shape]
    shapes += [(2 * NB, 6, TILES * EDGE, LANES), both_shape, (3,) + flat_shape, (3,) + flat_shape]
    shapes += [flat_shape, flat_shape]
    shapes += [(2, 6, EDGE * n, LANES) for n in FIELDS]
    shapes += [(2, 2, 3, EDGE * n, LANES) for n in FIELDS]
    shapes += [(2, 2, 6, EDGE * n, LANES) for n in FIELDS]
    shapes += [(2, 3, EDGE * n, LANES) for n in FIELDS]
    shapes += [(2, 12, EDGE * n, LANES) for n in FIELDS]
    shapes += [(2 * NB, 8, LANES), (5 * 64 * NB, LANES), (8, LANES), (members + 1, 8, LANES)]
    shapes += [(8 * NB, LANES), (2, 8, LANES), (2, 2, 6, 8, LANES), (2, 8, LANES)]
    shapes += [(2, 4, EDGE * n, LANES) for n in FIELDS]
    dma = pltpu.SemaphoreType.DMA
    scratch = [pltpu.VMEM(s, jnp.float32) for s in shapes]
    scratch += [dma((3,)), dma((3,)), dma((3,)), dma((3, 2, 6, 2)), dma((3, 2, 2, 6))]
    scratch += [dma((3, 2)), dma((3, 2)), dma, dma, dma((NB,)), dma((NB,))]
    scratch += [dma((2 * members,)), dma((members,))]
    return pl.pallas_call(
        functools.partial(main_kernel, members, devices),
        out_shape=jax.ShapeDtypeStruct((NB, EDGE, FACE), jnp.float32),
        in_specs=[SM, SM, SM, VM, ANY, ANY, ANY],
        out_specs=VM,
        scratch_shapes=scratch,
        compiler_params=pltpu.CompilerParams(
            collective_id=1, has_side_effects=True, vmem_limit_bytes=VMEM_LIMIT
        ),
    )(old_ids, neighbors, refine, coarse_inverse, field_old, source_old, kappa_old)


def solution(mesh):
    in_specs = (
        P(AXES),
        P(AXES, None, None),
        P(AXES, None, None),
        P(AXES, None, None),
        P(AXES),
        P(AXES, None),
        P("group", "member", None),
    )
    return jax.shard_map(
        local, mesh=mesh, in_specs=in_specs, out_specs=P(AXES, None, None), check_vma=False
    )
```

```python
import functools

import jax
import jax.numpy as jnp
from jax import lax
from jax.experimental import pallas as pl
from jax.experimental.pallas import tpu as pltpu
from jax.sharding import PartitionSpec as P

OMEGA = 0.8
AXES = ("group", "member")
NB, EDGE, FACE, LANES = 8, 32, 1024, 128
TILES, PARTS, PITCH = 8, 4, 48
HIGHEST = lax.Precision.HIGHEST
VMEM_LIMIT = 60 * 2**20
VM = pl.BlockSpec(memory_space=pltpu.VMEM)
ANY = pl.BlockSpec(memory_space=pl.ANY)
SM = pl.BlockSpec(memory_space=pltpu.SMEM)
MESH = pl.DeviceIdType.MESH
FIELDS = (2, 1)
EARLY, MIDDLE = 4, 6
OWN, ALONG_X, ALONG_Y, ALONG_Z, SOURCE = range(5)


def roll(value, steps):
    return pltpu.roll(value, steps % LANES, 1)


def spot(tile, part):
    return slice(PITCH * (tile + 1) + 8 + 8 * part, PITCH * (tile + 1) + 16 + 8 * part)


def flat(tile, part):
    return slice(EDGE * tile + 8 * part, EDGE * tile + 8 * part + 8)


def blocks_of(axis, side):
    return [b for b in range(NB) if (b >> axis) % 2 == side]


def octet_neighbors(octet, devices):
    nbits = devices.bit_length() - 1
    bits = [octet // 2**i % 2 for i in range(nbits)]
    result = []
    for axis in range(3):
        own = [i for i in range(nbits) if i % 3 == axis]
        extent = 2 ** len(own)
        coord = sum(bits[i] * 2**n for n, i in enumerate(own))
        base = octet - sum(bits[i] * 2**i for i in own)
        pair = []
        for step in (-1, 1):
            moved = coord + step
            inside = jnp.logical_and(moved >= 0, moved < extent)
            clipped = jnp.clip(moved, 0, extent - 1)
            index = base + sum(clipped // 2**n % 2 * 2**i for n, i in enumerate(own))
            pair.append((inside, index))
        result.append(pair)
    return result


def main_kernel(members, devices, old_ids, nbrs, refine, inverse, u_old, f_old, k_old, out_ref, *scratch):
    olds = scratch[0:3]
    u0, u1, k_ref, f_ref, omega, weight_sum, staged, moved, final_send, final_recv = scratch[3:13]
    send_out, own_in, recv_out, recv_in, ghosts = [scratch[13 + 2 * i : 15 + 2 * i] for i in range(5)]
    flags, acc, mine, all_sums, rows_e, edge_sums, got_sums, split_sums = scratch[23:31]
    edges = scratch[31:33]
    result, out_sem = olds[2].at[pl.ds(0, NB)], scratch[46]
    in_sem, move_send, move_recv, out_send, out_recv, inner_send, inner_recv = scratch[33:40]
    flag_send, flag_recv, last_send, last_recv, sum_send, sum_recv = scratch[40:46]

    group, member = lax.axis_index("group"), lax.axis_index("member")
    here = group * members + member
    odd = here % 2 == 1
    even = here % 2 == 0
    odd_int = here % 2
    has_q = here < devices - 1
    q_stays = jnp.logical_and(odd, has_q)
    p_split = jnp.logical_and(even, here > 0)
    around = [octet_neighbors(here, devices), octet_neighbors(here + 1, devices)]
    lane = lax.broadcasted_iota(jnp.int32, (8, LANES), 1)
    depth = lane % EDGE

    def where_is(index):
        return (index // members, index % members)

    loads = [
        pltpu.make_async_copy(ref, olds[i], in_sem.at[i]) for i, ref in enumerate((u_old, k_old, f_old))
    ]
    loads[0].start()

    def both(*preds):
        result = preds[0]
        for pred in preds[1:]:
            result = jnp.logical_and(result, pred)
        return result

    outgoing, incoming = {}, {}
    for s in (0, 1):
        for axis in (2, 1, 0):
            for side in (0, 1):
                inside, index = around[s][axis][side]
                exists = inside if s == 0 else both(inside, has_q)
                stays = inside if s == 0 else both(inside, q_stays)
                holder = both(index % 2 == 0, index > 0)
                for t in (0, 1):
                    target = index if t == 0 else jnp.maximum(index - 1, 0)
                    first = exists if t == 0 else both(exists, holder)
                    if s == 1 and t == 0 and axis == 0 and side == 0:
                        first = both(first, odd)
                    later = stays if t == 0 else both(stays, holder)
                    outgoing[s, axis, side, t] = (target, (first, later, later))
                receives = inside if s == 0 else both(inside, q_stays)
                for src in (0, 1):
                    source = index if src == 0 else jnp.maximum(index - 1, 0)
                    first = receives if src == 0 else both(receives, index > 0)
                    if s == 0 and src == 1 and axis == 0 and side == 1:
                        first = both(first, odd)
                    later = receives if src == 0 else both(receives, holder)
                    incoming[s, src, axis, side] = (source, (first, later, later))

    for b in range(NB):
        flags[NB + b] = jnp.ones((8, LANES), jnp.float32)
    barrier = pltpu.get_barrier_semaphore()
    expected = jnp.int32(members - 1)
    for step in range(1, members):
        pl.semaphore_signal(
            barrier, inc=1, device_id={"member": (member + step) % members}, device_id_type=MESH
        )
    for target, preds in outgoing.values():
        expected = expected + both(preds[0], target // members != group).astype(jnp.int32)
    for source, preds in incoming.values():

        @pl.when(both(preds[0], source // members != group))
        def _():
            pl.semaphore_signal(barrier, inc=1, device_id=where_is(source), device_id_type=MESH)

    last = member == members - 1
    sends_last = both(last, has_q)
    gets_last = group > 0
    next_group = jnp.minimum(group + 1, devices // members - 1)
    prev_last = jnp.maximum(group * members - 1, 0)
    expected = expected + jnp.where(sends_last, members, 0)

    @pl.when(gets_last)
    def _():
        pl.semaphore_signal(barrier, inc=1, device_id=where_is(prev_last), device_id_type=MESH)

    first_in_group = both(member == 0, gets_last)
    expected = expected + first_in_group.astype(jnp.int32)

    @pl.when(sends_last)
    def _():
        pl.semaphore_signal(barrier, inc=1, device_id=(next_group, 0), device_id_type=MESH)

    kept, onward = jnp.int32(0), jnp.int32(0)
    for slot in range(2 * NB):
        index = old_ids[slot]
        kept = kept + both(index >= here * NB, index < here * NB + NB).astype(jnp.int32)
        onward = onward + (index >= here * NB + NB).astype(jnp.int32)
    kept = jnp.minimum(kept, NB)
    lacking = NB - kept

    for b in range(NB):
        for face in range(6):
            has = jnp.where(nbrs[b, face] >= 0, 1.0, 0.0).astype(jnp.float32)
            flags[b, face : face + 1, :] = jnp.full((1, LANES), has, jnp.float32)
        half_scale = 0.5 + 0.5 * refine[b].astype(jnp.float32)
        flags[b, 6:7, :] = jnp.full((1, LANES), half_scale, jnp.float32)
        flags[b, 7:8, :] = 1.0 / jnp.full((1, LANES), half_scale, jnp.float32)

    def settle(i, store):
        loads[i].wait()
        if i < 2:
            loads[i + 1].start()

        def own(p, carry):
            slot = jnp.maximum(p - lacking, 0)
            for tile in range(TILES):
                for part in range(PARTS):
                    value = olds[i][slot, 8 * part : 8 * part + 8, LANES * tile : LANES * (tile + 1)]
                    store(p, tile, part, jnp.where(p >= lacking, value, 0.0))
            return carry

        def following(p, carry):
            for tile in range(TILES):
                for part in range(PARTS):
                    value = olds[i][kept + p, 8 * part : 8 * part + 8, LANES * tile : LANES * (tile + 1)]
                    value = jnp.where(p < onward, value, 0.0)
                    store(NB + p, tile, part, value)
                    staged[i, p, flat(tile, part), :] = value
            return carry

        lax.fori_loop(0, NB, own, 0)
        lax.fori_loop(0, NB, following, 0)

    def pack(phase, s, field, volume, outer=True, inner=True):
        rows = EDGE * field

        def put(axis, side, bit, start, value):
            here_rows = pl.ds(rows + start, 8)
            if side == bit:
                send_out[phase][s, 2 * axis + side, here_rows, :] = value
            else:
                own_in[phase][s, bit, 3 * 0 + axis, here_rows, :] = value

        def wanted(side, bit):
            return outer if side == bit else inner

        for bit in (0, 1):
            for side in (0, 1):
                if not wanted(side, bit):
                    continue
                for j, b in enumerate(blocks_of(0, bit)):
                    line = volume[NB * s + b, pl.ds(PITCH + 8 + 31 * side, 8, stride=PITCH), :]
                    put(0, side, bit, 8 * j, line)
                for part in range(PARTS):
                    packed = jnp.zeros((8, LANES), jnp.float32)
                    for j, b in enumerate(blocks_of(1, bit)):
                        piece = volume[NB * s + b, spot(7 * side, part), :]
                        packed = jnp.where(lane // EDGE == j, roll(piece, EDGE * (j - 3 * side)), packed)
                    put(1, side, bit, 8 * part, packed)
            for quad in range(4):
                packed = [jnp.zeros((8, LANES), jnp.float32) for _ in (0, 1)]
                for half in (0, 1):
                    for j, b in enumerate(blocks_of(2, bit)):
                        for part in range(PARTS):
                            slot = 8 * j + 2 * part + half
                            piece = roll(volume[NB * s + b, spot(quad + 4 * half, part), :], slot)
                            for side in (0, 1):
                                if wanted(side, bit):
                                    packed[side] = jnp.where(
                                        depth == (slot + 31 * side) % EDGE, piece, packed[side]
                                    )
                for side in (0, 1):
                    if wanted(side, bit):
                        put(2, side, bit, 8 * quad, packed[side])

    def out_copy(phase, s, axis, side, t, target):
        face = 2 * axis + 1 - side
        if phase == 2:
            source, place = edge_sums.at[s], got_sums.at[t, s, face]
        else:
            source, place = send_out[phase].at[s, 2 * axis + side], recv_out[phase].at[t, s, face]
        return pltpu.make_async_remote_copy(
            src_ref=source,
            dst_ref=place,
            send_sem=out_send.at[phase, s, 2 * axis + side, t],
            recv_sem=out_recv.at[phase, t, s, face],
            device_id=where_is(target),
            device_id_type=MESH,
        )

    follower = jnp.minimum(here + 1, devices - 1)
    leader = jnp.maximum(here - 1, 0)

    def inner_copy(phase, s):
        if phase == 2:
            source, place = edge_sums.at[s], split_sums.at[1 - s]
        else:
            source, place = own_in[phase].at[s, 1 - s], recv_in[phase].at[1 - s]
        return pltpu.make_async_remote_copy(
            src_ref=source,
            dst_ref=place,
            send_sem=inner_send.at[phase, s],
            recv_sem=inner_recv.at[phase, 1 - s],
            device_id=where_is(follower if s else leader),
            device_id_type=MESH,
        )

    flag_copy = pltpu.make_async_remote_copy(
        src_ref=flags.at[pl.ds(0, NB)],
        dst_ref=flags.at[pl.ds(NB, NB)],
        send_sem=flag_send,
        recv_sem=flag_recv,
        device_id=where_is(leader),
        device_id_type=MESH,
    )
    moves = [
        pltpu.make_async_remote_copy(
            src_ref=staged.at[i],
            dst_ref=moved.at[i],
            send_sem=move_send.at[i],
            recv_sem=move_recv.at[i],
            device_id=where_is(follower),
            device_id_type=MESH,
        )
        for i in range(3)
    ]

    def start_exchange(phase, which):
        @pl.when((p_split, q_stays)[which])
        def _():
            inner_copy(phase, which).start()

        for (s, axis, side, t), (target, preds) in outgoing.items():
            if s == which:

                @pl.when(preds[phase])
                def _():
                    out_copy(phase, s, axis, side, t, target).start()

    def take_exchange(phase, which):
        for (t, src, axis, side), (source, preds) in incoming.items():
            if t == which:

                @pl.when(preds[phase])
                def _():
                    out_copy(phase, src, axis, 1 - side, t, source).wait_recv()

        @pl.when((p_split, q_stays)[which])
        def _():
            inner_copy(phase, 1 - which).wait_recv()

    def end_exchange(phase):
        for (s, axis, side, t), (target, preds) in outgoing.items():

            @pl.when(preds[phase])
            def _():
                out_copy(phase, s, axis, side, t, target).wait_send()

        for s, split in enumerate((p_split, q_stays)):

            @pl.when(split)
            def _():
                inner_copy(phase, s).wait_send()

    def gather_ghosts(phase, t):
        split = (p_split, q_stays)[t]
        for axis in range(3):
            for side in (0, 1):
                face = 2 * axis + side
                total = 0.0
                for src in (0, 1):
                    pred = incoming[t, src, axis, side][1][phase]
                    if phase == 0 and (t, src, axis, side) == (0, 1, 0, 1):
                        own = jnp.where(even, send_out[0][1, 0], 0.0)
                        total = total + jnp.where(pred, recv_out[0][t, src, face], own)
                    else:
                        total = total + jnp.where(pred, recv_out[phase][t, src, face], 0.0)
                ghosts[phase][t, face] = total
                total = own_in[phase][t, side, axis]
                if side == t:
                    total = total + jnp.where(split, recv_in[phase][t, axis], 0.0)
                ghosts[phase][t, 6 + face] = total
        for bit in (0, 1):
            low, high = (4 if bit == 0 else 10), (5 if bit == 1 else 11)
            for chunk in range(4 * FIELDS[phase]):
                rows = slice(8 * chunk, 8 * chunk + 8)
                first = ghosts[phase][t, low, rows, :]
                second = roll(ghosts[phase][t, high, rows, :], 62)
                for half in (0, 1):
                    both_ends = jnp.where(depth % 2 != half, first, second)
                    edges[phase][t, 2 * bit + half, rows, :] = both_ends

    def fill(phase, q, field, volume, mirror):
        s, p = q // NB, q % NB
        rows = EDGE * field
        js = (p // 2, p % 2 + p // 4 * 2, p % 4)
        for side in (0, 1):
            kind = [jnp.where((p // 2**axis) % 2 == side, 0, 6) for axis in range(2)]
            ghost = ghosts[phase][s, kind[0] + side, pl.ds(pl.multiple_of(rows + 8 * js[0], 8), 8), :]
            has = flags[q, side : side + 1, :] > 0.5
            if mirror:
                spare = volume[q, pl.ds(PITCH + 8 + 31 * side, 8, stride=PITCH), :]
            else:
                spare = jnp.zeros_like(ghost)
            volume[q, pl.ds(PITCH + 7 + 33 * side, 8, stride=PITCH), :] = jnp.where(has, ghost, spare)
            has = flags[q, 2 + side : 3 + side, :] > 0.5
            for part in range(PARTS):
                ghost = ghosts[phase][s, kind[1] + 2 + side, rows + 8 * part : rows + 8 * part + 8, :]
                steps = EDGE * (3 - js[1]) if side == 0 else EDGE * ((4 - js[1]) % 4)
                ghost = pltpu.roll(ghost, steps, 1)
                if mirror:
                    spare = roll(volume[q, spot(7 * side, part), :], 96 - 64 * side)
                else:
                    spare = jnp.zeros_like(ghost)
                volume[q, spot(9 * side - 1, part), :] = jnp.where(has, ghost, spare)

    def z_edge(phase, q, field, tile, part, spare):
        s, p = q // NB, q % NB
        start = EDGE * field + 8 * (tile % 4)
        sheet = edges[phase][s, 2 * (p // 4) + tile // 4, start : start + 8, :]
        ghost = pltpu.roll(sheet, 97 - 2 * part - tile // 4 - 8 * (p % 4), 1)
        has = jnp.where(depth < EDGE // 2, flags[q, 4:5, :], flags[q, 5:6, :]) > 0.5
        return jnp.where(has, ghost, spare)

    def stencil(phase, q, volume, part):
        tiles = [volume[q, spot(t, part), :] for t in range(-1, TILES + 1)]
        down = [roll(t, EDGE) for t in tiles[:-1]]
        up = [None] + [roll(t, -EDGE) for t in tiles[1:]]
        for tile in range(TILES):
            value = tiles[tile + 1]
            top = PITCH * (tile + 1) + 8 + 8 * part
            x_minus = volume[q, top - 1 : top + 7, :]
            x_plus = volume[q, top + 1 : top + 9, :]
            y_minus = jnp.where(lane >= EDGE, down[tile + 1], down[tile])
            y_plus = jnp.where(lane < 3 * EDGE, up[tile + 1], up[tile + 2])
            edge = z_edge(phase, q, 0, tile, part, 0.0)
            z_minus = jnp.where(depth == 0, edge, roll(value, 1))
            z_plus = jnp.where(depth == EDGE - 1, edge, roll(value, -1))
            yield tile, value, (x_minus, x_plus, y_minus, y_plus, z_minus, z_plus)

    def weigh_inside(q, carry):
        for part in range(PARTS):
            tiles = [k_ref[q, spot(t, part), :] for t in range(TILES)]
            down = [roll(t, EDGE) for t in tiles]
            up = [roll(t, -EDGE) for t in tiles]
            for tile in range(TILES):
                place, k = flat(tile, part), tiles[tile]
                before, after = down[max(tile - 1, 0)], up[min(tile + 1, TILES - 1)]
                omega[q, 2, place, :] = k + jnp.where(lane >= EDGE, down[tile], before)
                omega[q, 3, place, :] = k + jnp.where(lane < 3 * EDGE, up[tile], after)
                omega[q, 4, place, :] = k + roll(k, 1)
                omega[q, 5, place, :] = k + roll(k, -1)
        return carry

    def weigh(q, part):
        before = roll(k_ref[q, spot(-1, part), :], EDGE)
        after = roll(k_ref[q, spot(TILES, part), :], -EDGE)
        for tile in range(TILES):
            place, k = flat(tile, part), k_ref[q, spot(tile, part), :]
            top = PITCH * (tile + 1) + 8 + 8 * part
            around_k = [k_ref[q, top - 1 : top + 7, :], k_ref[q, top + 1 : top + 9, :]]
            inside = [omega[q, face, place, :] for face in range(2, 6)]
            if tile == 0:
                inside[0] = jnp.where(lane >= EDGE, inside[0], k + before)
            if tile == TILES - 1:
                inside[1] = jnp.where(lane < 3 * EDGE, inside[1], k + after)
            edge = k + z_edge(0, q, 1, tile, part, k)
            inside[2] = jnp.where(depth == 0, edge, inside[2])
            inside[3] = jnp.where(depth == EDGE - 1, edge, inside[3])
            yield [k + beside for beside in around_k] + inside

    def valid(q):
        low = jnp.where(even, lacking, 0)
        return both(q >= low, q < NB + onward)

    def keep(kind, q, cell, value):
        acc[pl.ds(pl.multiple_of(8 * (8 * NB * kind + 4 * q + cell), 8), 8), :] = value

    def first_sweep(q, carry):
        fill(0, q, 0, u0, False)
        fill(0, q, 1, k_ref, True)
        holds = valid(q)
        totals = [jnp.zeros((8, LANES), jnp.float32) for _ in range(4)]
        for part in range(PARTS):
            for (tile, u, u_beside), weights in zip(stencil(0, q, u0, part), weigh(q, part)):
                total = sum(weights[1:], weights[0])
                scale = jnp.where(holds, OMEGA / total, 0.0)
                place = flat(tile, part)
                weight_sum[q, place, :] = total * (1.0 / OMEGA)
                right = f_ref[q, place, :]
                cell = part // 2 * 2 + tile // 4
                totals[cell] = totals[cell] + right
                gain = right * scale * flags[q, 7:8, :]
                f_ref[q, place, :] = gain
                new = (1.0 - OMEGA) * u + gain
                for face in range(6):
                    weight = weights[face] * scale
                    omega[q, face, place, :] = weight
                    new = new + weight * u_beside[face]
                u1[q, spot(tile, part), :] = new
        for cell in range(4):
            keep(SOURCE, q, cell, totals[cell])
        return carry

    sublane = lax.broadcasted_iota(jnp.int32, (8, LANES), 0)

    def second_sweep(q, send):
        fill(1, q, 0, u1, False)
        zero = jnp.zeros((8, LANES), jnp.float32)
        along_z = [zero] * 4
        along_y = {(layer, half): zero for layer in (0, 15, 16, 31) for half in (0, 1)}
        for part in range(PARTS):
            for tile, u, beside in stencil(1, q, u1, part):
                place = flat(tile, part)
                new = (1.0 - OMEGA) * u + f_ref[q, place, :]
                weights = [omega[q, face, place, :] for face in range(6)]
                for face in range(6):
                    new = new + weights[face] * beside[face]
                u0[q, spot(tile, part), :] = new
                if send:
                    final_send[q - NB, place, :] = new
                scaled = new * weight_sum[q, place, :]
                half, cell = part // 2, part // 2 * 2 + tile // 4
                outward = jnp.where(depth % (EDGE // 2) == EDGE // 2 - 1, weights[5], weights[4])
                along_z[cell] = along_z[cell] + outward * scaled
                if tile in (0, 4):
                    layer = 4 * tile
                    along_y[layer, half] = along_y[layer, half] + weights[2] * scaled
                if tile in (3, 7):
                    layer = 4 * tile + 3
                    along_y[layer, half] = along_y[layer, half] + weights[3] * scaled
        for layer, half in along_y:
            inside = lane < EDGE if layer in (0, 16) else lane >= 3 * EDGE
            along_y[layer, half] = jnp.where(inside, along_y[layer, half], 0.0)
        along_x = {}
        for layer, face in ((0, 0), (15, 1), (16, 0), (31, 1)):
            rows = pl.ds(layer, 8, stride=EDGE)
            value = u0[q, pl.ds(PITCH + 8 + layer, 8, stride=PITCH), :]
            along_x[layer] = omega[q, face, rows, :] * weight_sum[q, rows, :] * value
        middle = along_x[15] - along_x[16]
        own_x = (along_x[0] + middle, along_x[31] - middle)
        for a in (0, 1):
            middle = along_y[15, a] - along_y[16, a]
            own_y = (along_y[0, a] + middle, along_y[31, a] - middle)
            for b in (0, 1):
                upper = sublane // 4 == b
                keep(OWN, q, 2 * a + b, jnp.where(upper, own_x[a], 0.0) + own_y[b])
                keep(ALONG_X, q, 2 * a + b, jnp.where(upper, along_x[31 * a], 0.0))
                keep(ALONG_Y, q, 2 * a + b, along_y[31 * a, b])
                keep(ALONG_Z, q, 2 * a + b, along_z[2 * a + b])

    cell_lane = lax.broadcasted_iota(jnp.int32, (1, LANES), 1)
    block_of = cell_lane // 8 % NB
    corner = (cell_lane // 4 % 2, cell_lane // 2 % 2, cell_lane % 2)
    wide = (LANES, LANES)
    from_depth = lax.broadcasted_iota(jnp.int32, wide, 0) % EDGE
    to_corner = lax.broadcasted_iota(jnp.int32, wide, 1) % 2
    by_half = (from_depth // (EDGE // 2) == to_corner).astype(jnp.float32)

    def one_at(level):
        return (from_depth == level).astype(jnp.float32)

    def take(value, choose):
        return jnp.dot(value, choose, precision=HIGHEST, preferred_element_type=jnp.float32)

    def sums_of(kind):
        groups = []
        for group in range(8):
            start = 8 * (8 * NB * kind + 8 * group)
            groups.append(sum(acc[pl.ds(start + i, 8, stride=8), :] for i in range(8)))
        return jnp.concatenate(groups, axis=0)

    def pick(value, s, block, place):
        rows = lax.broadcasted_iota(jnp.int32, (4 * NB, LANES), 0)
        part = value[4 * NB * s : 4 * NB * (s + 1), :]
        return jnp.sum(jnp.where(rows == 4 * block + place, part, 0.0), axis=0, keepdims=True)

    def other(axis):
        bit = block_of // 2**axis % 2
        return block_of + 2**axis * (1 - 2 * bit)


    def pack_all(field, volume):
        def body(s, carry):
            pack(0, s, field, volume, inner=False)
            return carry

        pack(0, odd_int, field, volume)
        lax.fori_loop(1 - odd_int, 2 - odd_int, body, 0)

    def arrive(phase, t):
        take_exchange(phase, t)
        gather_ghosts(phase, t)

    def to_volume(volume):
        def store(q, tile, part, value):
            volume[q, spot(tile, part), :] = value

        return store

    def to_source(q, tile, part, value):
        f_ref[q, flat(tile, part), :] = value

    settle(0, to_volume(u0))
    pack_all(0, u0)
    settle(1, to_volume(k_ref))
    pack_all(1, k_ref)
    pl.semaphore_wait(barrier, expected)
    start_exchange(0, 1)
    start_exchange(0, 0)

    @pl.when(p_split)
    def _():
        flag_copy.start()

    @pl.when(even)
    def _():
        moves[0].start()
        moves[1].start()

    settle(2, to_source)

    @pl.when(even)
    def _():
        moves[2].start()

    @pl.when(odd)
    def _():
        lax.fori_loop(NB, 2 * NB, weigh_inside, 0)
        for i in range(3):
            moves[i].wait_recv()

        def merge(p, carry):
            for tile in range(TILES):
                for part in range(PARTS):
                    for i, volume in enumerate((u0, k_ref)):
                        volume[p, spot(tile, part), :] += moved[i, p, flat(tile, part), :]
                    f_ref[p, flat(tile, part), :] += moved[2, p, flat(tile, part), :]
            return carry

        lax.fori_loop(0, NB, merge, 0)
        pack(0, 0, 0, u0, outer=False)
        pack(0, 0, 1, k_ref, outer=False)

    lax.fori_loop(0, NB, weigh_inside, 0)
    @pl.when(q_stays)
    def _():
        flag_copy.wait_recv()

    @pl.when(odd)
    def _():
        arrive(0, 1)
        lax.fori_loop(NB, 2 * NB, first_sweep, 0)
        pack(1, 1, 0, u1)
        start_exchange(1, 1)

    arrive(0, 0)
    lax.fori_loop(0, NB, first_sweep, 0)
    pack(1, 0, 0, u1)
    start_exchange(1, 0)

    cells = take(sums_of(SOURCE), by_half)
    source_sums = [pick(cells, s, block_of, cell_lane // 2 % 4) for s in (0, 1)]

    def final_copy(p):
        return pltpu.make_async_remote_copy(
            src_ref=final_send.at[p],
            dst_ref=final_recv.at[p],
            send_sem=last_send.at[p],
            recv_sem=last_recv.at[p],
            device_id=where_is(follower),
            device_id_type=MESH,
        )

    @pl.when(odd)
    def _():
        arrive(1, 1)

        def body(q, carry):
            second_sweep(q, True)

            @pl.when(both(has_q, q < NB + EARLY))
            def _():
                final_copy(q - NB).start()

            return carry

        lax.fori_loop(NB, 2 * NB, body, 0)

    arrive(1, 0)

    def body(q, carry):
        second_sweep(q, False)
        return carry

    lax.fori_loop(0, NB, body, 0)

    middle = take(jnp.concatenate([sums_of(kind) for kind in (OWN, ALONG_X, ALONG_Y)], axis=0), by_half)
    crossing = one_at(15) - one_at(16)
    low_cells, high_cells = one_at(0) + crossing, one_at(EDGE - 1) - crossing
    z_sums = sums_of(ALONG_Z)
    own_z = take(z_sums, jnp.where(to_corner == 0, low_cells, high_cells))
    face_z = take(z_sums, jnp.where(to_corner == 0, one_at(EDGE - 1), one_at(0)))
    size = 8 * NB
    own_sums = []
    for s in (0, 1):
        own_sums.append(pick(middle[:size] + own_z, s, block_of, cell_lane // 2 % 4))
        face_x = pick(middle[size : 2 * size], s, other(0), 2 * (1 - corner[0]) + corner[1])
        face_y = pick(middle[2 * size :], s, other(1), 2 * (1 - corner[1]) + corner[0])
        near_z = pick(face_z, s, other(2), cell_lane // 2 % 4)
        edge_sums[s] = jnp.where(sublane == 0, face_x, jnp.where(sublane == 1, face_y, near_z))
    start_exchange(2, 0)

    @pl.when(odd)
    def _():
        start_exchange(2, 1)

    @pl.when(q_stays)
    def _():
        for p in range(EARLY, MIDDLE):
            final_copy(p).start()

    take_exchange(2, 0)

    @pl.when(odd)
    def _():
        take_exchange(2, 1)

    totals = []
    for t in (0, 1):
        combined = jnp.zeros((8, LANES), jnp.float32)
        for p in range(NB):
            combined = jnp.where(lane // 8 % NB == p, flags[NB * t + p], combined)
        beyond = jnp.zeros((1, LANES), jnp.float32)
        for axis in range(3):
            row = slice(axis, axis + 1)
            outer, linked = [], []
            for side in (0, 1):
                face = 2 * axis + side
                total = 0.0
                for src in (0, 1):
                    pred = incoming[t, src, axis, side][1][2]
                    total = total + jnp.where(pred, got_sums[t, src, face, row, :], 0.0)
                outer.append(total)
                linked.append(combined[face : face + 1, :])
            split = jnp.where((p_split, q_stays)[t], split_sums[t, row, :], 0.0)
            inner = edge_sums[t, row, :] + split
            outer = jnp.where(corner[axis] == 0, outer[0], outer[1])
            linked = jnp.where(corner[axis] == 0, linked[0], linked[1])
            beside = jnp.where(block_of // 2**axis % 2 == corner[axis], outer, inner)
            beyond = beyond + jnp.where(linked > 0.5, beside, 0.0)
        held = block_of < onward if t else block_of >= jnp.where(even, lacking, 0)
        change = combined[6:7, :] * (beyond - own_sums[t])
        totals.append(jnp.where(held, source_sums[t] + change, 0.0))
    low_half = jnp.where(odd, totals[1], totals[0])
    total = jnp.where(cell_lane < 64, low_half, jnp.where(odd, totals[0], 0.0))
    mine[...] = jnp.broadcast_to(total * (EDGE // 2) ** (-1.5), (8, LANES))

    def sum_copy(step):
        return pltpu.make_async_remote_copy(
            src_ref=mine,
            dst_ref=all_sums.at[member],
            send_sem=sum_send.at[step],
            recv_sem=sum_recv.at[step],
            device_id={"member": (member + step) % members},
            device_id_type=MESH,
        )

    def on_copy(step):
        return pltpu.make_async_remote_copy(
            src_ref=mine,
            dst_ref=all_sums.at[members],
            send_sem=sum_send.at[members + step],
            recv_sem=sum_recv.at[0],
            device_id=(next_group, step),
            device_id_type=MESH,
        )

    for step in range(1, members):
        sum_copy(step).start()

    @pl.when(sends_last)
    def _():
        for step in range(members):
            on_copy(step).start()

    @pl.when(q_stays)
    def _():
        for p in range(MIDDLE, NB):
            final_copy(p).start()

    all_sums[member] = mine[...]
    for step in range(1, members):
        sum_copy(step).wait_send()
        sum_copy(step).wait_recv()

    @pl.when(sends_last)
    def _():
        for step in range(members):
            on_copy(step).wait_send()

    @pl.when(gets_last)
    def _():
        on_copy(0).wait_recv()

    correction = jnp.zeros((8 * NB, LANES), jnp.float32)
    for pair in range(members // 2):
        if pair == 0:
            before = jnp.where(gets_last, all_sums[members, 0:1, :], 0.0)
        else:
            before = all_sums[2 * pair - 1, 0:1, :]
        even_cells = all_sums[2 * pair, 0:1, :] + before
        vector = jnp.where(cell_lane < 64, even_cells, all_sums[2 * pair + 1, 0:1, :])
        correction = correction + inverse[0, :, LANES * pair : LANES * (pair + 1)] * vector
    rows_e[...] = jnp.broadcast_to(jnp.sum(correction, axis=1, keepdims=True), (8 * NB, LANES))

    def out_copy_of(p):
        return pltpu.make_async_copy(result.at[p], out_ref.at[p], out_sem.at[p])

    def finish(p, carry):
        @pl.when(p_split)
        def _():
            final_copy(p).wait_recv()

        for cell in range(4):
            first = pl.multiple_of(8 * p, 8) + 2 * cell
            lift = jnp.where(depth < EDGE // 2, rows_e[pl.ds(first, 1), :], rows_e[pl.ds(first + 1, 1), :])
            for part in (2 * (cell // 2), 2 * (cell // 2) + 1):
                for tile in range(4 * (cell % 2), 4 * (cell % 2) + 4):
                    arrived = jnp.where(p_split, final_recv[p, flat(tile, part), :], 0.0)
                    value = u0[p, spot(tile, part), :] + arrived + lift
                    result[p, 8 * part : 8 * part + 8, LANES * tile : LANES * (tile + 1)] = value
        out_copy_of(p).start()
        return carry

    lax.fori_loop(0, NB, finish, 0)
    for p in range(NB):
        out_copy_of(p).wait()

    for phase in range(3):
        end_exchange(phase)

    @pl.when(p_split)
    def _():
        flag_copy.wait_send()

    @pl.when(even)
    def _():
        for i in range(3):
            moves[i].wait_send()

    @pl.when(q_stays)
    def _():
        for p in range(NB):
            final_copy(p).wait_send()


def local(old_ids, field_old, source_old, kappa_old, refine, neighbors, coarse_inverse):
    members = lax.axis_size("member")
    devices = lax.axis_size(AXES)
    flat_shape = (NB, TILES * EDGE, LANES)
    both_shape = (2 * NB, TILES * EDGE, LANES)
    padded = (2 * NB, 10 * PITCH, LANES)
    shapes = [field_old.shape] * 3 + [padded] * 3 + [both_shape]
    shapes += [(2 * NB, 6, TILES * EDGE, LANES), both_shape, (3,) + flat_shape, (3,) + flat_shape]
    shapes += [flat_shape, flat_shape]
    shapes += [(2, 6, EDGE * n, LANES) for n in FIELDS]
    shapes += [(2, 2, 3, EDGE * n, LANES) for n in FIELDS]
    shapes += [(2, 2, 6, EDGE * n, LANES) for n in FIELDS]
    shapes += [(2, 3, EDGE * n, LANES) for n in FIELDS]
    shapes += [(2, 12, EDGE * n, LANES) for n in FIELDS]
    shapes += [(2 * NB, 8, LANES), (5 * 64 * NB, LANES), (8, LANES), (members + 1, 8, LANES)]
    shapes += [(8 * NB, LANES), (2, 8, LANES), (2, 2, 6, 8, LANES), (2, 8, LANES)]
    shapes += [(2, 4, EDGE * n, LANES) for n in FIELDS]
    dma = pltpu.SemaphoreType.DMA
    scratch = [pltpu.VMEM(s, jnp.float32) for s in shapes]
    scratch += [dma((3,)), dma((3,)), dma((3,)), dma((3, 2, 6, 2)), dma((3, 2, 2, 6))]
    scratch += [dma((3, 2)), dma((3, 2)), dma, dma, dma((NB,)), dma((NB,))]
    scratch += [dma((2 * members,)), dma((members,)), dma((NB,))]
    return pl.pallas_call(
        functools.partial(main_kernel, members, devices),
        out_shape=jax.ShapeDtypeStruct((NB, EDGE, FACE), jnp.float32),
        in_specs=[SM, SM, SM, VM, ANY, ANY, ANY],
        out_specs=ANY,
        scratch_shapes=scratch,
        compiler_params=pltpu.CompilerParams(
            collective_id=1, has_side_effects=True, vmem_limit_bytes=VMEM_LIMIT
        ),
    )(old_ids, neighbors, refine, coarse_inverse, field_old, source_old, kappa_old)


def solution(mesh):
    in_specs = (
        P(AXES),
        P(AXES, None, None),
        P(AXES, None, None),
        P(AXES, None, None),
        P(AXES),
        P(AXES, None),
        P("group", "member", None),
    )
    return jax.shard_map(
        local, mesh=mesh, in_specs=in_specs, out_specs=P(AXES, None, None), check_vma=False
    )
```

```python
import functools

import jax
import jax.numpy as jnp
from jax import lax
from jax.experimental import pallas as pl
from jax.experimental.pallas import tpu as pltpu
from jax.sharding import PartitionSpec as P

OMEGA = 0.8
AXES = ("group", "member")
NB, EDGE, FACE, LANES = 8, 32, 1024, 128
TILES, PARTS, PITCH = 8, 4, 48
HIGHEST = lax.Precision.HIGHEST
VMEM_LIMIT = 60 * 2**20
VM = pl.BlockSpec(memory_space=pltpu.VMEM)
ANY = pl.BlockSpec(memory_space=pl.ANY)
SM = pl.BlockSpec(memory_space=pltpu.SMEM)
MESH = pl.DeviceIdType.MESH
FIELDS = (2, 1)
EARLY, MIDDLE = 4, 6
OWN, ALONG_X, ALONG_Y, ALONG_Z, SOURCE = range(5)


def roll(value, steps):
    return pltpu.roll(value, steps % LANES, 1)


def spot(tile, part):
    return slice(PITCH * (tile + 1) + 8 + 8 * part, PITCH * (tile + 1) + 16 + 8 * part)


def flat(tile, part):
    return slice(EDGE * tile + 8 * part, EDGE * tile + 8 * part + 8)


def blocks_of(axis, side):
    return [b for b in range(NB) if (b >> axis) % 2 == side]


def octet_neighbors(octet, devices):
    nbits = devices.bit_length() - 1
    bits = [octet // 2**i % 2 for i in range(nbits)]
    result = []
    for axis in range(3):
        own = [i for i in range(nbits) if i % 3 == axis]
        extent = 2 ** len(own)
        coord = sum(bits[i] * 2**n for n, i in enumerate(own))
        base = octet - sum(bits[i] * 2**i for i in own)
        pair = []
        for step in (-1, 1):
            moved = coord + step
            inside = jnp.logical_and(moved >= 0, moved < extent)
            clipped = jnp.clip(moved, 0, extent - 1)
            index = base + sum(clipped // 2**n % 2 * 2**i for n, i in enumerate(own))
            pair.append((inside, index))
        result.append(pair)
    return result


def main_kernel(members, devices, old_ids, nbrs, refine, inverse, u_old, f_old, k_old, out_ref, *scratch):
    olds = scratch[0:3]
    u0, u1, k_ref, f_ref, omega, weight_sum, staged, moved, final_send, final_recv = scratch[3:13]
    send_out, own_in, recv_out, recv_in, ghosts = [scratch[13 + 2 * i : 15 + 2 * i] for i in range(5)]
    flags, acc, mine, all_sums, rows_e, edge_sums, got_sums, split_sums = scratch[23:31]
    edges = scratch[31:33]
    result, out_sem = olds[2].at[pl.ds(0, NB)], scratch[46]
    in_sem, move_send, move_recv, out_send, out_recv, inner_send, inner_recv = scratch[33:40]
    flag_send, flag_recv, last_send, last_recv, sum_send, sum_recv = scratch[40:46]

    group, member = lax.axis_index("group"), lax.axis_index("member")
    here = group * members + member
    odd = here % 2 == 1
    even = here % 2 == 0
    odd_int = here % 2
    has_q = here < devices - 1
    q_stays = jnp.logical_and(odd, has_q)
    p_split = jnp.logical_and(even, here > 0)
    around = [octet_neighbors(here, devices), octet_neighbors(here + 1, devices)]
    lane = lax.broadcasted_iota(jnp.int32, (8, LANES), 1)
    depth = lane % EDGE

    def where_is(index):
        return (index // members, index % members)

    loads = [
        pltpu.make_async_copy(ref, olds[i], in_sem.at[i]) for i, ref in enumerate((u_old, k_old, f_old))
    ]
    loads[0].start()

    def both(*preds):
        result = preds[0]
        for pred in preds[1:]:
            result = jnp.logical_and(result, pred)
        return result

    outgoing, incoming = {}, {}
    for s in (0, 1):
        for axis in (2, 1, 0):
            for side in (0, 1):
                inside, index = around[s][axis][side]
                stays = inside if s == 0 else both(inside, q_stays)
                holder = both(index % 2 == 0, index > 0)
                for t in (0, 1):
                    target = index if t == 0 else jnp.maximum(index - 1, 0)
                    pred = stays if t == 0 else both(stays, holder)
                    outgoing[s, axis, side, t] = (target, pred)
                receives = inside if s == 0 else both(inside, q_stays)
                for src in (0, 1):
                    source = index if src == 0 else jnp.maximum(index - 1, 0)
                    pred = receives if src == 0 else both(receives, holder)
                    incoming[s, src, axis, side] = (source, pred)

    for b in range(NB):
        flags[NB + b] = jnp.ones((8, LANES), jnp.float32)
    barrier = pltpu.get_barrier_semaphore()
    expected = jnp.int32(members - 1)
    for step in range(1, members):
        pl.semaphore_signal(
            barrier, inc=1, device_id={"member": (member + step) % members}, device_id_type=MESH
        )
    for target, pred in outgoing.values():
        expected = expected + both(pred, target // members != group).astype(jnp.int32)
    for source, pred in incoming.values():

        @pl.when(both(pred, source // members != group))
        def _():
            pl.semaphore_signal(barrier, inc=1, device_id=where_is(source), device_id_type=MESH)

    last = member == members - 1
    sends_last = both(last, has_q)
    gets_last = group > 0
    next_group = jnp.minimum(group + 1, devices // members - 1)
    prev_last = jnp.maximum(group * members - 1, 0)
    expected = expected + jnp.where(sends_last, members, 0)

    @pl.when(gets_last)
    def _():
        pl.semaphore_signal(barrier, inc=1, device_id=where_is(prev_last), device_id_type=MESH)

    first_in_group = both(member == 0, gets_last)
    expected = expected + first_in_group.astype(jnp.int32)

    @pl.when(sends_last)
    def _():
        pl.semaphore_signal(barrier, inc=1, device_id=(next_group, 0), device_id_type=MESH)

    kept, onward = jnp.int32(0), jnp.int32(0)
    for slot in range(2 * NB):
        index = old_ids[slot]
        kept = kept + both(index >= here * NB, index < here * NB + NB).astype(jnp.int32)
        onward = onward + (index >= here * NB + NB).astype(jnp.int32)
    kept = jnp.minimum(kept, NB)
    lacking = NB - kept

    for b in range(NB):
        for face in range(6):
            has = jnp.where(nbrs[b, face] >= 0, 1.0, 0.0).astype(jnp.float32)
            flags[b, face : face + 1, :] = jnp.full((1, LANES), has, jnp.float32)
        half_scale = 0.5 + 0.5 * refine[b].astype(jnp.float32)
        flags[b, 6:7, :] = jnp.full((1, LANES), half_scale, jnp.float32)
        flags[b, 7:8, :] = 1.0 / jnp.full((1, LANES), half_scale, jnp.float32)

    def settle(i, store):
        loads[i].wait()
        if i < 2:
            loads[i + 1].start()

        def own(p, carry):
            slot = jnp.maximum(p - lacking, 0)
            for tile in range(TILES):
                for part in range(PARTS):
                    value = olds[i][slot, 8 * part : 8 * part + 8, LANES * tile : LANES * (tile + 1)]
                    store(p, tile, part, jnp.where(p >= lacking, value, 0.0))
            return carry

        def following(p, carry):
            for tile in range(TILES):
                for part in range(PARTS):
                    value = olds[i][kept + p, 8 * part : 8 * part + 8, LANES * tile : LANES * (tile + 1)]
                    value = jnp.where(p < onward, value, 0.0)
                    store(NB + p, tile, part, value)
                    staged[i, p, flat(tile, part), :] = value
            return carry

        lax.fori_loop(0, NB, own, 0)
        lax.fori_loop(0, NB, following, 0)

    def pack(phase, s, field, volume, outer=True, inner=True):
        rows = EDGE * field

        def put(axis, side, bit, start, value):
            here_rows = pl.ds(rows + start, 8)
            if side == bit:
                send_out[phase][s, 2 * axis + side, here_rows, :] = value
            else:
                own_in[phase][s, bit, 3 * 0 + axis, here_rows, :] = value

        def wanted(side, bit):
            return outer if side == bit else inner

        for bit in (0, 1):
            for side in (0, 1):
                if not wanted(side, bit):
                    continue
                for j, b in enumerate(blocks_of(0, bit)):
                    line = volume[NB * s + b, pl.ds(PITCH + 8 + 31 * side, 8, stride=PITCH), :]
                    put(0, side, bit, 8 * j, line)
                for part in range(PARTS):
                    packed = jnp.zeros((8, LANES), jnp.float32)
                    for j, b in enumerate(blocks_of(1, bit)):
                        piece = volume[NB * s + b, spot(7 * side, part), :]
                        packed = jnp.where(lane // EDGE == j, roll(piece, EDGE * (j - 3 * side)), packed)
                    put(1, side, bit, 8 * part, packed)
            for quad in range(4):
                packed = [jnp.zeros((8, LANES), jnp.float32) for _ in (0, 1)]
                for half in (0, 1):
                    for j, b in enumerate(blocks_of(2, bit)):
                        for part in range(PARTS):
                            slot = 8 * j + 2 * part + half
                            piece = roll(volume[NB * s + b, spot(quad + 4 * half, part), :], slot)
                            for side in (0, 1):
                                if wanted(side, bit):
                                    packed[side] = jnp.where(
                                        depth == (slot + 31 * side) % EDGE, piece, packed[side]
                                    )
                for side in (0, 1):
                    if wanted(side, bit):
                        put(2, side, bit, 8 * quad, packed[side])

    def out_copy(phase, s, axis, side, t, target):
        face = 2 * axis + 1 - side
        if phase == 2:
            source, place = edge_sums.at[s], got_sums.at[t, s, face]
        else:
            source, place = send_out[phase].at[s, 2 * axis + side], recv_out[phase].at[t, s, face]
        return pltpu.make_async_remote_copy(
            src_ref=source,
            dst_ref=place,
            send_sem=out_send.at[phase, s, 2 * axis + side, t],
            recv_sem=out_recv.at[phase, t, s, face],
            device_id=where_is(target),
            device_id_type=MESH,
        )

    follower = jnp.minimum(here + 1, devices - 1)
    leader = jnp.maximum(here - 1, 0)

    def inner_copy(phase, s):
        if phase == 2:
            source, place = edge_sums.at[s], split_sums.at[1 - s]
        else:
            source, place = own_in[phase].at[s, 1 - s], recv_in[phase].at[1 - s]
        return pltpu.make_async_remote_copy(
            src_ref=source,
            dst_ref=place,
            send_sem=inner_send.at[phase, s],
            recv_sem=inner_recv.at[phase, 1 - s],
            device_id=where_is(follower if s else leader),
            device_id_type=MESH,
        )

    flag_copy = pltpu.make_async_remote_copy(
        src_ref=flags.at[pl.ds(0, NB)],
        dst_ref=flags.at[pl.ds(NB, NB)],
        send_sem=flag_send,
        recv_sem=flag_recv,
        device_id=where_is(leader),
        device_id_type=MESH,
    )
    moves = [
        pltpu.make_async_remote_copy(
            src_ref=staged.at[i],
            dst_ref=moved.at[i],
            send_sem=move_send.at[i],
            recv_sem=move_recv.at[i],
            device_id=where_is(follower),
            device_id_type=MESH,
        )
        for i in range(3)
    ]

    def start_exchange(phase, which):
        @pl.when((p_split, q_stays)[which])
        def _():
            inner_copy(phase, which).start()

        for (s, axis, side, t), (target, pred) in outgoing.items():
            if s == which:

                @pl.when(pred)
                def _():
                    out_copy(phase, s, axis, side, t, target).start()

    def take_exchange(phase, which):
        for (t, src, axis, side), (source, pred) in incoming.items():
            if t == which:

                @pl.when(pred)
                def _():
                    out_copy(phase, src, axis, 1 - side, t, source).wait_recv()

        @pl.when((p_split, q_stays)[which])
        def _():
            inner_copy(phase, 1 - which).wait_recv()

    def end_exchange(phase):
        for (s, axis, side, t), (target, pred) in outgoing.items():

            @pl.when(pred)
            def _():
                out_copy(phase, s, axis, side, t, target).wait_send()

        for s, split in enumerate((p_split, q_stays)):

            @pl.when(split)
            def _():
                inner_copy(phase, s).wait_send()

    def gather_ghosts(phase, t):
        split = (p_split, q_stays)[t]
        for axis in range(3):
            for side in (0, 1):
                face = 2 * axis + side
                total = 0.0
                for src in (0, 1):
                    pred = incoming[t, src, axis, side][1]
                    total = total + jnp.where(pred, recv_out[phase][t, src, face], 0.0)
                ghosts[phase][t, face] = total
                total = own_in[phase][t, side, axis]
                if side == t:
                    total = total + jnp.where(split, recv_in[phase][t, axis], 0.0)
                ghosts[phase][t, 6 + face] = total
        for bit in (0, 1):
            low, high = (4 if bit == 0 else 10), (5 if bit == 1 else 11)
            for chunk in range(4 * FIELDS[phase]):
                rows = slice(8 * chunk, 8 * chunk + 8)
                first = ghosts[phase][t, low, rows, :]
                second = roll(ghosts[phase][t, high, rows, :], 62)
                for half in (0, 1):
                    both_ends = jnp.where(depth % 2 != half, first, second)
                    edges[phase][t, 2 * bit + half, rows, :] = both_ends

    def fill(phase, q, field, volume, mirror):
        s, p = q // NB, q % NB
        rows = EDGE * field
        js = (p // 2, p % 2 + p // 4 * 2, p % 4)
        for side in (0, 1):
            kind = [jnp.where((p // 2**axis) % 2 == side, 0, 6) for axis in range(2)]
            ghost = ghosts[phase][s, kind[0] + side, pl.ds(pl.multiple_of(rows + 8 * js[0], 8), 8), :]
            has = flags[q, side : side + 1, :] > 0.5
            if mirror:
                spare = volume[q, pl.ds(PITCH + 8 + 31 * side, 8, stride=PITCH), :]
            else:
                spare = jnp.zeros_like(ghost)
            volume[q, pl.ds(PITCH + 7 + 33 * side, 8, stride=PITCH), :] = jnp.where(has, ghost, spare)
            has = flags[q, 2 + side : 3 + side, :] > 0.5
            for part in range(PARTS):
                ghost = ghosts[phase][s, kind[1] + 2 + side, rows + 8 * part : rows + 8 * part + 8, :]
                steps = EDGE * (3 - js[1]) if side == 0 else EDGE * ((4 - js[1]) % 4)
                ghost = pltpu.roll(ghost, steps, 1)
                if mirror:
                    spare = roll(volume[q, spot(7 * side, part), :], 96 - 64 * side)
                else:
                    spare = jnp.zeros_like(ghost)
                volume[q, spot(9 * side - 1, part), :] = jnp.where(has, ghost, spare)

    def z_edge(phase, q, field, tile, part, spare):
        s, p = q // NB, q % NB
        start = EDGE * field + 8 * (tile % 4)
        sheet = edges[phase][s, 2 * (p // 4) + tile // 4, start : start + 8, :]
        ghost = pltpu.roll(sheet, 97 - 2 * part - tile // 4 - 8 * (p % 4), 1)
        has = jnp.where(depth < EDGE // 2, flags[q, 4:5, :], flags[q, 5:6, :]) > 0.5
        return jnp.where(has, ghost, spare)

    def stencil(phase, q, volume, part):
        tiles = [volume[q, spot(t, part), :] for t in range(-1, TILES + 1)]
        down = [roll(t, EDGE) for t in tiles[:-1]]
        up = [None] + [roll(t, -EDGE) for t in tiles[1:]]
        for tile in range(TILES):
            value = tiles[tile + 1]
            top = PITCH * (tile + 1) + 8 + 8 * part
            x_minus = volume[q, top - 1 : top + 7, :]
            x_plus = volume[q, top + 1 : top + 9, :]
            y_minus = jnp.where(lane >= EDGE, down[tile + 1], down[tile])
            y_plus = jnp.where(lane < 3 * EDGE, up[tile + 1], up[tile + 2])
            edge = z_edge(phase, q, 0, tile, part, 0.0)
            z_minus = jnp.where(depth == 0, edge, roll(value, 1))
            z_plus = jnp.where(depth == EDGE - 1, edge, roll(value, -1))
            yield tile, value, (x_minus, x_plus, y_minus, y_plus, z_minus, z_plus)

    def weigh_inside(q, carry):
        for part in range(PARTS):
            tiles = [k_ref[q, spot(t, part), :] for t in range(TILES)]
            down = [roll(t, EDGE) for t in tiles]
            up = [roll(t, -EDGE) for t in tiles]
            for tile in range(TILES):
                place, k = flat(tile, part), tiles[tile]
                before, after = down[max(tile - 1, 0)], up[min(tile + 1, TILES - 1)]
                omega[q, 2, place, :] = k + jnp.where(lane >= EDGE, down[tile], before)
                omega[q, 3, place, :] = k + jnp.where(lane < 3 * EDGE, up[tile], after)
                omega[q, 4, place, :] = k + roll(k, 1)
                omega[q, 5, place, :] = k + roll(k, -1)
        return carry

    def weigh(q, part):
        before = roll(k_ref[q, spot(-1, part), :], EDGE)
        after = roll(k_ref[q, spot(TILES, part), :], -EDGE)
        for tile in range(TILES):
            place, k = flat(tile, part), k_ref[q, spot(tile, part), :]
            top = PITCH * (tile + 1) + 8 + 8 * part
            around_k = [k_ref[q, top - 1 : top + 7, :], k_ref[q, top + 1 : top + 9, :]]
            inside = [omega[q, face, place, :] for face in range(2, 6)]
            if tile == 0:
                inside[0] = jnp.where(lane >= EDGE, inside[0], k + before)
            if tile == TILES - 1:
                inside[1] = jnp.where(lane < 3 * EDGE, inside[1], k + after)
            edge = k + z_edge(0, q, 1, tile, part, k)
            inside[2] = jnp.where(depth == 0, edge, inside[2])
            inside[3] = jnp.where(depth == EDGE - 1, edge, inside[3])
            yield [k + beside for beside in around_k] + inside

    def valid(q):
        low = jnp.where(even, lacking, 0)
        return both(q >= low, q < NB + onward)

    def keep(kind, q, cell, value):
        acc[pl.ds(pl.multiple_of(8 * (8 * NB * kind + 4 * q + cell), 8), 8), :] = value

    def first_sweep(q, carry):
        fill(0, q, 0, u0, False)
        fill(0, q, 1, k_ref, True)
        holds = valid(q)
        totals = [jnp.zeros((8, LANES), jnp.float32) for _ in range(4)]
        for part in range(PARTS):
            for (tile, u, u_beside), weights in zip(stencil(0, q, u0, part), weigh(q, part)):
                total = sum(weights[1:], weights[0])
                scale = jnp.where(holds, OMEGA / total, 0.0)
                place = flat(tile, part)
                weight_sum[q, place, :] = total * (1.0 / OMEGA)
                right = f_ref[q, place, :]
                cell = part // 2 * 2 + tile // 4
                totals[cell] = totals[cell] + right
                gain = right * scale * flags[q, 7:8, :]
                f_ref[q, place, :] = gain
                new = (1.0 - OMEGA) * u + gain
                for face in range(6):
                    weight = weights[face] * scale
                    omega[q, face, place, :] = weight
                    new = new + weight * u_beside[face]
                u1[q, spot(tile, part), :] = new
        for cell in range(4):
            keep(SOURCE, q, cell, totals[cell])
        return carry

    sublane = lax.broadcasted_iota(jnp.int32, (8, LANES), 0)

    def second_sweep(q, send):
        fill(1, q, 0, u1, False)
        zero = jnp.zeros((8, LANES), jnp.float32)
        along_z = [zero] * 4
        along_y = {(layer, half): zero for layer in (0, 15, 16, 31) for half in (0, 1)}
        for part in range(PARTS):
            for tile, u, beside in stencil(1, q, u1, part):
                place = flat(tile, part)
                new = (1.0 - OMEGA) * u + f_ref[q, place, :]
                weights = [omega[q, face, place, :] for face in range(6)]
                for face in range(6):
                    new = new + weights[face] * beside[face]
                u0[q, spot(tile, part), :] = new
                if send:
                    final_send[q - NB, place, :] = new
                scaled = new * weight_sum[q, place, :]
                half, cell = part // 2, part // 2 * 2 + tile // 4
                outward = jnp.where(depth % (EDGE // 2) == EDGE // 2 - 1, weights[5], weights[4])
                along_z[cell] = along_z[cell] + outward * scaled
                if tile in (0, 4):
                    layer = 4 * tile
                    along_y[layer, half] = along_y[layer, half] + weights[2] * scaled
                if tile in (3, 7):
                    layer = 4 * tile + 3
                    along_y[layer, half] = along_y[layer, half] + weights[3] * scaled
        for layer, half in along_y:
            inside = lane < EDGE if layer in (0, 16) else lane >= 3 * EDGE
            along_y[layer, half] = jnp.where(inside, along_y[layer, half], 0.0)
        along_x = {}
        for layer, face in ((0, 0), (15, 1), (16, 0), (31, 1)):
            rows = pl.ds(layer, 8, stride=EDGE)
            value = u0[q, pl.ds(PITCH + 8 + layer, 8, stride=PITCH), :]
            along_x[layer] = omega[q, face, rows, :] * weight_sum[q, rows, :] * value
        middle = along_x[15] - along_x[16]
        own_x = (along_x[0] + middle, along_x[31] - middle)
        for a in (0, 1):
            middle = along_y[15, a] - along_y[16, a]
            own_y = (along_y[0, a] + middle, along_y[31, a] - middle)
            for b in (0, 1):
                upper = sublane // 4 == b
                keep(OWN, q, 2 * a + b, jnp.where(upper, own_x[a], 0.0) + own_y[b])
                keep(ALONG_X, q, 2 * a + b, jnp.where(upper, along_x[31 * a], 0.0))
                keep(ALONG_Y, q, 2 * a + b, along_y[31 * a, b])
                keep(ALONG_Z, q, 2 * a + b, along_z[2 * a + b])

    cell_lane = lax.broadcasted_iota(jnp.int32, (1, LANES), 1)
    block_of = cell_lane // 8 % NB
    corner = (cell_lane // 4 % 2, cell_lane // 2 % 2, cell_lane % 2)
    wide = (LANES, LANES)
    from_depth = lax.broadcasted_iota(jnp.int32, wide, 0) % EDGE
    to_corner = lax.broadcasted_iota(jnp.int32, wide, 1) % 2
    by_half = (from_depth // (EDGE // 2) == to_corner).astype(jnp.float32)

    def one_at(level):
        return (from_depth == level).astype(jnp.float32)

    def take(value, choose):
        return jnp.dot(value, choose, precision=HIGHEST, preferred_element_type=jnp.float32)

    def sums_of(kind):
        groups = []
        for group in range(8):
            start = 8 * (8 * NB * kind + 8 * group)
            groups.append(sum(acc[pl.ds(start + i, 8, stride=8), :] for i in range(8)))
        return jnp.concatenate(groups, axis=0)

    def pick(value, s, block, place):
        rows = lax.broadcasted_iota(jnp.int32, (4 * NB, LANES), 0)
        part = value[4 * NB * s : 4 * NB * (s + 1), :]
        return jnp.sum(jnp.where(rows == 4 * block + place, part, 0.0), axis=0, keepdims=True)

    def other(axis):
        bit = block_of // 2**axis % 2
        return block_of + 2**axis * (1 - 2 * bit)


    def arrive(phase, t):
        take_exchange(phase, t)
        gather_ghosts(phase, t)

    def to_volume(volume):
        def store(q, tile, part, value):
            volume[q, spot(tile, part), :] = value

        return store

    def to_source(q, tile, part, value):
        f_ref[q, flat(tile, part), :] = value

    settle(0, to_volume(u0))
    pack(0, odd_int, 0, u0)
    settle(1, to_volume(k_ref))
    pack(0, odd_int, 1, k_ref)
    pl.semaphore_wait(barrier, expected)
    def merge(arrays):
        def body(p, carry):
            for tile in range(TILES):
                for part in range(PARTS):
                    for i, volume in arrays:
                        place = flat(tile, part) if i == 2 else spot(tile, part)
                        volume[p, place, :] += moved[i, p, flat(tile, part), :]
            return carry

        for i, _ in arrays:
            moves[i].wait_recv()
        lax.fori_loop(0, NB, body, 0)

    @pl.when(even)
    def _():
        start_exchange(0, 0)
        moves[0].start()
        moves[1].start()

        @pl.when(p_split)
        def _():
            flag_copy.start()

    @pl.when(odd)
    def _():
        start_exchange(0, 1)
        merge(((0, u0), (1, k_ref)))
        pack(0, 0, 0, u0)
        pack(0, 0, 1, k_ref)
        start_exchange(0, 0)

    settle(2, to_source)

    @pl.when(even)
    def _():
        moves[2].start()

    @pl.when(odd)
    def _():
        lax.fori_loop(NB, 2 * NB, weigh_inside, 0)

    lax.fori_loop(0, NB, weigh_inside, 0)

    @pl.when(odd)
    def _():
        merge(((2, f_ref),))

    @pl.when(q_stays)
    def _():
        flag_copy.wait_recv()

    @pl.when(odd)
    def _():
        arrive(0, 1)
        lax.fori_loop(NB, 2 * NB, first_sweep, 0)
        pack(1, 1, 0, u1)
        start_exchange(1, 1)

    arrive(0, 0)
    lax.fori_loop(0, NB, first_sweep, 0)
    pack(1, 0, 0, u1)
    start_exchange(1, 0)

    cells = take(sums_of(SOURCE), by_half)
    source_sums = [pick(cells, s, block_of, cell_lane // 2 % 4) for s in (0, 1)]

    def final_copy(p):
        return pltpu.make_async_remote_copy(
            src_ref=final_send.at[p],
            dst_ref=final_recv.at[p],
            send_sem=last_send.at[p],
            recv_sem=last_recv.at[p],
            device_id=where_is(follower),
            device_id_type=MESH,
        )

    @pl.when(odd)
    def _():
        arrive(1, 1)

        def body(q, carry):
            second_sweep(q, True)

            @pl.when(both(has_q, q < NB + EARLY))
            def _():
                final_copy(q - NB).start()

            return carry

        lax.fori_loop(NB, 2 * NB, body, 0)

    arrive(1, 0)

    def body(q, carry):
        second_sweep(q, False)
        return carry

    lax.fori_loop(0, NB, body, 0)

    middle = take(jnp.concatenate([sums_of(kind) for kind in (OWN, ALONG_X, ALONG_Y)], axis=0), by_half)
    crossing = one_at(15) - one_at(16)
    low_cells, high_cells = one_at(0) + crossing, one_at(EDGE - 1) - crossing
    z_sums = sums_of(ALONG_Z)
    own_z = take(z_sums, jnp.where(to_corner == 0, low_cells, high_cells))
    face_z = take(z_sums, jnp.where(to_corner == 0, one_at(EDGE - 1), one_at(0)))
    size = 8 * NB
    own_sums = []
    for s in (0, 1):
        own_sums.append(pick(middle[:size] + own_z, s, block_of, cell_lane // 2 % 4))
        face_x = pick(middle[size : 2 * size], s, other(0), 2 * (1 - corner[0]) + corner[1])
        face_y = pick(middle[2 * size :], s, other(1), 2 * (1 - corner[1]) + corner[0])
        near_z = pick(face_z, s, other(2), cell_lane // 2 % 4)
        edge_sums[s] = jnp.where(sublane == 0, face_x, jnp.where(sublane == 1, face_y, near_z))
    start_exchange(2, 0)

    @pl.when(odd)
    def _():
        start_exchange(2, 1)

    @pl.when(q_stays)
    def _():
        for p in range(EARLY, MIDDLE):
            final_copy(p).start()

    take_exchange(2, 0)

    @pl.when(odd)
    def _():
        take_exchange(2, 1)

    totals = []
    for t in (0, 1):
        combined = jnp.zeros((8, LANES), jnp.float32)
        for p in range(NB):
            combined = jnp.where(lane // 8 % NB == p, flags[NB * t + p], combined)
        beyond = jnp.zeros((1, LANES), jnp.float32)
        for axis in range(3):
            row = slice(axis, axis + 1)
            outer, linked = [], []
            for side in (0, 1):
                face = 2 * axis + side
                total = 0.0
                for src in (0, 1):
                    pred = incoming[t, src, axis, side][1]
                    total = total + jnp.where(pred, got_sums[t, src, face, row, :], 0.0)
                outer.append(total)
                linked.append(combined[face : face + 1, :])
            split = jnp.where((p_split, q_stays)[t], split_sums[t, row, :], 0.0)
            inner = edge_sums[t, row, :] + split
            outer = jnp.where(corner[axis] == 0, outer[0], outer[1])
            linked = jnp.where(corner[axis] == 0, linked[0], linked[1])
            beside = jnp.where(block_of // 2**axis % 2 == corner[axis], outer, inner)
            beyond = beyond + jnp.where(linked > 0.5, beside, 0.0)
        held = block_of < onward if t else block_of >= jnp.where(even, lacking, 0)
        change = combined[6:7, :] * (beyond - own_sums[t])
        totals.append(jnp.where(held, source_sums[t] + change, 0.0))
    low_half = jnp.where(odd, totals[1], totals[0])
    total = jnp.where(cell_lane < 64, low_half, jnp.where(odd, totals[0], 0.0))
    mine[...] = jnp.broadcast_to(total * (EDGE // 2) ** (-1.5), (8, LANES))

    def sum_copy(step):
        return pltpu.make_async_remote_copy(
            src_ref=mine,
            dst_ref=all_sums.at[member],
            send_sem=sum_send.at[step],
            recv_sem=sum_recv.at[step],
            device_id={"member": (member + step) % members},
            device_id_type=MESH,
        )

    def on_copy(step):
        return pltpu.make_async_remote_copy(
            src_ref=mine,
            dst_ref=all_sums.at[members],
            send_sem=sum_send.at[members + step],
            recv_sem=sum_recv.at[0],
            device_id=(next_group, step),
            device_id_type=MESH,
        )

    for step in range(1, members):
        sum_copy(step).start()

    @pl.when(sends_last)
    def _():
        for step in range(members):
            on_copy(step).start()

    @pl.when(q_stays)
    def _():
        for p in range(MIDDLE, NB):
            final_copy(p).start()

    all_sums[member] = mine[...]
    for step in range(1, members):
        sum_copy(step).wait_send()
        sum_copy(step).wait_recv()

    @pl.when(sends_last)
    def _():
        for step in range(members):
            on_copy(step).wait_send()

    @pl.when(gets_last)
    def _():
        on_copy(0).wait_recv()

    correction = jnp.zeros((8 * NB, LANES), jnp.float32)
    for pair in range(members // 2):
        if pair == 0:
            before = jnp.where(gets_last, all_sums[members, 0:1, :], 0.0)
        else:
            before = all_sums[2 * pair - 1, 0:1, :]
        even_cells = all_sums[2 * pair, 0:1, :] + before
        vector = jnp.where(cell_lane < 64, even_cells, all_sums[2 * pair + 1, 0:1, :])
        correction = correction + inverse[0, :, LANES * pair : LANES * (pair + 1)] * vector
    rows_e[...] = jnp.broadcast_to(jnp.sum(correction, axis=1, keepdims=True), (8 * NB, LANES))

    def out_copy_of(p):
        return pltpu.make_async_copy(result.at[p], out_ref.at[p], out_sem.at[p])

    def finish(p, carry):
        @pl.when(p_split)
        def _():
            final_copy(p).wait_recv()

        for cell in range(4):
            first = pl.multiple_of(8 * p, 8) + 2 * cell
            lift = jnp.where(depth < EDGE // 2, rows_e[pl.ds(first, 1), :], rows_e[pl.ds(first + 1, 1), :])
            for part in (2 * (cell // 2), 2 * (cell // 2) + 1):
                for tile in range(4 * (cell % 2), 4 * (cell % 2) + 4):
                    arrived = jnp.where(p_split, final_recv[p, flat(tile, part), :], 0.0)
                    value = u0[p, spot(tile, part), :] + arrived + lift
                    result[p, 8 * part : 8 * part + 8, LANES * tile : LANES * (tile + 1)] = value
        out_copy_of(p).start()
        return carry

    lax.fori_loop(0, NB, finish, 0)
    for p in range(NB):
        out_copy_of(p).wait()

    for phase in range(3):
        end_exchange(phase)

    @pl.when(p_split)
    def _():
        flag_copy.wait_send()

    @pl.when(even)
    def _():
        for i in range(3):
            moves[i].wait_send()

    @pl.when(q_stays)
    def _():
        for p in range(NB):
            final_copy(p).wait_send()


def local(old_ids, field_old, source_old, kappa_old, refine, neighbors, coarse_inverse):
    members = lax.axis_size("member")
    devices = lax.axis_size(AXES)
    flat_shape = (NB, TILES * EDGE, LANES)
    both_shape = (2 * NB, TILES * EDGE, LANES)
    padded = (2 * NB, 10 * PITCH, LANES)
    shapes = [field_old.shape] * 3 + [padded] * 3 + [both_shape]
    shapes += [(2 * NB, 6, TILES * EDGE, LANES), both_shape, (3,) + flat_shape, (3,) + flat_shape]
    shapes += [flat_shape, flat_shape]
    shapes += [(2, 6, EDGE * n, LANES) for n in FIELDS]
    shapes += [(2, 2, 3, EDGE * n, LANES) for n in FIELDS]
    shapes += [(2, 2, 6, EDGE * n, LANES) for n in FIELDS]
    shapes += [(2, 3, EDGE * n, LANES) for n in FIELDS]
    shapes += [(2, 12, EDGE * n, LANES) for n in FIELDS]
    shapes += [(2 * NB, 8, LANES), (5 * 64 * NB, LANES), (8, LANES), (members + 1, 8, LANES)]
    shapes += [(8 * NB, LANES), (2, 8, LANES), (2, 2, 6, 8, LANES), (2, 8, LANES)]
    shapes += [(2, 4, EDGE * n, LANES) for n in FIELDS]
    dma = pltpu.SemaphoreType.DMA
    scratch = [pltpu.VMEM(s, jnp.float32) for s in shapes]
    scratch += [dma((3,)), dma((3,)), dma((3,)), dma((3, 2, 6, 2)), dma((3, 2, 2, 6))]
    scratch += [dma((3, 2)), dma((3, 2)), dma, dma, dma((NB,)), dma((NB,))]
    scratch += [dma((2 * members,)), dma((members,)), dma((NB,))]
    return pl.pallas_call(
        functools.partial(main_kernel, members, devices),
        out_shape=jax.ShapeDtypeStruct((NB, EDGE, FACE), jnp.float32),
        in_specs=[SM, SM, SM, VM, ANY, ANY, ANY],
        out_specs=ANY,
        scratch_shapes=scratch,
        compiler_params=pltpu.CompilerParams(
            collective_id=1, has_side_effects=True, vmem_limit_bytes=VMEM_LIMIT
        ),
    )(old_ids, neighbors, refine, coarse_inverse, field_old, source_old, kappa_old)


def solution(mesh):
    in_specs = (
        P(AXES),
        P(AXES, None, None),
        P(AXES, None, None),
        P(AXES, None, None),
        P(AXES),
        P(AXES, None),
        P("group", "member", None),
    )
    return jax.shard_map(
        local, mesh=mesh, in_specs=in_specs, out_specs=P(AXES, None, None), check_vma=False
    )
```

```python
import functools

import jax
import jax.numpy as jnp
from jax import lax
from jax.experimental import pallas as pl
from jax.experimental.pallas import tpu as pltpu
from jax.sharding import PartitionSpec as P

OMEGA = 0.8
AXES = ("group", "member")
NB, EDGE, FACE, LANES = 8, 32, 1024, 128
TILES, PARTS, PITCH = 8, 4, 48
HIGHEST = lax.Precision.HIGHEST
VMEM_LIMIT = 60 * 2**20
VM = pl.BlockSpec(memory_space=pltpu.VMEM)
ANY = pl.BlockSpec(memory_space=pl.ANY)
SM = pl.BlockSpec(memory_space=pltpu.SMEM)
MESH = pl.DeviceIdType.MESH
FIELDS = (2, 1)
EARLY, MIDDLE = 4, 7
OWN, ALONG_X, ALONG_Y, ALONG_Z, SOURCE = range(5)


def roll(value, steps):
    return pltpu.roll(value, steps % LANES, 1)


def spot(tile, part):
    return slice(PITCH * (tile + 1) + 8 + 8 * part, PITCH * (tile + 1) + 16 + 8 * part)


def flat(tile, part):
    return slice(EDGE * tile + 8 * part, EDGE * tile + 8 * part + 8)


def blocks_of(axis, side):
    return [b for b in range(NB) if (b >> axis) % 2 == side]


def octet_neighbors(octet, devices):
    nbits = devices.bit_length() - 1
    bits = [octet // 2**i % 2 for i in range(nbits)]
    result = []
    for axis in range(3):
        own = [i for i in range(nbits) if i % 3 == axis]
        extent = 2 ** len(own)
        coord = sum(bits[i] * 2**n for n, i in enumerate(own))
        base = octet - sum(bits[i] * 2**i for i in own)
        pair = []
        for step in (-1, 1):
            moved = coord + step
            inside = jnp.logical_and(moved >= 0, moved < extent)
            clipped = jnp.clip(moved, 0, extent - 1)
            index = base + sum(clipped // 2**n % 2 * 2**i for n, i in enumerate(own))
            pair.append((inside, index))
        result.append(pair)
    return result


def main_kernel(members, devices, old_ids, nbrs, refine, inverse, u_old, f_old, k_old, out_ref, *scratch):
    olds = scratch[0:3]
    u0, u1, k_ref, f_ref, omega, weight_sum, staged, moved, final_send, final_recv = scratch[3:13]
    send_out, own_in, recv_out, recv_in, ghosts = [scratch[13 + 2 * i : 15 + 2 * i] for i in range(5)]
    flags, acc, mine, all_sums, rows_e, edge_sums, got_sums, split_sums = scratch[23:31]
    edges = scratch[31:33]
    result, out_sem = olds[2].at[pl.ds(0, NB)], scratch[46]
    in_sem, move_send, move_recv, out_send, out_recv, inner_send, inner_recv = scratch[33:40]
    flag_send, flag_recv, last_send, last_recv, sum_send, sum_recv = scratch[40:46]

    group, member = lax.axis_index("group"), lax.axis_index("member")
    here = group * members + member
    odd = here % 2 == 1
    even = here % 2 == 0
    odd_int = here % 2
    has_q = here < devices - 1
    q_stays = jnp.logical_and(odd, has_q)
    p_split = jnp.logical_and(even, here > 0)
    around = [octet_neighbors(here, devices), octet_neighbors(here + 1, devices)]
    lane = lax.broadcasted_iota(jnp.int32, (8, LANES), 1)
    depth = lane % EDGE

    def where_is(index):
        return (index // members, index % members)

    loads = [
        pltpu.make_async_copy(ref, olds[i], in_sem.at[i]) for i, ref in enumerate((u_old, k_old, f_old))
    ]
    loads[0].start()
    loads[1].start()

    def both(*preds):
        result = preds[0]
        for pred in preds[1:]:
            result = jnp.logical_and(result, pred)
        return result

    outgoing, incoming = {}, {}
    for s in (0, 1):
        for axis in (2, 1, 0):
            for side in (0, 1):
                inside, index = around[s][axis][side]
                stays = inside if s == 0 else both(inside, q_stays)
                holder = both(index % 2 == 0, index > 0)
                for t in (0, 1):
                    target = index if t == 0 else jnp.maximum(index - 1, 0)
                    pred = stays if t == 0 else both(stays, holder)
                    outgoing[s, axis, side, t] = (target, pred)
                receives = inside if s == 0 else both(inside, q_stays)
                for src in (0, 1):
                    source = index if src == 0 else jnp.maximum(index - 1, 0)
                    pred = receives if src == 0 else both(receives, holder)
                    incoming[s, src, axis, side] = (source, pred)

    for b in range(NB):
        flags[NB + b] = jnp.ones((8, LANES), jnp.float32)
    barrier = pltpu.get_barrier_semaphore()
    expected = jnp.int32(members - 1)
    for step in range(1, members):
        pl.semaphore_signal(
            barrier, inc=1, device_id={"member": (member + step) % members}, device_id_type=MESH
        )
    for target, pred in outgoing.values():
        expected = expected + both(pred, target // members != group).astype(jnp.int32)
    for source, pred in incoming.values():

        @pl.when(both(pred, source // members != group))
        def _():
            pl.semaphore_signal(barrier, inc=1, device_id=where_is(source), device_id_type=MESH)

    last = member == members - 1
    sends_last = both(last, has_q)
    gets_last = group > 0
    next_group = jnp.minimum(group + 1, devices // members - 1)
    prev_last = jnp.maximum(group * members - 1, 0)
    expected = expected + jnp.where(sends_last, members, 0)

    @pl.when(gets_last)
    def _():
        pl.semaphore_signal(barrier, inc=1, device_id=where_is(prev_last), device_id_type=MESH)

    first_in_group = both(member == 0, gets_last)
    expected = expected + first_in_group.astype(jnp.int32)

    @pl.when(sends_last)
    def _():
        pl.semaphore_signal(barrier, inc=1, device_id=(next_group, 0), device_id_type=MESH)

    kept, onward = jnp.int32(0), jnp.int32(0)
    for slot in range(2 * NB):
        index = old_ids[slot]
        kept = kept + both(index >= here * NB, index < here * NB + NB).astype(jnp.int32)
        onward = onward + (index >= here * NB + NB).astype(jnp.int32)
    kept = jnp.minimum(kept, NB)
    lacking = NB - kept

    for b in range(NB):
        for face in range(6):
            has = jnp.where(nbrs[b, face] >= 0, 1.0, 0.0).astype(jnp.float32)
            flags[b, face : face + 1, :] = jnp.full((1, LANES), has, jnp.float32)
        half_scale = 0.5 + 0.5 * refine[b].astype(jnp.float32)
        flags[b, 6:7, :] = jnp.full((1, LANES), half_scale, jnp.float32)
        flags[b, 7:8, :] = 1.0 / jnp.full((1, LANES), half_scale, jnp.float32)

    def settle(i, store):
        loads[i].wait()
        if i == 1:
            loads[2].start()

        def own(p, carry):
            slot = jnp.maximum(p - lacking, 0)
            for tile in range(TILES):
                for part in range(PARTS):
                    value = olds[i][slot, 8 * part : 8 * part + 8, LANES * tile : LANES * (tile + 1)]
                    store(p, tile, part, jnp.where(p >= lacking, value, 0.0))
            return carry

        def following(p, carry):
            for tile in range(TILES):
                for part in range(PARTS):
                    value = olds[i][kept + p, 8 * part : 8 * part + 8, LANES * tile : LANES * (tile + 1)]
                    value = jnp.where(p < onward, value, 0.0)
                    store(NB + p, tile, part, value)
                    staged[i, p, flat(tile, part), :] = value
            return carry

        lax.fori_loop(0, NB, own, 0)
        lax.fori_loop(0, NB, following, 0)

    def pack(phase, s, field, volume, outer=True, inner=True):
        rows = EDGE * field

        def put(axis, side, bit, start, value):
            here_rows = pl.ds(rows + start, 8)
            if side == bit:
                send_out[phase][s, 2 * axis + side, here_rows, :] = value
            else:
                own_in[phase][s, bit, 3 * 0 + axis, here_rows, :] = value

        def wanted(side, bit):
            return outer if side == bit else inner

        for bit in (0, 1):
            for side in (0, 1):
                if not wanted(side, bit):
                    continue
                for j, b in enumerate(blocks_of(0, bit)):
                    line = volume[NB * s + b, pl.ds(PITCH + 8 + 31 * side, 8, stride=PITCH), :]
                    put(0, side, bit, 8 * j, line)
                for part in range(PARTS):
                    packed = jnp.zeros((8, LANES), jnp.float32)
                    for j, b in enumerate(blocks_of(1, bit)):
                        piece = volume[NB * s + b, spot(7 * side, part), :]
                        packed = jnp.where(lane // EDGE == j, roll(piece, EDGE * (j - 3 * side)), packed)
                    put(1, side, bit, 8 * part, packed)
            for quad in range(4):
                packed = [jnp.zeros((8, LANES), jnp.float32) for _ in (0, 1)]
                for half in (0, 1):
                    for j, b in enumerate(blocks_of(2, bit)):
                        for part in range(PARTS):
                            slot = 8 * j + 2 * part + half
                            piece = roll(volume[NB * s + b, spot(quad + 4 * half, part), :], slot)
                            for side in (0, 1):
                                if wanted(side, bit):
                                    packed[side] = jnp.where(
                                        depth == (slot + 31 * side) % EDGE, piece, packed[side]
                                    )
                for side in (0, 1):
                    if wanted(side, bit):
                        put(2, side, bit, 8 * quad, packed[side])

    def out_copy(phase, s, axis, side, t, target):
        face = 2 * axis + 1 - side
        if phase == 2:
            source, place = edge_sums.at[s], got_sums.at[t, s, face]
        else:
            source, place = send_out[phase].at[s, 2 * axis + side], recv_out[phase].at[t, s, face]
        return pltpu.make_async_remote_copy(
            src_ref=source,
            dst_ref=place,
            send_sem=out_send.at[phase, s, 2 * axis + side, t],
            recv_sem=out_recv.at[phase, t, s, face],
            device_id=where_is(target),
            device_id_type=MESH,
        )

    follower = jnp.minimum(here + 1, devices - 1)
    leader = jnp.maximum(here - 1, 0)

    def inner_copy(phase, s):
        if phase == 2:
            source, place = edge_sums.at[s], split_sums.at[1 - s]
        else:
            source, place = own_in[phase].at[s, 1 - s], recv_in[phase].at[1 - s]
        return pltpu.make_async_remote_copy(
            src_ref=source,
            dst_ref=place,
            send_sem=inner_send.at[phase, s],
            recv_sem=inner_recv.at[phase, 1 - s],
            device_id=where_is(follower if s else leader),
            device_id_type=MESH,
        )

    flag_copy = pltpu.make_async_remote_copy(
        src_ref=flags.at[pl.ds(0, NB)],
        dst_ref=flags.at[pl.ds(NB, NB)],
        send_sem=flag_send,
        recv_sem=flag_recv,
        device_id=where_is(leader),
        device_id_type=MESH,
    )
    moves = [
        pltpu.make_async_remote_copy(
            src_ref=staged.at[i],
            dst_ref=moved.at[i],
            send_sem=move_send.at[i],
            recv_sem=move_recv.at[i],
            device_id=where_is(follower),
            device_id_type=MESH,
        )
        for i in range(3)
    ]

    def start_exchange(phase, which):
        @pl.when((p_split, q_stays)[which])
        def _():
            inner_copy(phase, which).start()

        for (s, axis, side, t), (target, pred) in outgoing.items():
            if s == which:

                @pl.when(pred)
                def _():
                    out_copy(phase, s, axis, side, t, target).start()

    def take_exchange(phase, which):
        for (t, src, axis, side), (source, pred) in incoming.items():
            if t == which:

                @pl.when(pred)
                def _():
                    out_copy(phase, src, axis, 1 - side, t, source).wait_recv()

        @pl.when((p_split, q_stays)[which])
        def _():
            inner_copy(phase, 1 - which).wait_recv()

    def end_exchange(phase):
        for (s, axis, side, t), (target, pred) in outgoing.items():

            @pl.when(pred)
            def _():
                out_copy(phase, s, axis, side, t, target).wait_send()

        for s, split in enumerate((p_split, q_stays)):

            @pl.when(split)
            def _():
                inner_copy(phase, s).wait_send()

    def gather_ghosts(phase, t):
        split = (p_split, q_stays)[t]
        for axis in range(3):
            for side in (0, 1):
                face = 2 * axis + side
                total = 0.0
                for src in (0, 1):
                    pred = incoming[t, src, axis, side][1]
                    total = total + jnp.where(pred, recv_out[phase][t, src, face], 0.0)
                ghosts[phase][t, face] = total
                total = own_in[phase][t, side, axis]
                if side == t:
                    total = total + jnp.where(split, recv_in[phase][t, axis], 0.0)
                ghosts[phase][t, 6 + face] = total
        for bit in (0, 1):
            low, high = (4 if bit == 0 else 10), (5 if bit == 1 else 11)
            for chunk in range(4 * FIELDS[phase]):
                rows = slice(8 * chunk, 8 * chunk + 8)
                first = ghosts[phase][t, low, rows, :]
                second = roll(ghosts[phase][t, high, rows, :], 62)
                for half in (0, 1):
                    both_ends = jnp.where(depth % 2 != half, first, second)
                    edges[phase][t, 2 * bit + half, rows, :] = both_ends

    def fill(phase, q, field, volume, mirror):
        s, p = q // NB, q % NB
        rows = EDGE * field
        js = (p // 2, p % 2 + p // 4 * 2, p % 4)
        for side in (0, 1):
            kind = [jnp.where((p // 2**axis) % 2 == side, 0, 6) for axis in range(2)]
            ghost = ghosts[phase][s, kind[0] + side, pl.ds(pl.multiple_of(rows + 8 * js[0], 8), 8), :]
            has = flags[q, side : side + 1, :] > 0.5
            if mirror:
                spare = volume[q, pl.ds(PITCH + 8 + 31 * side, 8, stride=PITCH), :]
            else:
                spare = jnp.zeros_like(ghost)
            volume[q, pl.ds(PITCH + 7 + 33 * side, 8, stride=PITCH), :] = jnp.where(has, ghost, spare)
            has = flags[q, 2 + side : 3 + side, :] > 0.5
            for part in range(PARTS):
                ghost = ghosts[phase][s, kind[1] + 2 + side, rows + 8 * part : rows + 8 * part + 8, :]
                steps = EDGE * (3 - js[1]) if side == 0 else EDGE * ((4 - js[1]) % 4)
                ghost = pltpu.roll(ghost, steps, 1)
                if mirror:
                    spare = roll(volume[q, spot(7 * side, part), :], 96 - 64 * side)
                else:
                    spare = jnp.zeros_like(ghost)
                volume[q, spot(9 * side - 1, part), :] = jnp.where(has, ghost, spare)

    def z_edge(phase, q, field, tile, part, spare):
        s, p = q // NB, q % NB
        start = EDGE * field + 8 * (tile % 4)
        sheet = edges[phase][s, 2 * (p // 4) + tile // 4, start : start + 8, :]
        ghost = pltpu.roll(sheet, 97 - 2 * part - tile // 4 - 8 * (p % 4), 1)
        has = jnp.where(depth < EDGE // 2, flags[q, 4:5, :], flags[q, 5:6, :]) > 0.5
        return jnp.where(has, ghost, spare)

    def stencil(phase, q, volume, part):
        tiles = [volume[q, spot(t, part), :] for t in range(-1, TILES + 1)]
        down = [roll(t, EDGE) for t in tiles[:-1]]
        up = [None] + [roll(t, -EDGE) for t in tiles[1:]]
        for tile in range(TILES):
            value = tiles[tile + 1]
            top = PITCH * (tile + 1) + 8 + 8 * part
            x_minus = volume[q, top - 1 : top + 7, :]
            x_plus = volume[q, top + 1 : top + 9, :]
            y_minus = jnp.where(lane >= EDGE, down[tile + 1], down[tile])
            y_plus = jnp.where(lane < 3 * EDGE, up[tile + 1], up[tile + 2])
            edge = z_edge(phase, q, 0, tile, part, 0.0)
            z_minus = jnp.where(depth == 0, edge, roll(value, 1))
            z_plus = jnp.where(depth == EDGE - 1, edge, roll(value, -1))
            yield tile, value, (x_minus, x_plus, y_minus, y_plus, z_minus, z_plus)

    def weigh_inside(q, carry):
        for part in range(PARTS):
            tiles = [k_ref[q, spot(t, part), :] for t in range(TILES)]
            down = [roll(t, EDGE) for t in tiles]
            up = [roll(t, -EDGE) for t in tiles]
            for tile in range(TILES):
                place, k = flat(tile, part), tiles[tile]
                before, after = down[max(tile - 1, 0)], up[min(tile + 1, TILES - 1)]
                omega[q, 2, place, :] = k + jnp.where(lane >= EDGE, down[tile], before)
                omega[q, 3, place, :] = k + jnp.where(lane < 3 * EDGE, up[tile], after)
                omega[q, 4, place, :] = k + roll(k, 1)
                omega[q, 5, place, :] = k + roll(k, -1)
        return carry

    def weigh(q, part):
        before = roll(k_ref[q, spot(-1, part), :], EDGE)
        after = roll(k_ref[q, spot(TILES, part), :], -EDGE)
        for tile in range(TILES):
            place, k = flat(tile, part), k_ref[q, spot(tile, part), :]
            top = PITCH * (tile + 1) + 8 + 8 * part
            around_k = [k_ref[q, top - 1 : top + 7, :], k_ref[q, top + 1 : top + 9, :]]
            inside = [omega[q, face, place, :] for face in range(2, 6)]
            if tile == 0:
                inside[0] = jnp.where(lane >= EDGE, inside[0], k + before)
            if tile == TILES - 1:
                inside[1] = jnp.where(lane < 3 * EDGE, inside[1], k + after)
            edge = k + z_edge(0, q, 1, tile, part, k)
            inside[2] = jnp.where(depth == 0, edge, inside[2])
            inside[3] = jnp.where(depth == EDGE - 1, edge, inside[3])
            yield [k + beside for beside in around_k] + inside

    def valid(q):
        low = jnp.where(even, lacking, 0)
        return both(q >= low, q < NB + onward)

    def keep(kind, q, cell, value):
        acc[pl.ds(pl.multiple_of(8 * (8 * NB * kind + 4 * q + cell), 8), 8), :] = value

    def first_sweep(q, carry):
        fill(0, q, 0, u0, False)
        fill(0, q, 1, k_ref, True)
        holds = valid(q)
        totals = [jnp.zeros((8, LANES), jnp.float32) for _ in range(4)]
        for part in range(PARTS):
            for (tile, u, u_beside), weights in zip(stencil(0, q, u0, part), weigh(q, part)):
                total = sum(weights[1:], weights[0])
                scale = jnp.where(holds, OMEGA / total, 0.0)
                place = flat(tile, part)
                weight_sum[q, place, :] = total * (1.0 / OMEGA)
                right = f_ref[q, place, :]
                cell = part // 2 * 2 + tile // 4
                totals[cell] = totals[cell] + right
                gain = right * scale * flags[q, 7:8, :]
                f_ref[q, place, :] = gain
                new = (1.0 - OMEGA) * u + gain
                for face in range(6):
                    weight = weights[face] * scale
                    omega[q, face, place, :] = weight
                    new = new + weight * u_beside[face]
                u1[q, spot(tile, part), :] = new
        for cell in range(4):
            keep(SOURCE, q, cell, totals[cell])
        return carry

    sublane = lax.broadcasted_iota(jnp.int32, (8, LANES), 0)

    def second_sweep(q, send):
        fill(1, q, 0, u1, False)
        zero = jnp.zeros((8, LANES), jnp.float32)
        along_z = [zero] * 4
        along_y = {(layer, half): zero for layer in (0, 15, 16, 31) for half in (0, 1)}
        for part in range(PARTS):
            for tile, u, beside in stencil(1, q, u1, part):
                place = flat(tile, part)
                new = (1.0 - OMEGA) * u + f_ref[q, place, :]
                weights = [omega[q, face, place, :] for face in range(6)]
                for face in range(6):
                    new = new + weights[face] * beside[face]
                u0[q, spot(tile, part), :] = new
                if send:
                    final_send[q - NB, place, :] = new
                scaled = new * weight_sum[q, place, :]
                half, cell = part // 2, part // 2 * 2 + tile // 4
                outward = jnp.where(depth % (EDGE // 2) == EDGE // 2 - 1, weights[5], weights[4])
                along_z[cell] = along_z[cell] + outward * scaled
                if tile in (0, 4):
                    layer = 4 * tile
                    along_y[layer, half] = along_y[layer, half] + weights[2] * scaled
                if tile in (3, 7):
                    layer = 4 * tile + 3
                    along_y[layer, half] = along_y[layer, half] + weights[3] * scaled
        for layer, half in along_y:
            inside = lane < EDGE if layer in (0, 16) else lane >= 3 * EDGE
            along_y[layer, half] = jnp.where(inside, along_y[layer, half], 0.0)
        along_x = {}
        for layer, face in ((0, 0), (15, 1), (16, 0), (31, 1)):
            rows = pl.ds(layer, 8, stride=EDGE)
            value = u0[q, pl.ds(PITCH + 8 + layer, 8, stride=PITCH), :]
            along_x[layer] = omega[q, face, rows, :] * weight_sum[q, rows, :] * value
        middle = along_x[15] - along_x[16]
        own_x = (along_x[0] + middle, along_x[31] - middle)
        for a in (0, 1):
            middle = along_y[15, a] - along_y[16, a]
            own_y = (along_y[0, a] + middle, along_y[31, a] - middle)
            for b in (0, 1):
                upper = sublane // 4 == b
                keep(OWN, q, 2 * a + b, jnp.where(upper, own_x[a], 0.0) + own_y[b])
                keep(ALONG_X, q, 2 * a + b, jnp.where(upper, along_x[31 * a], 0.0))
                keep(ALONG_Y, q, 2 * a + b, along_y[31 * a, b])
                keep(ALONG_Z, q, 2 * a + b, along_z[2 * a + b])

    cell_lane = lax.broadcasted_iota(jnp.int32, (1, LANES), 1)
    block_of = cell_lane // 8 % NB
    corner = (cell_lane // 4 % 2, cell_lane // 2 % 2, cell_lane % 2)
    wide = (LANES, LANES)
    from_depth = lax.broadcasted_iota(jnp.int32, wide, 0) % EDGE
    to_corner = lax.broadcasted_iota(jnp.int32, wide, 1) % 2
    by_half = (from_depth // (EDGE // 2) == to_corner).astype(jnp.float32)

    def one_at(level):
        return (from_depth == level).astype(jnp.float32)

    def take(value, choose):
        return jnp.dot(value, choose, precision=HIGHEST, preferred_element_type=jnp.float32)

    def sums_of(kind):
        groups = []
        for group in range(8):
            start = 8 * (8 * NB * kind + 8 * group)
            groups.append(sum(acc[pl.ds(start + i, 8, stride=8), :] for i in range(8)))
        return jnp.concatenate(groups, axis=0)

    def pick(value, s, block, place):
        rows = lax.broadcasted_iota(jnp.int32, (4 * NB, LANES), 0)
        part = value[4 * NB * s : 4 * NB * (s + 1), :]
        return jnp.sum(jnp.where(rows == 4 * block + place, part, 0.0), axis=0, keepdims=True)

    def other(axis):
        bit = block_of // 2**axis % 2
        return block_of + 2**axis * (1 - 2 * bit)


    def arrive(phase, t):
        take_exchange(phase, t)
        gather_ghosts(phase, t)

    def to_volume(volume):
        def store(q, tile, part, value):
            volume[q, spot(tile, part), :] = value

        return store

    def to_source(q, tile, part, value):
        f_ref[q, flat(tile, part), :] = value

    settle(0, to_volume(u0))
    pack(0, odd_int, 0, u0)
    settle(1, to_volume(k_ref))
    pack(0, odd_int, 1, k_ref)
    pl.semaphore_wait(barrier, expected)
    def merge(arrays):
        def body(p, carry):
            for tile in range(TILES):
                for part in range(PARTS):
                    for i, volume in arrays:
                        place = flat(tile, part) if i == 2 else spot(tile, part)
                        volume[p, place, :] += moved[i, p, flat(tile, part), :]
            return carry

        for i, _ in arrays:
            moves[i].wait_recv()
        lax.fori_loop(0, NB, body, 0)

    @pl.when(even)
    def _():
        start_exchange(0, 0)
        moves[0].start()
        moves[1].start()

        @pl.when(p_split)
        def _():
            flag_copy.start()

    @pl.when(odd)
    def _():
        start_exchange(0, 1)
        merge(((0, u0), (1, k_ref)))
        pack(0, 0, 0, u0)
        pack(0, 0, 1, k_ref)
        start_exchange(0, 0)

    settle(2, to_source)

    @pl.when(even)
    def _():
        moves[2].start()

    @pl.when(odd)
    def _():
        lax.fori_loop(NB, 2 * NB, weigh_inside, 0)

    lax.fori_loop(0, NB, weigh_inside, 0)

    @pl.when(odd)
    def _():
        merge(((2, f_ref),))

    @pl.when(q_stays)
    def _():
        flag_copy.wait_recv()

    @pl.when(odd)
    def _():
        arrive(0, 1)
        lax.fori_loop(NB, 2 * NB, first_sweep, 0)
        pack(1, 1, 0, u1)
        start_exchange(1, 1)

    arrive(0, 0)
    lax.fori_loop(0, NB, first_sweep, 0)
    pack(1, 0, 0, u1)
    start_exchange(1, 0)

    cells = take(sums_of(SOURCE), by_half)
    source_sums = [pick(cells, s, block_of, cell_lane // 2 % 4) for s in (0, 1)]

    def final_copy(p):
        return pltpu.make_async_remote_copy(
            src_ref=final_send.at[p],
            dst_ref=final_recv.at[p],
            send_sem=last_send.at[p],
            recv_sem=last_recv.at[p],
            device_id=where_is(follower),
            device_id_type=MESH,
        )

    @pl.when(odd)
    def _():
        arrive(1, 1)

        def body(q, carry):
            second_sweep(q, True)

            @pl.when(both(has_q, q < NB + EARLY))
            def _():
                final_copy(q - NB).start()

            return carry

        lax.fori_loop(NB, 2 * NB, body, 0)

    arrive(1, 0)

    def body(q, carry):
        second_sweep(q, False)
        return carry

    lax.fori_loop(0, NB, body, 0)

    middle = take(jnp.concatenate([sums_of(kind) for kind in (OWN, ALONG_X, ALONG_Y)], axis=0), by_half)
    crossing = one_at(15) - one_at(16)
    low_cells, high_cells = one_at(0) + crossing, one_at(EDGE - 1) - crossing
    z_sums = sums_of(ALONG_Z)
    own_z = take(z_sums, jnp.where(to_corner == 0, low_cells, high_cells))
    face_z = take(z_sums, jnp.where(to_corner == 0, one_at(EDGE - 1), one_at(0)))
    size = 8 * NB
    own_sums = []
    for s in (0, 1):
        own_sums.append(pick(middle[:size] + own_z, s, block_of, cell_lane // 2 % 4))
        face_x = pick(middle[size : 2 * size], s, other(0), 2 * (1 - corner[0]) + corner[1])
        face_y = pick(middle[2 * size :], s, other(1), 2 * (1 - corner[1]) + corner[0])
        near_z = pick(face_z, s, other(2), cell_lane // 2 % 4)
        edge_sums[s] = jnp.where(sublane == 0, face_x, jnp.where(sublane == 1, face_y, near_z))
    start_exchange(2, 0)

    @pl.when(odd)
    def _():
        start_exchange(2, 1)

    @pl.when(q_stays)
    def _():
        for p in range(EARLY, MIDDLE):
            final_copy(p).start()

    take_exchange(2, 0)

    @pl.when(odd)
    def _():
        take_exchange(2, 1)

    totals = []
    for t in (0, 1):
        combined = jnp.zeros((8, LANES), jnp.float32)
        for p in range(NB):
            combined = jnp.where(lane // 8 % NB == p, flags[NB * t + p], combined)
        beyond = jnp.zeros((1, LANES), jnp.float32)
        for axis in range(3):
            row = slice(axis, axis + 1)
            outer, linked = [], []
            for side in (0, 1):
                face = 2 * axis + side
                total = 0.0
                for src in (0, 1):
                    pred = incoming[t, src, axis, side][1]
                    total = total + jnp.where(pred, got_sums[t, src, face, row, :], 0.0)
                outer.append(total)
                linked.append(combined[face : face + 1, :])
            split = jnp.where((p_split, q_stays)[t], split_sums[t, row, :], 0.0)
            inner = edge_sums[t, row, :] + split
            outer = jnp.where(corner[axis] == 0, outer[0], outer[1])
            linked = jnp.where(corner[axis] == 0, linked[0], linked[1])
            beside = jnp.where(block_of // 2**axis % 2 == corner[axis], outer, inner)
            beyond = beyond + jnp.where(linked > 0.5, beside, 0.0)
        held = block_of < onward if t else block_of >= jnp.where(even, lacking, 0)
        change = combined[6:7, :] * (beyond - own_sums[t])
        totals.append(jnp.where(held, source_sums[t] + change, 0.0))
    low_half = jnp.where(odd, totals[1], totals[0])
    total = jnp.where(cell_lane < 64, low_half, jnp.where(odd, totals[0], 0.0))
    mine[...] = jnp.broadcast_to(total * (EDGE // 2) ** (-1.5), (8, LANES))

    def sum_copy(step):
        return pltpu.make_async_remote_copy(
            src_ref=mine,
            dst_ref=all_sums.at[member],
            send_sem=sum_send.at[step],
            recv_sem=sum_recv.at[step],
            device_id={"member": (member + step) % members},
            device_id_type=MESH,
        )

    def on_copy(step):
        return pltpu.make_async_remote_copy(
            src_ref=mine,
            dst_ref=all_sums.at[members],
            send_sem=sum_send.at[members + step],
            recv_sem=sum_recv.at[0],
            device_id=(next_group, step),
            device_id_type=MESH,
        )

    for step in range(1, members):
        sum_copy(step).start()

    @pl.when(sends_last)
    def _():
        for step in range(members):
            on_copy(step).start()

    @pl.when(q_stays)
    def _():
        for p in range(MIDDLE, NB):
            final_copy(p).start()

    all_sums[member] = mine[...]
    for step in range(1, members):
        sum_copy(step).wait_send()
        sum_copy(step).wait_recv()

    @pl.when(sends_last)
    def _():
        for step in range(members):
            on_copy(step).wait_send()

    @pl.when(gets_last)
    def _():
        on_copy(0).wait_recv()

    correction = jnp.zeros((8 * NB, LANES), jnp.float32)
    for pair in range(members // 2):
        if pair == 0:
            before = jnp.where(gets_last, all_sums[members, 0:1, :], 0.0)
        else:
            before = all_sums[2 * pair - 1, 0:1, :]
        even_cells = all_sums[2 * pair, 0:1, :] + before
        vector = jnp.where(cell_lane < 64, even_cells, all_sums[2 * pair + 1, 0:1, :])
        correction = correction + inverse[0, :, LANES * pair : LANES * (pair + 1)] * vector
    rows_e[...] = jnp.broadcast_to(jnp.sum(correction, axis=1, keepdims=True), (8 * NB, LANES))

    def out_copy_of(p):
        return pltpu.make_async_copy(result.at[p], out_ref.at[p], out_sem.at[p])

    def finish(p, carry):
        @pl.when(p_split)
        def _():
            final_copy(p).wait_recv()

        for cell in range(4):
            first = pl.multiple_of(8 * p, 8) + 2 * cell
            lift = jnp.where(depth < EDGE // 2, rows_e[pl.ds(first, 1), :], rows_e[pl.ds(first + 1, 1), :])
            for part in (2 * (cell // 2), 2 * (cell // 2) + 1):
                for tile in range(4 * (cell % 2), 4 * (cell % 2) + 4):
                    arrived = jnp.where(p_split, final_recv[p, flat(tile, part), :], 0.0)
                    value = u0[p, spot(tile, part), :] + arrived + lift
                    result[p, 8 * part : 8 * part + 8, LANES * tile : LANES * (tile + 1)] = value
        out_copy_of(p).start()
        return carry

    lax.fori_loop(0, NB, finish, 0)
    for p in range(NB):
        out_copy_of(p).wait()

    for phase in range(3):
        end_exchange(phase)

    @pl.when(p_split)
    def _():
        flag_copy.wait_send()

    @pl.when(even)
    def _():
        for i in range(3):
            moves[i].wait_send()

    @pl.when(q_stays)
    def _():
        for p in range(NB):
            final_copy(p).wait_send()


def local(old_ids, field_old, source_old, kappa_old, refine, neighbors, coarse_inverse):
    members = lax.axis_size("member")
    devices = lax.axis_size(AXES)
    flat_shape = (NB, TILES * EDGE, LANES)
    both_shape = (2 * NB, TILES * EDGE, LANES)
    padded = (2 * NB, 10 * PITCH, LANES)
    shapes = [field_old.shape] * 3 + [padded] * 3 + [both_shape]
    shapes += [(2 * NB, 6, TILES * EDGE, LANES), both_shape, (3,) + flat_shape, (3,) + flat_shape]
    shapes += [flat_shape, flat_shape]
    shapes += [(2, 6, EDGE * n, LANES) for n in FIELDS]
    shapes += [(2, 2, 3, EDGE * n, LANES) for n in FIELDS]
    shapes += [(2, 2, 6, EDGE * n, LANES) for n in FIELDS]
    shapes += [(2, 3, EDGE * n, LANES) for n in FIELDS]
    shapes += [(2, 12, EDGE * n, LANES) for n in FIELDS]
    shapes += [(2 * NB, 8, LANES), (5 * 64 * NB, LANES), (8, LANES), (members + 1, 8, LANES)]
    shapes += [(8 * NB, LANES), (2, 8, LANES), (2, 2, 6, 8, LANES), (2, 8, LANES)]
    shapes += [(2, 4, EDGE * n, LANES) for n in FIELDS]
    dma = pltpu.SemaphoreType.DMA
    scratch = [pltpu.VMEM(s, jnp.float32) for s in shapes]
    scratch += [dma((3,)), dma((3,)), dma((3,)), dma((3, 2, 6, 2)), dma((3, 2, 2, 6))]
    scratch += [dma((3, 2)), dma((3, 2)), dma, dma, dma((NB,)), dma((NB,))]
    scratch += [dma((2 * members,)), dma((members,)), dma((NB,))]
    return pl.pallas_call(
        functools.partial(main_kernel, members, devices),
        out_shape=jax.ShapeDtypeStruct((NB, EDGE, FACE), jnp.float32),
        in_specs=[SM, SM, SM, VM, ANY, ANY, ANY],
        out_specs=ANY,
        scratch_shapes=scratch,
        compiler_params=pltpu.CompilerParams(
            collective_id=1, has_side_effects=True, vmem_limit_bytes=VMEM_LIMIT
        ),
    )(old_ids, neighbors, refine, coarse_inverse, field_old, source_old, kappa_old)


def solution(mesh):
    in_specs = (
        P(AXES),
        P(AXES, None, None),
        P(AXES, None, None),
        P(AXES, None, None),
        P(AXES),
        P(AXES, None),
        P("group", "member", None),
    )
    return jax.shard_map(
        local, mesh=mesh, in_specs=in_specs, out_specs=P(AXES, None, None), check_vma=False
    )
```
